256 devices in a mesh: dp: 32 (over y, z), ctx: 8 (over x, core).
Axes of the slice: x: 4, y: 4, z: 8, core: 2. Of those that a mesh axis runs over, the one named last changes fastest.
Arguments:
- long_tokens: bfloat16 [32, 2048, 1024], P('dp', 'ctx'), may hold values from -6 to 6
- short_tokens: bfloat16 [32, 64, 16, 1024], P('dp', 'ctx'), may hold values from -6 to 6
- projection: bfloat16 [1024, 2048], replicated, may hold values from -0.1875 to 0.1875
- time_bias: float32 [4, 16], replicated, may hold values from -4 to 4
- long_length: int32 [32], P('dp'), may hold values from 257 to 2048, as said below
- short_length: int32 [32, 64], P('dp', 'ctx'), may hold values from 1 to 16, as said below
- long_time: int32 [32, 2048], P('dp', 'ctx'), may hold values from 0 to 5093, as said below
- short_time: int32 [32, 64, 16], P('dp', 'ctx'), may hold values from 0 to 1029, as said below
- destination: int32 [32, 64], P('dp', 'ctx'), may hold values from 0 to 255, as said below
- long_cotangent: bfloat16 [32, 2048, 512], P('dp', 'ctx'), may hold values from -6 to 6
- short_cotangent: bfloat16 [32, 64, 16, 512], P('dp', 'ctx'), may hold values from -6 to 6
Outputs:
- long_output: bfloat16 [32, 2048, 512], P('dp', 'ctx')
- short_output: bfloat16 [32, 64, 16, 512], P('dp', 'ctx')
- long_token_grad: bfloat16 [32, 2048, 1024], P('dp', 'ctx')
- short_token_grad: bfloat16 [32, 64, 16, 1024], P('dp', 'ctx')
- projection_grad: float32 [1024, 2048], P('dp', 'ctx')
- bias_grad: float32 [4, 16], replicated
The draws below stay inside these ranges and needn't reach their ends.
Inputs may be any that keep to these rules, and one draw needn't show every extreme that they name: `long_length`: positions at or past a stream's length are padding. Some split stream is always 2048 long. `short_length`: positions at or past a stream's length are padding. Some bucket is always full. `long_time`: nondecreasing along each stream. `short_time`: nondecreasing along each stream. `destination`: for every ctx index the map of the first step is one to one on the 256 buckets of that ctx index, and the buckets of one device go to different dp indices.
All inputs are finite; a program needn't handle non-finite values.
Results may differ from the reference program's by a relative error of at most 0.025.
Values may be sent and summed in bfloat16 or wider, within the bound.
A program may use at most 128 MiB of HBM per device.

```python
import jax
import jax.numpy as jnp
from jax import lax

D = 1024
HEADS = 4
DH = 128
NBT = 16
SLEN = 16
NS = 8
DW = 512
LONG = 2048
N_DP = 32
N_CTX = 8


def rising_times(key, shape, rate):
    key_steps, key_size, key_base, key_pick = jax.random.split(key, 4)
    streams = 1
    for extent in shape[:-1]:
        streams = streams * extent
    count = shape[-1]
    taken = (jax.random.randint(key_steps, (streams, count), 0, rate) == 0).astype(jnp.int32)
    sizes = jax.random.randint(key_size, (streams, count), 1, 3)
    steps = taken * sizes
    base = jax.random.randint(key_base, (streams, 1), 0, 1000)
    picked = jax.random.permutation(key_pick, streams)
    lowest = picked[0]
    highest = picked[1]
    stream_ids = jnp.arange(streams, dtype=jnp.int32)[:, None]
    steps = jnp.where(stream_ids == highest, 2, steps)
    base = jnp.where(stream_ids == highest, 999, base)
    base = jnp.where(stream_ids == lowest, 0, base)
    times = base + jnp.cumsum(steps, axis=-1) - steps[:, :1]
    return times.reshape(shape).astype(jnp.int32)


def draw_long_length(key, part):
    key = jax.random.fold_in(key, 11)
    key_values, key_chosen = jax.random.split(key)
    lengths = jax.random.randint(key_values, (N_DP,), LONG // 8 + 1, LONG + 1)
    chosen = jax.random.randint(key_chosen, (), 0, N_DP)
    return jnp.where(jnp.arange(N_DP) == chosen, LONG, lengths).astype(jnp.int32)


def draw_short_length(key, part):
    key = jax.random.fold_in(key, 13)
    key_values, key_chosen = jax.random.split(key)
    lengths = jax.random.randint(key_values, (N_DP * N_CTX * NS,), 1, SLEN + 1)
    chosen = jax.random.randint(key_chosen, (), 0, N_DP * N_CTX * NS)
    lengths = jnp.where(jnp.arange(N_DP * N_CTX * NS) == chosen, SLEN, lengths)
    return lengths.reshape(N_DP, N_CTX * NS).astype(jnp.int32)


def draw_long_time(key, part):
    key = jax.random.fold_in(key, 15)
    return rising_times(key, (N_DP, LONG), max(LONG // (2 * NBT), 1))


def draw_short_time(key, part):
    key = jax.random.fold_in(key, 19)
    return rising_times(key, (N_DP, N_CTX * NS, SLEN), max(SLEN // NBT, 1))


def draw_destination(key, part):
    key = jax.random.fold_in(key, 17)

    def column(index):
        column_key = jax.random.fold_in(key, index)
        key_outer, key_inner, key_offset, key_slot = jax.random.split(column_key, 4)
        outer = jax.random.permutation(key_outer, N_DP)
        inner = jax.random.permutation(key_inner, N_DP)
        offsets = jax.random.permutation(key_offset, N_DP)[:NS]
        slots = jax.random.permutation(key_slot, NS)
        shifted = (inner[:, None] + offsets[None, :]) % N_DP
        peers = outer[shifted]
        return peers * NS + slots[None, :]
    table = jax.vmap(column)(jnp.arange(N_CTX))
    return jnp.transpose(table, (1, 0, 2)).reshape(N_DP, N_CTX * NS).astype(jnp.int32)


def steps_of(rng, dims, cuts, low, top_value):
    gain, own = 1.0, jax.random.fold_in(rng, 6)
    for position, shards_of in cuts:
        heights = jnp.exp(jax.random.uniform(jax.random.fold_in(own, position), (shards_of,), jnp.float32, low / len(cuts), top_value / len(cuts)))
        gain = gain * jnp.repeat(heights, dims[position] // shards_of).reshape([-1 if axis == position else 1 for axis in range(len(dims))])
    return gain


def scatter_about(own_key, shape, scale, reach, cuts=(), kind=jnp.bfloat16):
    values = scale * jax.random.normal(own_key, shape, jnp.float32)
    if cuts:
        values = values * steps_of(own_key, shape, cuts, -0.22, 0.18)
    return jnp.clip(values, -reach, reach).astype(kind)


def setup_inputs(seed: int = 0) -> dict:
    splits = jax.random.split(jax.random.key(seed), 12)
    return {
        "long_tokens": scatter_about(splits[0], (N_DP, LONG, D), 1.0, 6.0, ((0, 32), (1, 8))),
        "short_tokens": scatter_about(splits[1], (N_DP, N_CTX * NS, SLEN, D), 1.0, 6.0, ((0, 32), (1, 8))),
        "projection": scatter_about(splits[2], (D, 4 * DW), D ** -0.5, 0.1875),
        "time_bias": scatter_about(splits[3], (HEADS, NBT), 1.0, 4.0, (), jnp.float32),
        "long_length": draw_long_length(jax.random.fold_in(splits[11], 71), 0),
        "short_length": draw_short_length(jax.random.fold_in(splits[11], 71), 0),
        "long_time": draw_long_time(jax.random.fold_in(splits[11], 71), 0),
        "short_time": draw_short_time(jax.random.fold_in(splits[11], 71), 0),
        "destination": draw_destination(jax.random.fold_in(splits[11], 71), 0),
        "long_cotangent": scatter_about(splits[9], (N_DP, LONG, DW), 1.0, 6.0, ((0, 32), (1, 8))),
        "short_cotangent": scatter_about(splits[10], (N_DP, N_CTX * NS, SLEN, DW), 1.0, 6.0, ((0, 32), (1, 8))),
    }


epsilon = 1e-05

def silu_grad(value):
    sigma = jax.nn.sigmoid(value)
    return sigma * (1.0 + value * (1.0 - sigma))

def layer_norm(mixed):
    average = lax.optimization_barrier(jnp.mean(mixed, axis=-1, keepdims=True))
    centred = mixed - average
    spread = lax.optimization_barrier(jnp.mean(centred * centred, axis=-1, keepdims=True))
    return centred * lax.rsqrt(spread + epsilon)

def pair_terms(queries, keys, query_time, key_time, query_place, key_place, length, table):
    scores = jnp.einsum('rhd,chd->hrc', queries.astype(jnp.float32), keys.astype(jnp.float32)) * DH ** (-0.5)
    bucket = jnp.clip(query_time[:, None] - key_time[None, :], 0, NBT - 1)
    bias = jnp.zeros(scores.shape, jnp.float32)
    for bucket_id in range(NBT):
        bias = jnp.where((bucket == bucket_id)[None], table[:, bucket_id][:, None, None], bias)
    visible = (key_place[None, :] <= query_place[:, None]) & (key_place[None, :] < length) & (query_place[:, None] < length)
    return (scores + bias, visible, bucket)

def bucket_sums(score_grad, bucket):
    return jnp.stack([lax.optimization_barrier(jnp.sum(jnp.where((bucket == bucket_id)[None], score_grad, 0.0), axis=(1, 2))) for bucket_id in range(NBT)], axis=1)

def stream(tokens, weights, table, times, length, cotangent):
    rows = tokens.shape[0]
    width = HEADS * DH
    projected = jnp.dot(tokens, weights, preferred_element_type=jnp.float32)
    activations = jax.nn.silu(projected).astype(jnp.bfloat16)
    gates = activations[:, :width]
    values = activations[:, width:2 * width].reshape(rows, HEADS, DH)
    queries = activations[:, 2 * width:3 * width].reshape(rows, HEADS, DH)
    keys = activations[:, 3 * width:].reshape(rows, HEADS, DH)
    places = jnp.arange(rows, dtype=jnp.int32)
    block = min(512, rows)

    def one_block(carry, index):
        key_grad, value_grad, table_grad = carry
        start = (index * block).astype(jnp.int32)
        query_rows = lax.dynamic_slice_in_dim(queries, start, block, 0)
        query_time = lax.dynamic_slice_in_dim(times, start, block, 0)
        query_place = lax.dynamic_slice_in_dim(places, start, block, 0)
        gate_rows = lax.dynamic_slice_in_dim(gates, start, block, 0).astype(jnp.float32)
        cot_rows = lax.dynamic_slice_in_dim(cotangent, start, block, 0).astype(jnp.float32)
        total, visible, bucket = pair_terms(query_rows, keys, query_time, times, query_place, places, length, table)
        weights_p = jnp.where(visible[None], jax.nn.silu(total), 0.0).astype(jnp.bfloat16)
        mixed = jnp.einsum('hrc,chd->rhd', weights_p.astype(jnp.float32), values.astype(jnp.float32)).reshape(block, width)
        normed = layer_norm(mixed)
        output = (normed * gate_rows).astype(jnp.bfloat16)
        gate_grad = cot_rows * normed
        pullback = jax.vjp(layer_norm, mixed)[1]
        mixed_grad = pullback(cot_rows * gate_rows)[0].astype(jnp.bfloat16).reshape(block, HEADS, DH)
        prob_grad = jnp.einsum('rhd,chd->hrc', mixed_grad.astype(jnp.float32), values.astype(jnp.float32))
        score_grad = jnp.where(visible[None], prob_grad * silu_grad(total), 0.0)
        score_half = score_grad.astype(jnp.bfloat16).astype(jnp.float32)
        query_grad = jnp.einsum('hrc,chd->rhd', score_half, keys.astype(jnp.float32)) * DH ** (-0.5)
        key_part = jnp.einsum('hrc,rhd->chd', score_half, query_rows.astype(jnp.float32)) * DH ** (-0.5)
        value_part = jnp.einsum('hrc,rhd->chd', weights_p.astype(jnp.float32), mixed_grad.astype(jnp.float32))
        carry = (key_grad + key_part, value_grad + value_part, table_grad + bucket_sums(score_grad, bucket))
        return (carry, (output, gate_grad, query_grad.reshape(block, width)))
    start_carry = (jnp.zeros((rows, HEADS, DH), jnp.float32), jnp.zeros((rows, HEADS, DH), jnp.float32), jnp.zeros((HEADS, NBT), jnp.float32))
    carry, stacked = lax.scan(one_block, start_carry, jnp.arange(rows // block, dtype=jnp.int32))
    key_grad, value_grad, table_grad = carry
    outputs = stacked[0].reshape(rows, width)
    gate_grad = stacked[1].reshape(rows, width)
    query_grad = stacked[2].reshape(rows, width)
    grads = jnp.concatenate([gate_grad, value_grad.reshape(rows, width), query_grad, key_grad.reshape(rows, width)], axis=1)
    act_grad = (grads * silu_grad(projected)).astype(jnp.bfloat16)
    token_grad = jnp.dot(act_grad, weights.T, preferred_element_type=jnp.float32).astype(jnp.bfloat16)
    return (outputs, token_grad, act_grad, table_grad)

def reference(long_tokens, short_tokens, projection, time_bias, long_length, short_length, long_time, short_time, destination, long_cotangent, short_cotangent):
    width = HEADS * DH

    def long_group(carry, inputs):
        tokens, times, length, cotangent = inputs
        outputs, token_grad, act_grad, table_grad = stream(tokens, projection, time_bias, times, length, cotangent)
        weight_sum = carry[0] + jnp.dot(tokens.T, act_grad, preferred_element_type=jnp.float32)
        return ((weight_sum, carry[1] + table_grad), (outputs, token_grad))
    start_carry = (jnp.zeros((D, 4 * width), jnp.float32), jnp.zeros((HEADS, NBT), jnp.float32))
    carry, long_parts = lax.scan(long_group, start_carry, (long_tokens, long_time, long_length, long_cotangent))
    columns = N_CTX * NS
    home_column = jnp.arange(columns, dtype=jnp.int32)
    target_peer = (destination // NS).astype(jnp.int32)
    target_column = ((home_column // NS)[None, :] * NS + destination % NS).astype(jnp.int32)
    balanced_tokens = jnp.zeros_like(short_tokens).at[target_peer, target_column].set(short_tokens)
    balanced_time = jnp.zeros_like(short_time).at[target_peer, target_column].set(short_time)
    balanced_length = jnp.zeros_like(short_length).at[target_peer, target_column].set(short_length)

    def short_group(carry, inputs):
        tokens, times, lengths, cotangent = inputs
        outputs, token_grad, act_grad, table_grad = jax.vmap(stream, in_axes=(0, None, None, 0, 0, 0))(tokens, projection, time_bias, times, lengths, cotangent)
        weight_sum = carry[0] + jnp.dot(tokens.reshape(-1, D).T, act_grad.reshape(-1, 4 * width), preferred_element_type=jnp.float32)
        return ((weight_sum, carry[1] + lax.optimization_barrier(jnp.sum(table_grad, axis=0))), (outputs, token_grad))
    carry, short_parts = lax.scan(short_group, carry, (balanced_tokens, balanced_time, balanced_length, short_cotangent))
    short_token_grad = short_parts[1][target_peer, target_column]
    return (long_parts[0], short_parts[0], long_parts[1], short_token_grad, carry[0], carry[1])
```

```python
import functools

import jax
import jax.numpy as jnp
from jax import lax
from jax.experimental import pallas as pl
from jax.experimental.pallas import tpu as pltpu
from jax.sharding import PartitionSpec as P

epsilon = 1e-05
MESH = pl.DeviceIdType.MESH
BF = jnp.bfloat16
F32 = jnp.float32
CHIPS = 4
ROWS = 256
HEAD = 128
LEVELS = 16
SLEN = 16
SHORT = 128
MODEL = 1024
BLOCK = 512
SCALE = HEAD ** (-0.5)
VMEM_LIMIT = 56 * 1024 * 1024


def sigmoid(value):
    return 0.5 * jnp.tanh(0.5 * value) + 0.5


def silu_grad(value):
    sigma = sigmoid(value)
    return sigma * (1.0 + value * (1.0 - sigma))


def dot_nn(a, b):
    return jnp.dot(a, b, preferred_element_type=F32)


def dot_nt(a, b):
    return lax.dot_general(a, b, (((1,), (1,)), ((), ())), preferred_element_type=F32)


def dot_tn(a, b):
    return lax.dot_general(a, b, (((0,), (0,)), ((), ())), preferred_element_type=F32)


def column_of(row):
    return jnp.transpose(jnp.broadcast_to(row, (128, 128)))


def iota(shape, axis):
    return lax.broadcasted_iota(jnp.int32, shape, axis)


def remote(src, dst, send_sem, recv_sem, dp, ctx):
    return pltpu.make_async_remote_copy(
        src_ref=src,
        dst_ref=dst,
        send_sem=send_sem,
        recv_sem=recv_sem,
        device_id=(dp, ctx),
        device_id_type=MESH,
    )


def place():
    dp = lax.axis_index("dp")
    ctx = lax.axis_index("ctx")
    return dp, ctx, lax.div(ctx, 2), lax.rem(ctx, 2)


def greet(dp, ctx, n_dp):
    barrier = pltpu.get_barrier_semaphore()

    def to_dp(o, carry):
        pl.semaphore_signal(
            barrier, inc=1, device_id=(lax.rem(dp + o, n_dp), ctx), device_id_type=MESH
        )
        return carry

    lax.fori_loop(1, n_dp, to_dp, 0)

    def to_ctx(o, carry):
        pl.semaphore_signal(
            barrier, inc=1, device_id=(dp, lax.rem(ctx + o, 2 * CHIPS)), device_id_type=MESH
        )
        return carry

    lax.fori_loop(1, 2 * CHIPS, to_ctx, 0)
    pl.semaphore_wait(barrier, n_dp - 1 + 2 * CHIPS - 1)


def lookup(table, diff):
    index = jnp.clip(diff, 0.0, LEVELS - 1.0).astype(jnp.int32)
    parts = [
        jnp.take_along_axis(table, index[:, i : i + 128], axis=1)
        for i in range(0, index.shape[1], 128)
    ]
    return parts[0] if len(parts) == 1 else jnp.concatenate(parts, axis=1)


def gather_kernel(
    n_dp,
    tok,
    w,
    lcot,
    meta,
    scot,
    tok_g,
    p_g,
    act_g,
    kv,
    c_g,
    times,
    c_home,
    place_m,
    wx,
    dtile,
    dest_g,
    cbuf,
    crecv,
    w_sem,
    tok_s,
    tok_r,
    c_s,
    c_r,
    t_s,
    t_r,
    kv_s,
    kv_r,
    d_s,
    d_r,
    s_s,
    s_r,
):
    dp, ctx, chip, core = place()
    sib = ctx + 1 - 2 * core
    loads = []
    for k in range(4):
        col = pl.multiple_of(k * BLOCK + chip * HEAD, HEAD)
        load = pltpu.make_async_copy(
            w.at[:, pl.ds(col, HEAD)], wx.at[:, k * HEAD : (k + 1) * HEAD], w_sem.at[k]
        )
        load.start()
        loads.append(load)
    dtile[...] = jnp.broadcast_to(meta[5:6, :], (8, 128))
    greet(dp, ctx, n_dp)

    def tok_copy(d):
        return remote(
            tok,
            tok_g.at[chip],
            tok_s.at[d],
            tok_r.at[d],
            dp,
            2 * lax.rem(chip + d, CHIPS) + core,
        )

    def c_copy(d):
        peer = lax.rem(chip + d, CHIPS)
        return remote(
            lcot.at[:, pl.ds(pl.multiple_of(peer * HEAD, HEAD), HEAD)],
            c_g.at[chip],
            c_s.at[d],
            c_r.at[d],
            dp,
            2 * peer + core,
        )

    def t_copy(o):
        return remote(
            meta, times.at[ctx], t_s.at[o], t_r.at[o], dp, lax.rem(ctx + o, 2 * CHIPS)
        )

    def d_copy(o):
        return remote(dtile, dest_g.at[dp], d_s.at[o], d_r.at[o], lax.rem(dp + o, n_dp), ctx)

    def s_copy(o):
        peer = lax.rem(dp + o, n_dp)
        return remote(cbuf.at[peer], crecv.at[dp], s_s.at[o], s_r.at[o], peer, ctx)

    for d in (1, 3, 2):
        tok_copy(d).start()

    def start_d(o, carry):
        d_copy(o).start()
        return carry

    lax.fori_loop(1, n_dp, start_d, 0)

    def start_t(o, carry):
        t_copy(o).start()
        return carry

    lax.fori_loop(1, 2 * CHIPS, start_t, 0)
    for d in (1, 3, 2):
        c_copy(d).start()
    tok_g[chip] = tok[...]
    c_g[chip] = lcot[:, pl.ds(pl.multiple_of(chip * HEAD, HEAD), HEAD)]
    times[ctx] = meta[...]
    dest_g[dp] = dtile[...]
    for load in loads:
        load.wait()

    def kv_copy(d):
        src = lax.rem(chip + CHIPS - d, CHIPS)
        return remote(
            kv.at[2 * src + core], kv.at[2 * src + core], kv_s.at[d], kv_r.at[d], dp, sib
        )

    def project(step, carry):
        d = step ^ (step >> 1)
        src = lax.rem(chip + CHIPS - d, CHIPS)

        @pl.when(step > 0)
        def _():
            remote(tok, tok_g.at[src], tok_s.at[d], tok_r.at[d], dp, sib).wait_recv()

        projected = dot_nn(tok_g[src], wx[...])
        p_g[src] = projected
        act = (projected * sigmoid(projected)).astype(BF)
        act_g[src] = act
        kv[2 * src + core, :, 0:HEAD] = act[:, 3 * HEAD : 4 * HEAD]
        kv[2 * src + core, :, HEAD : 2 * HEAD] = act[:, HEAD : 2 * HEAD]
        kv_copy(d).start()
        return carry

    project(0, 0)

    def wait_d(o, carry):
        src = lax.rem(dp + n_dp - o, n_dp)
        remote(dtile, dest_g.at[src], d_s.at[o], d_r.at[o], src, ctx).wait_recv()
        return carry

    lax.fori_loop(1, n_dp, wait_d, 0)
    dest = dest_g[...]
    code = jnp.sum(
        jnp.where((dest >> 3) == dp, ((dest & 7) + 1).astype(F32), 0.0), axis=2, keepdims=True
    )
    code = jnp.broadcast_to(code, (n_dp, 8, 128))
    code = jnp.concatenate([code, code], axis=1).reshape(n_dp * SLEN, 128)
    shape = (n_dp * SLEN, 128)
    same = (iota(shape, 0) & 15) == (iota(shape, 1) & 15)
    slot = ((iota(shape, 1) >> 4) + 1).astype(F32)
    placer = jnp.where(same & (code == slot), 1.0, 0.0).astype(BF)
    place_m[...] = placer
    cbuf[...] = dot_nn(placer, scot[...]).astype(BF).reshape(cbuf.shape)

    def start_s(o, carry):
        s_copy(o).start()
        return carry

    lax.fori_loop(1, n_dp, start_s, 0)
    crecv[dp] = cbuf[dp]

    lax.fori_loop(1, CHIPS, project, 0)

    def wait_s(o, carry):
        src = lax.rem(dp + n_dp - o, n_dp)
        remote(cbuf.at[src], crecv.at[src], s_s.at[o], s_r.at[o], src, ctx).wait_recv()
        return carry

    lax.fori_loop(1, n_dp, wait_s, 0)
    owner = column_of((meta[4:5, :] >> 3).astype(F32))
    owner = jnp.concatenate([owner] * (n_dp * SLEN // 128), axis=1)
    shape = (SHORT, n_dp * SLEN)
    same = (iota(shape, 0) & 15) == (iota(shape, 1) & 15)
    chooser = jnp.where(
        same & (owner == (iota(shape, 1) >> 4).astype(F32)), 1.0, 0.0
    ).astype(BF)
    c_home[...] = dot_nn(chooser, crecv[...].reshape(n_dp * SLEN, BLOCK)).astype(BF)

    for d in (1, 3, 2):
        src = lax.rem(chip + CHIPS - d, CHIPS)
        remote(c_g.at[src], c_g.at[src], c_s.at[d], c_r.at[d], dp, sib).wait_recv()
    for d in range(CHIPS):
        src = lax.rem(chip + CHIPS - d, CHIPS)
        other = kv.at[2 * src + 1 - core]
        remote(other, other, kv_s.at[d], kv_r.at[d], dp, sib).wait_recv()

    def wait_t(o, carry):
        src = lax.rem(ctx + 2 * CHIPS - o, 2 * CHIPS)
        remote(meta, times.at[src], t_s.at[o], t_r.at[o], dp, src).wait_recv()
        return carry

    lax.fori_loop(1, 2 * CHIPS, wait_t, 0)

    def ended_t(o, carry):
        t_copy(o).wait_send()
        return carry

    lax.fori_loop(1, 2 * CHIPS, ended_t, 0)
    for d in (1, 3, 2):
        tok_copy(d).wait_send()
        c_copy(d).wait_send()
    for d in range(CHIPS):
        kv_copy(d).wait_send()

    def ended(o, carry):
        d_copy(o).wait_send()
        s_copy(o).wait_send()
        return carry

    lax.fori_loop(1, n_dp, ended, 0)


def short_kernel(
    n_dp, tok, w, cot, meta, table, token_grad, grad_heads, outbuf, bias, p_ref, grad_flat
):
    tokens = tok[...]
    for k in range(4):
        p_ref[:, k * BLOCK : (k + 1) * BLOCK] = dot_nn(tokens, w[:, k * BLOCK : (k + 1) * BLOCK])
    shape = (SHORT, SHORT)
    row = iota(shape, 0)
    col = iota(shape, 1)
    time_row = meta[2:3, :].astype(F32)
    time_col = column_of(time_row)
    length_col = column_of(meta[3:4, :].astype(F32))
    inside = (row & 15).astype(F32) < length_col
    visible = ((row >> 4) == (col >> 4)) & (col <= row) & inside
    diff = time_col - time_row
    acts, weights, slopes, mixes = [], [], [], []
    for h in range(4):
        parts = []
        for k in range(4):
            v = p_ref[:, k * BLOCK + h * HEAD : k * BLOCK + (h + 1) * HEAD]
            parts.append((v * sigmoid(v)).astype(BF))
        acts.append(parts)
        gates, values, queries, keys = parts
        tab = jnp.broadcast_to(table[h : h + 1, :], shape)
        total = dot_nt(queries, keys) * SCALE + lookup(tab, diff)
        sg = sigmoid(total)
        weight = total * sg
        weights.append(jnp.where(visible, weight, 0.0).astype(BF))
        slopes.append(jnp.where(visible, sg + weight * (1.0 - sg), 0.0))
        mixes.append(dot_nn(weights[h], values))
    mean = sum(jnp.sum(m, axis=1, keepdims=True) for m in mixes) / BLOCK
    centred = [m - mean for m in mixes]
    spread = sum(jnp.sum(m * m, axis=1, keepdims=True) for m in centred) / BLOCK
    scale = lax.rsqrt(spread + epsilon)
    normed = [m * scale for m in centred]
    cots = [cot[:, h * HEAD : (h + 1) * HEAD].astype(F32) for h in range(4)]
    qs = [cots[h] * acts[h][0].astype(F32) for h in range(4)]
    mean_q = sum(jnp.sum(q, axis=1, keepdims=True) for q in qs) / BLOCK
    mean_qn = sum(jnp.sum(q * n, axis=1, keepdims=True) for q, n in zip(qs, normed)) / BLOCK

    bucket = jnp.clip(diff, 0.0, LEVELS - 1.0).astype(jnp.int32)
    level = iota((LEVELS, 128), 0)
    lane = iota((LEVELS, 128), 1)
    sums = jnp.zeros((LEVELS, 128), F32)
    outs = []
    for h in range(4):
        gates, values, queries, keys = acts[h]
        outs.append((normed[h] * gates.astype(F32)).astype(BF))
        mixed_grad = ((qs[h] - mean_q - normed[h] * mean_qn) * scale).astype(BF)
        grad = dot_nt(mixed_grad, values) * slopes[h]
        rows = [
            jnp.sum(jnp.where(bucket == b, grad, 0.0), axis=0, keepdims=True)
            for b in range(LEVELS)
        ]
        per_level = jnp.sum(jnp.concatenate(rows, axis=0), axis=1, keepdims=True)
        sums = sums + jnp.where(lane == h, per_level, 0.0)
        half = grad.astype(BF)
        grads = [
            cots[h] * normed[h],
            dot_tn(weights[h], mixed_grad),
            dot_nn(half, keys) * SCALE,
            dot_tn(half, queries) * SCALE,
        ]
        for k in range(4):
            v = p_ref[:, k * BLOCK + h * HEAD : k * BLOCK + (h + 1) * HEAD]
            g = (grads[k] * silu_grad(v)).astype(BF)
            grad_heads[h, :, k * HEAD : (k + 1) * HEAD] = g
            grad_flat[:, k * BLOCK + h * HEAD : k * BLOCK + (h + 1) * HEAD] = g
    bias[...] = sums
    out = jnp.concatenate(outs, axis=1)
    shape = (n_dp * SLEN, SHORT)
    same = (iota(shape, 0) & 15) == (iota(shape, 1) & 15)
    target = (meta[4:5, :] >> 3).astype(F32)
    sender = jnp.where(same & (target == (iota(shape, 0) >> 4).astype(F32)), 1.0, 0.0).astype(BF)
    outbuf[...] = dot_nn(sender, out).astype(BF).reshape(outbuf.shape)
    flat = grad_flat[...]
    for i in range(0, MODEL, 256):
        token_grad[:, i : i + 256] = dot_nt(flat, w[i : i + 256, :]).astype(BF)


def attend_kernel(
    n_dp,
    act,
    p_g,
    kv,
    cot,
    times,
    table,
    stok,
    sgrad,
    outbuf,
    place_m,
    sbias,
    grad,
    out,
    bias,
    stok_g,
    sgrad_g,
    short_out,
    orecv,
    weight_s,
    slope_s,
    mixed_s,
    hot_s,
    tcol_s,
    trow_s,
    stat_s,
    dk_s,
    dv_s,
    dq_s,
    hist_s,
    tot_s,
    sib_send,
    sib_recv,
    st_s,
    st_r,
    sg_s,
    sg_r,
    o_s,
    o_r,
    stat_sem_s,
    stat_sem_r,
    sib_s,
    sib_r,
):
    dp, ctx, chip, core = place()
    sib = ctx + 1 - 2 * core
    greet(dp, ctx, n_dp)

    def st_copy(d):
        return remote(
            stok, stok_g.at[chip], st_s.at[d], st_r.at[d], dp, 2 * lax.rem(chip + d, CHIPS) + core
        )

    def sg_copy(d):
        peer = lax.rem(chip + d, CHIPS)
        return remote(
            sgrad.at[peer], sgrad_g.at[chip], sg_s.at[d], sg_r.at[d], dp, 2 * peer + core
        )

    def o_copy(o):
        peer = lax.rem(dp + o, n_dp)
        return remote(outbuf.at[peer], orecv.at[dp], o_s.at[o], o_r.at[o], peer, ctx)

    def start_o(o, carry):
        o_copy(o).start()
        return carry

    lax.fori_loop(1, n_dp, start_o, 0)
    for d in (1, 3, 2):
        sg_copy(d).start()
        st_copy(d).start()
    orecv[dp] = outbuf[dp]
    stok_g[chip] = stok[...]
    sgrad_g[chip] = sgrad[chip]

    tab = jnp.broadcast_to(table[pl.ds(chip, 1), :], (ROWS, 128))
    length = times[0, 6:7, 0:1].astype(F32)
    lane = iota((ROWS, 128), 1)

    def times_of(b, carry):
        row = jnp.concatenate([times[b, 0:1, :], times[b, 1:2, :]], axis=1).astype(F32)
        trow_s[b] = jnp.broadcast_to(row, (8, ROWS))
        col = jnp.concatenate([column_of(row[:, 0:128]), column_of(row[:, 128:256])], axis=0)
        tcol_s[b] = col
        hot_s[b] = jnp.where((col.astype(jnp.int32) & 15) == lane, 1.0, 0.0).astype(BF)
        return carry

    lax.fori_loop(0, 2 * CHIPS, times_of, 0)
    dk_s[...] = jnp.zeros_like(dk_s)
    dv_s[...] = jnp.zeros_like(dv_s)
    hist_s[...] = jnp.zeros_like(hist_s)
    tot_s[...] = jnp.zeros_like(tot_s)

    def stat_copy(qs, d):
        return remote(
            stat_s.at[qs, chip],
            stat_s.at[qs, chip],
            stat_sem_s.at[qs, d],
            stat_sem_r.at[qs, d],
            dp,
            2 * lax.rem(chip + d, CHIPS) + core,
        )

    def forward(step, carry):
        qs = CHIPS - 1 - step
        block = 2 * qs + core
        queries = act[qs, :, 2 * HEAD : 3 * HEAD]
        tq = tcol_s[block][:, 0:1]
        spot = iota((ROWS, 1), 0) + block * ROWS
        limit = jnp.where(spot.astype(F32) < length, spot, -1)
        mixed_s[qs] = jnp.zeros((ROWS, HEAD), F32)

        def tile(kb, carry):
            keys = kv[kb, :, 0:HEAD]
            values = kv[kb, :, HEAD : 2 * HEAD]
            tk = trow_s[kb][0:1, :]
            total = dot_nt(queries, keys) * SCALE + lookup(tab, tq - tk)
            sg = sigmoid(total)
            weight = total * sg
            visible = (iota((ROWS, ROWS), 1) + kb * ROWS) <= limit
            weight16 = jnp.where(visible, weight, 0.0).astype(BF)
            weight_s[qs, kb] = weight16
            slope_s[qs, kb] = jnp.where(visible, sg + weight * (1.0 - sg), 0.0)
            mixed_s[qs] += dot_nn(weight16, values)
            return carry

        lax.fori_loop(0, block + 1, tile, 0)
        mixed = mixed_s[qs]
        q = cot[qs].astype(F32) * act[qs, :, 0:HEAD].astype(F32)
        s1 = jnp.sum(mixed, axis=1, keepdims=True)
        centred = mixed - s1 * (1.0 / HEAD)
        s2 = jnp.sum(centred * centred, axis=1, keepdims=True)
        s3 = jnp.sum(q, axis=1, keepdims=True)
        s4 = jnp.sum(q * centred, axis=1, keepdims=True)
        stats = jnp.where(
            lane == 0, s1, jnp.where(lane == 1, s2, jnp.where(lane == 2, s3, s4))
        )
        stat_s[qs, chip] = jnp.transpose(stats)[0:8, :]
        for d in (1, 3, 2):
            stat_copy(qs, d).start()
        return carry

    lax.fori_loop(0, CHIPS, forward, 0)

    def sib_copy(qs):
        return remote(
            sib_send.at[qs], sib_recv.at[qs], sib_s.at[qs], sib_r.at[qs], dp, sib
        )

    def backward(step, carry):
        qs = CHIPS - 1 - step
        block = 2 * qs + core
        for d in (1, 3, 2):
            src = lax.rem(chip + CHIPS - d, CHIPS)
            remote(
                stat_s.at[qs, src],
                stat_s.at[qs, src],
                stat_sem_s.at[qs, d],
                stat_sem_r.at[qs, d],
                dp,
                sib,
            ).wait_recv()
        stats = [stat_s[qs, h] for h in range(4)]
        mean = sum(s[0:1, :] for s in stats) * (1.0 / BLOCK)
        gaps = [s[0:1, :] * (1.0 / HEAD) - mean for s in stats]
        spread = sum(s[1:2, :] + HEAD * g * g for s, g in zip(stats, gaps)) * (1.0 / BLOCK)
        scale = lax.rsqrt(spread + epsilon)
        mean_q = sum(s[2:3, :] for s in stats) * (1.0 / BLOCK)
        mean_qn = sum(s[3:4, :] + g * s[2:3, :] for s, g in zip(stats, gaps))
        mean_qn = mean_qn * scale * (1.0 / BLOCK)
        whole = jnp.concatenate(
            [mean, scale, mean_q, mean_qn, jnp.zeros((124, ROWS), F32)], axis=0
        )
        cols = jnp.transpose(whole)
        mean, scale = cols[:, 0:1], cols[:, 1:2]
        mean_q, mean_qn = cols[:, 2:3], cols[:, 3:4]
        normed = (mixed_s[qs] - mean) * scale
        gates = act[qs, :, 0:HEAD].astype(F32)
        cotangent = cot[qs].astype(F32)
        out[qs] = (normed * gates).astype(BF)
        mixed_grad = ((cotangent * gates - mean_q - normed * mean_qn) * scale).astype(BF)
        grad[qs, :, 0:HEAD] = (cotangent * normed * silu_grad(p_g[qs, :, 0:HEAD])).astype(BF)
        queries = act[qs, :, 2 * HEAD : 3 * HEAD]
        tq = tcol_s[block][:, 0:1]
        dq_s[...] = jnp.zeros_like(dq_s)
        hist_s[0] = jnp.zeros((ROWS, 128), F32)

        def tile(kb, carry):
            keys = kv[kb, :, 0:HEAD]
            values = kv[kb, :, HEAD : 2 * HEAD]
            tk = trow_s[kb][0:1, :]
            score = dot_nt(mixed_grad, values) * slope_s[qs, kb]
            near = jnp.where(tq - tk < LEVELS - 1.0, score, 0.0).astype(BF)
            half = score.astype(BF)
            tot_s[...] += jnp.sum(score.reshape(ROWS // 8, 8, ROWS), axis=0)
            hist_s[0] += dot_nn(near, hot_s[kb])
            dq_s[...] += dot_nn(half, keys)
            dk_s[kb] += dot_tn(half, queries)
            dv_s[kb] += dot_tn(weight_s[qs, kb], mixed_grad)
            return carry

        lax.fori_loop(0, block + 1, tile, 0)
        hist_s[1, 0:128, :] += lax.dot_general(
            hot_s[block].astype(F32),
            hist_s[0],
            (((0,), (0,)), ((), ())),
            precision=lax.Precision.HIGHEST,
            preferred_element_type=F32,
        )
        grad[qs, :, 2 * HEAD : 3 * HEAD] = (
            dq_s[...] * SCALE * silu_grad(p_g[qs, :, 2 * HEAD : 3 * HEAD])
        ).astype(BF)
        other = 2 * qs + 1 - core
        sib_send[qs, :, 0:HEAD] = dk_s[other].astype(BF)
        sib_send[qs, :, HEAD : 2 * HEAD] = dv_s[other].astype(BF)
        sib_copy(qs).start()
        return carry

    lax.fori_loop(0, CHIPS, backward, 0)

    hist = hist_s[1, 0:128, :]
    shape = (128, 128)
    gap = (iota(shape, 0) - iota(shape, 1)) & 15
    rows = [
        jnp.sum(jnp.where(gap == b, hist, 0.0), axis=0, keepdims=True) for b in range(LEVELS - 1)
    ]
    total = jnp.sum(tot_s[...], axis=0, keepdims=True)
    rows.append(total[:, 0:128] + total[:, 128:256] - sum(rows))
    levels = jnp.sum(jnp.concatenate(rows, axis=0), axis=1, keepdims=True)
    bias[...] = sbias[...] + jnp.where(iota((LEVELS, 128), 1) == chip, levels, 0.0)

    def finish(step, carry):
        qs = CHIPS - 1 - step
        sib_copy(qs).wait_recv()
        mine = 2 * qs + core
        dk = (dk_s[mine] + sib_recv[qs, :, 0:HEAD].astype(F32)) * SCALE
        dv = dv_s[mine] + sib_recv[qs, :, HEAD : 2 * HEAD].astype(F32)
        grad[qs, :, HEAD : 2 * HEAD] = (dv * silu_grad(p_g[qs, :, HEAD : 2 * HEAD])).astype(BF)
        grad[qs, :, 3 * HEAD : 4 * HEAD] = (
            dk * silu_grad(p_g[qs, :, 3 * HEAD : 4 * HEAD])
        ).astype(BF)
        return carry

    lax.fori_loop(0, CHIPS, finish, 0)

    def wait_o(o, carry):
        src = lax.rem(dp + n_dp - o, n_dp)
        remote(outbuf.at[src], orecv.at[src], o_s.at[o], o_r.at[o], src, ctx).wait_recv()
        return carry

    lax.fori_loop(1, n_dp, wait_o, 0)
    short_out[...] = dot_tn(
        place_m[...], orecv[...].reshape(n_dp * SLEN, BLOCK)
    ).astype(BF)
    for d in (1, 3, 2):
        src = lax.rem(chip + CHIPS - d, CHIPS)
        remote(stok, stok_g.at[src], st_s.at[d], st_r.at[d], dp, sib).wait_recv()
        remote(sgrad.at[src], sgrad_g.at[src], sg_s.at[d], sg_r.at[d], dp, sib).wait_recv()
        st_copy(d).wait_send()
        sg_copy(d).wait_send()

    def ended_q(qs, carry):
        sib_copy(qs).wait_send()
        for d in (1, 3, 2):
            stat_copy(qs, d).wait_send()
        return carry

    lax.fori_loop(0, CHIPS, ended_q, 0)

    def ended(o, carry):
        o_copy(o).wait_send()
        return carry

    lax.fori_loop(1, n_dp, ended, 0)


def finish_kernel(
    n_dp,
    part,
    grad,
    out,
    tok_g,
    stok_g,
    sgrad_g,
    bias,
    w,
    long_out,
    token_grad,
    proj_grad,
    bias_out,
    wh,
    grad_h,
    half_send,
    half_recv,
    own,
    rs_send,
    rs_recv,
    b_dp,
    b_mid,
    b_ctx,
    piece,
    w_sem,
    g_s,
    g_r,
    l_s,
    l_r,
    p_s,
    p_r,
    rs_s,
    rs_r,
    b1_s,
    b1_r,
    b2_s,
    b2_r,
    f_s,
    f_r,
):
    dp, ctx, chip, core = place()
    sib = ctx + 1 - 2 * core

    def w_copy(h, k):
        return pltpu.make_async_copy(
            w.at[:, k * BLOCK + h * HEAD : k * BLOCK + (h + 1) * HEAD],
            wh.at[h, :, k * HEAD : (k + 1) * HEAD],
            w_sem.at[h, k],
        )

    for h in range(4):
        for k in range(4):
            w_copy(h, k).start()
    greet(dp, ctx, n_dp)

    def g_copy(d):
        peer = lax.rem(chip + d, CHIPS)
        return remote(grad.at[peer], grad_h.at[chip], g_s.at[d], g_r.at[d], dp, 2 * peer + core)

    def l_copy(d):
        peer = lax.rem(chip + d, CHIPS)
        return remote(
            out.at[peer],
            long_out.at[:, pl.ds(pl.multiple_of(chip * HEAD, HEAD), HEAD)],
            l_s.at[d],
            l_r.at[d],
            dp,
            2 * peer + core,
        )

    def b1_copy(o):
        return remote(bias, b_dp.at[dp], b1_s.at[o], b1_r.at[o], lax.rem(dp + o, n_dp), ctx)

    def b2_copy(o):
        return remote(
            b_mid, b_ctx.at[ctx], b2_s.at[o], b2_r.at[o], dp, lax.rem(ctx + o, 2 * CHIPS)
        )

    def rs_copy(o):
        peer = lax.rem(dp + o, n_dp)
        return remote(rs_send.at[peer], rs_recv.at[dp], rs_s.at[o], rs_r.at[o], peer, ctx)

    for d in (1, 3, 2):
        g_copy(d).start()
    for d in (1, 3, 2):
        l_copy(d).start()

    def start_b1(o, carry):
        b1_copy(o).start()
        return carry

    lax.fori_loop(1, n_dp, start_b1, 0)
    b_dp[dp] = bias[...]
    grad_h[chip] = grad[chip]
    long_out[:, pl.ds(pl.multiple_of(chip * HEAD, HEAD), HEAD)] = out[chip]

    def outer(cols, target):
        def one(s, carry):
            a = dot_tn(tok_g[s], grad[s, :, pl.ds(cols, 2 * HEAD)])
            b = dot_tn(stok_g[s], sgrad_g[s, :, pl.ds(cols, 2 * HEAD)])

            @pl.when(s == 0)
            def _():
                target[...] = a + b

            @pl.when(s > 0)
            def _():
                target[...] += a + b

            return carry

        lax.fori_loop(0, CHIPS, one, 0)

    outer(pl.multiple_of((1 - core) * 2 * HEAD, 2 * HEAD), own)
    half_send[...] = own[...].astype(BF)
    pair = remote(half_send, half_recv, p_s, p_r, dp, sib)
    pair.start()
    outer(pl.multiple_of(core * 2 * HEAD, 2 * HEAD), own)
    pair.wait_recv()
    rs_send[...] = (own[...] + half_recv[...].astype(F32)).astype(BF).reshape(rs_send.shape)

    def start_rs(o, carry):
        rs_copy(o).start()
        return carry

    lax.fori_loop(1, n_dp, start_rs, 0)
    rs_recv[dp] = rs_send[dp]

    def wait_b1(o, carry):
        src = lax.rem(dp + n_dp - o, n_dp)
        remote(bias, b_dp.at[src], b1_s.at[o], b1_r.at[o], src, ctx).wait_recv()
        return carry

    lax.fori_loop(1, n_dp, wait_b1, 0)
    b_mid[...] = jnp.sum(b_dp[...], axis=0)

    def start_b2(o, carry):
        b2_copy(o).start()
        return carry

    lax.fori_loop(1, 2 * CHIPS, start_b2, 0)
    b_ctx[ctx] = b_mid[...]

    for h in range(4):
        for k in range(4):
            w_copy(h, k).wait()

    total = jnp.zeros((ROWS, MODEL), F32)
    for d in (0, 1, 3, 2):
        src = lax.rem(chip + CHIPS - d, CHIPS)
        if d:
            remote(grad.at[src], grad_h.at[src], g_s.at[d], g_r.at[d], dp, sib).wait_recv()
        total = total + dot_nt(grad_h[src], wh[src])
    token_grad[...] = total.astype(BF)

    def wait_rs(o, carry):
        src = lax.rem(dp + n_dp - o, n_dp)
        remote(rs_send.at[src], rs_recv.at[src], rs_s.at[o], rs_r.at[o], src, ctx).wait_recv()
        return carry

    lax.fori_loop(1, n_dp, wait_rs, 0)
    piece[...] = jnp.sum(rs_recv[...].astype(F32), axis=0)

    col_out = pl.multiple_of(lax.rem(chip, 2) * HEAD, HEAD)
    mine = lax.rem(chip, 2)

    def f_copy(i):
        target = 2 * (2 * core + i) + lax.div(chip, 2)
        return target, remote(
            piece.at[:, i * HEAD : (i + 1) * HEAD],
            proj_grad.at[:, pl.ds(col_out, HEAD)],
            f_s.at[i],
            f_r.at[mine],
            dp,
            target,
        )

    for i in range(2):
        target, copy = f_copy(i)

        @pl.when(target != ctx)
        def _():
            copy.start()

        @pl.when(target == ctx)
        def _():
            proj_grad[:, pl.ds(col_out, HEAD)] = piece[:, i * HEAD : (i + 1) * HEAD]

    def wait_b2(o, carry):
        src = lax.rem(ctx + 2 * CHIPS - o, 2 * CHIPS)
        remote(b_mid, b_ctx.at[src], b2_s.at[o], b2_r.at[o], dp, src).wait_recv()
        return carry

    lax.fori_loop(1, 2 * CHIPS, wait_b2, 0)
    bias_out[...] = jnp.sum(b_ctx[...], axis=0)
    for d in (1, 3, 2):
        src = lax.rem(chip + CHIPS - d, CHIPS)
        remote(
            out.at[src],
            long_out.at[:, pl.ds(pl.multiple_of(src * HEAD, HEAD), HEAD)],
            l_s.at[d],
            l_r.at[d],
            dp,
            sib,
        ).wait_recv()
    for half in range(2):
        source = 2 * (2 * core + half) + lax.div(chip, 2)

        @pl.when(source != ctx)
        def _():
            remote(
                piece.at[:, 0:HEAD],
                proj_grad.at[:, half * HEAD : (half + 1) * HEAD],
                f_s.at[half],
                f_r.at[half],
                dp,
                source,
            ).wait_recv()

    for i in range(2):
        target, copy = f_copy(i)

        @pl.when(target != ctx)
        def _():
            copy.wait_send()

    for d in (1, 3, 2):
        g_copy(d).wait_send()
        l_copy(d).wait_send()
    pair.wait_send()

    def ended(o, carry):
        rs_copy(o).wait_send()
        b1_copy(o).wait_send()
        return carry

    lax.fori_loop(1, n_dp, ended, 0)

    def ended_b2(o, carry):
        b2_copy(o).wait_send()
        return carry

    lax.fori_loop(1, 2 * CHIPS, ended_b2, 0)


VM = pl.BlockSpec(memory_space=pltpu.VMEM)
ANY = pl.BlockSpec(memory_space=pl.ANY)
DMA = pltpu.SemaphoreType.DMA


def shaped(shape, dtype):
    return jax.ShapeDtypeStruct(shape, dtype)


def params(collective):
    if collective is None:
        return pltpu.CompilerParams(vmem_limit_bytes=VMEM_LIMIT)
    return pltpu.CompilerParams(
        vmem_limit_bytes=VMEM_LIMIT, collective_id=collective, has_side_effects=True
    )


def per_device(
    n_dp,
    long_tokens,
    short_tokens,
    projection,
    time_bias,
    long_length,
    short_length,
    long_time,
    short_time,
    destination,
    long_cotangent,
    short_cotangent,
):
    lanes = jnp.zeros((1, 120), jnp.int32) - 1
    target = destination[0]
    meta = jnp.concatenate(
        [
            long_time.reshape(2, 128),
            short_time.reshape(1, 128),
            jnp.repeat(short_length[0], SLEN)[None],
            jnp.repeat(target, SLEN)[None],
            jnp.concatenate([target[None], lanes], axis=1),
            jnp.broadcast_to(long_length[:, None], (1, 128)),
            jnp.zeros((1, 128), jnp.int32),
        ],
        axis=0,
    )
    table = jnp.pad(time_bias, ((0, 4), (0, 128 - LEVELS)))
    stok = short_tokens.reshape(SHORT, MODEL)
    scot = short_cotangent.reshape(SHORT, BLOCK)

    tok_g, p_g, act, kv, c_g, times, c_home, place_m = pl.pallas_call(
        functools.partial(gather_kernel, n_dp),
        out_shape=(
            shaped((CHIPS, ROWS, MODEL), BF),
            shaped((CHIPS, ROWS, BLOCK), F32),
            shaped((CHIPS, ROWS, BLOCK), BF),
            shaped((2 * CHIPS, ROWS, 2 * HEAD), BF),
            shaped((CHIPS, ROWS, HEAD), BF),
            shaped((2 * CHIPS, 8, 128), jnp.int32),
            shaped((SHORT, BLOCK), BF),
            shaped((n_dp * SLEN, 128), BF),
        ),
        in_specs=[VM, ANY, VM, VM, VM],
        out_specs=(VM,) * 8,
        scratch_shapes=[
            pltpu.VMEM((MODEL, BLOCK), BF),
            pltpu.VMEM((8, 128), jnp.int32),
            pltpu.VMEM((n_dp, 8, 128), jnp.int32),
            pltpu.VMEM((n_dp, SLEN, BLOCK), BF),
            pltpu.VMEM((n_dp, SLEN, BLOCK), BF),
            DMA((4,)),
            DMA((CHIPS,)),
            DMA((CHIPS,)),
            DMA((CHIPS,)),
            DMA((CHIPS,)),
            DMA((2 * CHIPS,)),
            DMA((2 * CHIPS,)),
            DMA((CHIPS,)),
            DMA((CHIPS,)),
            DMA((n_dp,)),
            DMA((n_dp,)),
            DMA((n_dp,)),
            DMA((n_dp,)),
        ],
        compiler_params=params(0),
        name="gather",
    )(long_tokens[0], projection, long_cotangent[0], meta, scot)

    short_grad, grad_heads, outbuf, sbias = pl.pallas_call(
        functools.partial(short_kernel, n_dp),
        out_shape=(
            shaped((SHORT, MODEL), BF),
            shaped((CHIPS, SHORT, BLOCK), BF),
            shaped((n_dp, SLEN, BLOCK), BF),
            shaped((LEVELS, 128), F32),
        ),
        in_specs=[VM] * 5,
        out_specs=(VM,) * 4,
        scratch_shapes=[
            pltpu.VMEM((SHORT, 4 * BLOCK), F32),
            pltpu.VMEM((SHORT, 4 * BLOCK), BF),
        ],
        compiler_params=params(None),
        name="short",
    )(stok, projection, c_home, meta, table)

    grad, out, bias, stok_g, sgrad_g, short_out = pl.pallas_call(
        functools.partial(attend_kernel, n_dp),
        out_shape=(
            shaped((CHIPS, ROWS, BLOCK), BF),
            shaped((CHIPS, ROWS, HEAD), BF),
            shaped((LEVELS, 128), F32),
            shaped((CHIPS, SHORT, MODEL), BF),
            shaped((CHIPS, SHORT, BLOCK), BF),
            shaped((SHORT, BLOCK), BF),
        ),
        in_specs=[VM] * 11,
        out_specs=(VM,) * 6,
        scratch_shapes=[
            pltpu.VMEM((n_dp, SLEN, BLOCK), BF),
            pltpu.VMEM((CHIPS, 2 * CHIPS, ROWS, ROWS), BF),
            pltpu.VMEM((CHIPS, 2 * CHIPS, ROWS, ROWS), F32),
            pltpu.VMEM((CHIPS, ROWS, HEAD), F32),
            pltpu.VMEM((2 * CHIPS, ROWS, 128), BF),
            pltpu.VMEM((2 * CHIPS, ROWS, 128), F32),
            pltpu.VMEM((2 * CHIPS, 8, ROWS), F32),
            pltpu.VMEM((CHIPS, CHIPS, 8, ROWS), F32),
            pltpu.VMEM((2 * CHIPS, ROWS, HEAD), F32),
            pltpu.VMEM((2 * CHIPS, ROWS, HEAD), F32),
            pltpu.VMEM((ROWS, HEAD), F32),
            pltpu.VMEM((2, ROWS, 128), F32),
            pltpu.VMEM((8, ROWS), F32),
            pltpu.VMEM((CHIPS, ROWS, 2 * HEAD), BF),
            pltpu.VMEM((CHIPS, ROWS, 2 * HEAD), BF),
            DMA((CHIPS,)),
            DMA((CHIPS,)),
            DMA((CHIPS,)),
            DMA((CHIPS,)),
            DMA((n_dp,)),
            DMA((n_dp,)),
            DMA((CHIPS, CHIPS)),
            DMA((CHIPS, CHIPS)),
            DMA((CHIPS,)),
            DMA((CHIPS,)),
        ],
        compiler_params=params(1),
        name="attend",
    )(act, p_g, kv, c_g, times, table, stok, grad_heads, outbuf, place_m, sbias)

    part = MODEL // n_dp
    long_out, token_grad, proj_grad, bias_out = pl.pallas_call(
        functools.partial(finish_kernel, n_dp, part),
        out_shape=(
            shaped((ROWS, BLOCK), BF),
            shaped((ROWS, MODEL), BF),
            shaped((part, 2 * HEAD), F32),
            shaped((LEVELS, 128), F32),
        ),
        in_specs=[VM] * 6 + [ANY],
        out_specs=(VM,) * 4,
        scratch_shapes=[
            pltpu.VMEM((CHIPS, MODEL, BLOCK), BF),
            pltpu.VMEM((CHIPS, ROWS, BLOCK), BF),
            pltpu.VMEM((MODEL, 2 * HEAD), BF),
            pltpu.VMEM((MODEL, 2 * HEAD), BF),
            pltpu.VMEM((MODEL, 2 * HEAD), F32),
            pltpu.VMEM((n_dp, part, 2 * HEAD), BF),
            pltpu.VMEM((n_dp, part, 2 * HEAD), BF),
            pltpu.VMEM((n_dp, LEVELS, 128), F32),
            pltpu.VMEM((LEVELS, 128), F32),
            pltpu.VMEM((2 * CHIPS, LEVELS, 128), F32),
            pltpu.VMEM((part, 2 * HEAD), F32),
            DMA((4, 4)),
            DMA((CHIPS,)),
            DMA((CHIPS,)),
            DMA((CHIPS,)),
            DMA((CHIPS,)),
            DMA,
            DMA,
            DMA((n_dp,)),
            DMA((n_dp,)),
            DMA((n_dp,)),
            DMA((n_dp,)),
            DMA((2 * CHIPS,)),
            DMA((2 * CHIPS,)),
            DMA((2,)),
            DMA((2,)),
        ],
        compiler_params=params(2),
        name="finish",
    )(grad, out, tok_g, stok_g, sgrad_g, bias, projection)
    return (
        long_out[None],
        short_out.reshape(short_cotangent.shape),
        token_grad[None],
        short_grad.reshape(short_tokens.shape),
        proj_grad,
        jnp.transpose(bias_out[:, 0:4]),
    )


def solution(mesh):
    return jax.shard_map(
        functools.partial(per_device, mesh.shape["dp"]),
        mesh=mesh,
        in_specs=(
            P("dp", "ctx", None),
            P("dp", "ctx", None, None),
            P(),
            P(),
            P("dp"),
            P("dp", "ctx"),
            P("dp", "ctx"),
            P("dp", "ctx", None),
            P("dp", "ctx"),
            P("dp", "ctx", None),
            P("dp", "ctx", None, None),
        ),
        out_specs=(
            P("dp", "ctx", None),
            P("dp", "ctx", None, None),
            P("dp", "ctx", None),
            P("dp", "ctx", None, None),
            P("dp", "ctx"),
            P(),
        ),
        check_vma=False,
    )
```

```python
import functools

import jax
import jax.numpy as jnp
from jax import lax
from jax.experimental import pallas as pl
from jax.experimental.pallas import tpu as pltpu
from jax.sharding import PartitionSpec as P

epsilon = 1e-05
MESH = pl.DeviceIdType.MESH
BF = jnp.bfloat16
F32 = jnp.float32
CHIPS = 4
ROWS = 256
HEAD = 128
LEVELS = 16
SLEN = 16
SHORT = 128
LONG_ROWS = CHIPS * ROWS
ALL_ROWS = CHIPS * (ROWS + SHORT)
PAIR = 2 * ROWS
MODEL = 1024
BLOCK = 512
SCALE = HEAD ** (-0.5)
VMEM_LIMIT = 56 * 1024 * 1024


def sigmoid(value):
    return 0.5 * jnp.tanh(0.5 * value) + 0.5


def silu_grad(value):
    sigma = sigmoid(value)
    return sigma * (1.0 + value * (1.0 - sigma))


def dot_nn(a, b):
    return jnp.dot(a, b, preferred_element_type=F32)


def dot_nt(a, b):
    return lax.dot_general(a, b, (((1,), (1,)), ((), ())), preferred_element_type=F32)


def dot_tn(a, b):
    return lax.dot_general(a, b, (((0,), (0,)), ((), ())), preferred_element_type=F32)


def column_of(row):
    return jnp.transpose(jnp.broadcast_to(row, (128, 128)))


def iota(shape, axis):
    return lax.broadcasted_iota(jnp.int32, shape, axis)


def remote(src, dst, send_sem, recv_sem, dp, ctx):
    return pltpu.make_async_remote_copy(
        src_ref=src,
        dst_ref=dst,
        send_sem=send_sem,
        recv_sem=recv_sem,
        device_id=(dp, ctx),
        device_id_type=MESH,
    )


def place():
    dp = lax.axis_index("dp")
    ctx = lax.axis_index("ctx")
    return dp, ctx, lax.div(ctx, 2), lax.rem(ctx, 2)


def lookup(table, diff):
    index = jnp.clip(diff, 0.0, LEVELS - 1.0).astype(jnp.int32)
    parts = [
        jnp.take_along_axis(table, index[:, i : i + 128], axis=1)
        for i in range(0, index.shape[1], 128)
    ]
    return parts[0] if len(parts) == 1 else jnp.concatenate(parts, axis=1)


def exact_dot(a, b):
    return lax.dot_general(
        a,
        b,
        (((1,), (0,)), ((), ())),
        precision=lax.Precision.HIGHEST,
        preferred_element_type=F32,
    )


def rows_at(block, rows):
    return pl.ds(pl.multiple_of(block * rows, rows), rows)


def lanes_at(block):
    return pl.ds(pl.multiple_of(block * HEAD, HEAD), HEAD)


def layer_kernel(
    n_dp,
    tok,
    stok,
    w,
    lcot,
    scot,
    ltime,
    stime,
    slen,
    dest_in,
    llen,
    tbias,
    long_out,
    short_out,
    token_grad,
    short_grad,
    proj_grad,
    bias_out,
    wh,
    tok_all,
    grad_all,
    p_s,
    act_s,
    kv,
    c_g,
    tmeta,
    times,
    tab_s,
    ints,
    dtile,
    dest_g,
    place_s,
    cbuf,
    crecv,
    sp_s,
    sact_s,
    sweight_s,
    sslope_s,
    snorm_s,
    sscale_s,
    c_home,
    sgrad_s,
    obuf,
    orecv,
    sbias_s,
    weight_s,
    slope_s,
    mixed_s,
    out_s,
    hot_s,
    tcol_s,
    stat_s,
    dk_s,
    dv_s,
    dq_s,
    hist_s,
    htot_s,
    tot_s,
    sib_send,
    sib_recv,
    grad_h,
    half_send,
    half_recv,
    own,
    rs_send,
    rs_recv,
    b_send,
    b_dp,
    b_mid,
    b_ctx,
    piece,
    w_sem,
    tok_s,
    tok_r,
    fwd_s,
    fwd_r,
    c_s,
    c_r,
    t_s,
    t_r,
    kv_s,
    kv_r,
    st_s,
    st_r,
    sg_s,
    sg_r,
    d_s,
    d_r,
    s_s,
    s_r,
    o_s,
    o_r,
    stat_ss,
    stat_sr,
    sib_s,
    sib_r,
    g_s,
    g_r,
    l_s,
    l_r,
    p_ss,
    p_sr,
    rs_s,
    rs_r,
    b1_s,
    b1_r,
    b2_s,
    b2_r,
    f_s,
    f_r,
):
    dp, ctx, chip, core = place()
    sib = ctx + 1 - 2 * core
    up = lax.rem(chip + 1, CHIPS)
    down = lax.rem(chip + CHIPS - 1, CHIPS)
    far = lax.rem(chip + 2, CHIPS)
    half_rows = ROWS // 2
    barrier = pltpu.get_barrier_semaphore()

    def greet_ctx(o, carry):
        pl.semaphore_signal(
            barrier, inc=1, device_id=(dp, lax.rem(ctx + o, 2 * CHIPS)), device_id_type=MESH
        )
        return carry

    def greet_dp(o, carry):
        pl.semaphore_signal(
            barrier, inc=1, device_id=(lax.rem(dp + o, n_dp), ctx), device_id_type=MESH
        )
        return carry

    lax.fori_loop(1, 2 * CHIPS, greet_ctx, 0)
    lax.fori_loop(1, n_dp, greet_dp, 0)

    def w_copy(h, k):
        return pltpu.make_async_copy(
            w.at[:, k * BLOCK + h * HEAD : k * BLOCK + (h + 1) * HEAD],
            wh.at[h, :, k * HEAD : (k + 1) * HEAD],
            w_sem.at[h, k],
        )

    for h in range(4):
        for k in range(4):
            w_copy(h, k).start()
    tmeta[...] = jnp.broadcast_to(ltime[...], (8, ROWS))
    ints[...] = jnp.zeros((8, 128), jnp.int32) - 1
    ints[0:1, 0:8] = slen[...]
    ints[1:2, 0:8] = dest_in[...]
    dtile[...] = jnp.broadcast_to(ints[1:2, :], (8, 128))
    tab_s[...] = jnp.zeros_like(tab_s)
    tab_s[0:4, 0:LEVELS] = tbias[...]

    def half_copy(peer, half, index):
        return remote(
            tok.at[half * half_rows : (half + 1) * half_rows, :],
            tok_all.at[rows_at(2 * chip + half, half_rows), :],
            tok_s.at[index, half],
            tok_r.at[index, half],
            dp,
            2 * peer + core,
        )

    def half_wait(src, half, index):
        here = tok_all.at[rows_at(2 * src + half, half_rows), :]
        remote(here, here, tok_s.at[index, half], tok_r.at[index, half], dp, sib).wait_recv()

    def pass_copy(src, half, peer):
        here = tok_all.at[rows_at(2 * src + half, half_rows), :]
        return remote(here, here, fwd_s.at[half], fwd_r.at[half], dp, 2 * peer + core)

    def c_copy(d):
        peer = lax.rem(chip + d, CHIPS)
        return remote(
            lcot.at[:, lanes_at(peer)], c_g.at[chip], c_s.at[d], c_r.at[d], dp, 2 * peer + core
        )

    def t_copy(o):
        return remote(
            tmeta, times.at[ctx], t_s.at[o], t_r.at[o], dp, lax.rem(ctx + o, 2 * CHIPS)
        )

    def kv_copy(src):
        here = kv.at[rows_at(2 * src + core, ROWS), :]
        return remote(here, here, kv_s.at[src], kv_r.at[src], dp, sib)

    def kv_wait(src):
        here = kv.at[rows_at(2 * src + 1 - core, ROWS), :]
        remote(here, here, kv_s.at[src], kv_r.at[src], dp, sib).wait_recv()

    def st_copy(d):
        return remote(
            stok,
            tok_all.at[pl.ds(pl.multiple_of(LONG_ROWS + chip * SHORT, SHORT), SHORT), :],
            st_s.at[d],
            st_r.at[d],
            dp,
            2 * lax.rem(chip + d, CHIPS) + core,
        )

    def sg_copy(d):
        peer = lax.rem(chip + d, CHIPS)
        return remote(
            sgrad_s.at[peer],
            grad_all.at[pl.ds(pl.multiple_of(LONG_ROWS + chip * SHORT, SHORT), SHORT), :],
            sg_s.at[d],
            sg_r.at[d],
            dp,
            2 * peer + core,
        )

    def dp_start(source, target, send, recv):
        def one(o, carry):
            peer = lax.rem(dp + o, n_dp)
            remote(source.at[peer], target.at[dp], send, recv, peer, ctx).start()
            return carry

        lax.fori_loop(1, n_dp, one, 0)

    def dp_all(source, target, send, recv):
        return remote(
            source.at[0 : n_dp - 1], target.at[0 : n_dp - 1], send, recv, dp, sib
        )

    def one_start(source, target, send, recv):
        def one(o, carry):
            remote(source, target.at[dp], send, recv, lax.rem(dp + o, n_dp), ctx).start()
            return carry

        lax.fori_loop(1, n_dp, one, 0)

    def one_all(target, send, recv):
        here = target.at[0 : n_dp - 1]
        return remote(here, here, send, recv, dp, sib)

    pl.semaphore_wait(barrier, n_dp - 1 + 2 * CHIPS - 1)
    half_copy(up, 0, 0).start()
    half_copy(down, 1, 1).start()
    half_copy(up, 1, 0).start()
    half_copy(down, 0, 1).start()
    one_start(dtile, dest_g, d_s, d_r)

    def start_t(o, carry):
        t_copy(o).start()
        return carry

    lax.fori_loop(1, 2 * CHIPS, start_t, 0)
    tok_all[rows_at(chip, ROWS), :] = tok[...]
    tok_all[pl.ds(pl.multiple_of(LONG_ROWS + chip * SHORT, SHORT), SHORT), :] = stok[...]
    c_g[chip] = lcot[:, lanes_at(chip)]
    times[ctx] = tmeta[...]
    dest_g[dp] = dtile[...]
    for h in range(4):
        for k in range(4):
            w_copy(h, k).wait()

    def project(src):
        projected = dot_nn(tok_all[rows_at(src, ROWS), :], wh[chip])
        p_s[src] = projected
        act = (projected * sigmoid(projected)).astype(BF)
        act_s[src] = act
        kv[rows_at(2 * src + core, ROWS), 0:HEAD] = act[:, 3 * HEAD : 4 * HEAD]
        kv[rows_at(2 * src + core, ROWS), HEAD : 2 * HEAD] = act[:, HEAD : 2 * HEAD]
        kv_copy(src).start()

    project(chip)

    lane16 = iota((16, 128), 1)
    spread_time = exact_dot(
        stime[0].astype(F32), jnp.where((lane16 & 15) == iota((16, 128), 0), 1.0, 0.0)
    )
    pick = (iota((8, 128), 1) >> 4) == iota((8, 128), 0)
    stime_row = jnp.sum(jnp.where(pick, spread_time, 0.0), axis=0, keepdims=True)
    repeat = jnp.where((iota((128, 128), 1) >> 4) == iota((128, 128), 0), 1.0, 0.0)
    rep_rows = exact_dot(ints[...].astype(F32), repeat)
    slen_row, home_row = rep_rows[0:1, :], rep_rows[1:2, :]
    owner_row = (home_row.astype(jnp.int32) >> 3).astype(F32)
    shape = (SHORT, SHORT)
    row = iota(shape, 0)
    col = iota(shape, 1)
    stime_diff = column_of(stime_row) - stime_row
    inside = (row & 15).astype(F32) < column_of(slen_row)
    svisible = ((row >> 4) == (col >> 4)) & (col <= row) & inside

    half_wait(down, 0, 0)
    pass_copy(down, 0, up).start()
    half_wait(up, 1, 1)
    pass_copy(up, 1, down).start()
    for d in (1, 3, 2):
        c_copy(d).start()

    one_all(dest_g, d_s, d_r).wait_recv()
    dest = dest_g[...]
    code = jnp.sum(
        jnp.where((dest >> 3) == dp, ((dest & 7) + 1).astype(F32), 0.0), axis=2, keepdims=True
    )
    code = jnp.broadcast_to(code, (n_dp, 8, 128))
    code = jnp.concatenate([code, code], axis=1).reshape(n_dp * SLEN, 128)
    shape = (n_dp * SLEN, 128)
    same = (iota(shape, 0) & 15) == (iota(shape, 1) & 15)
    slot = ((iota(shape, 1) >> 4) + 1).astype(F32)
    placer = jnp.where(same & (code == slot), 1.0, 0.0).astype(BF)
    place_s[...] = placer
    cbuf[...] = dot_nn(placer, scot[...]).astype(BF).reshape(cbuf.shape)
    dp_start(cbuf, crecv, s_s, s_r)
    crecv[dp] = cbuf[dp]

    short_tokens = stok[...]
    mixes = []
    for h in range(4):
        projected = dot_nn(short_tokens, wh[h])
        sp_s[h] = projected
        act = (projected * sigmoid(projected)).astype(BF)
        sact_s[h] = act
        queries, keys = act[:, 2 * HEAD : 3 * HEAD], act[:, 3 * HEAD : 4 * HEAD]
        tab = jnp.broadcast_to(tab_s[h : h + 1, :], (SHORT, 128))
        total = dot_nt(queries, keys) * SCALE + lookup(tab, stime_diff)
        sg = sigmoid(total)
        weight = total * sg
        weight16 = jnp.where(svisible, weight, 0.0).astype(BF)
        sweight_s[h] = weight16
        sslope_s[h] = jnp.where(svisible, sg + weight * (1.0 - sg), 0.0)
        mixes.append(dot_nn(weight16, act[:, HEAD : 2 * HEAD]))
    mean = sum(jnp.sum(m, axis=1, keepdims=True) for m in mixes) * (1.0 / BLOCK)
    centred = [m - mean for m in mixes]
    spread = sum(jnp.sum(m * m, axis=1, keepdims=True) for m in centred) * (1.0 / BLOCK)
    scale = lax.rsqrt(spread + epsilon)
    sscale_s[...] = jnp.broadcast_to(scale, sscale_s.shape)
    for h in range(4):
        snorm_s[h] = centred[h] * scale

    half_wait(down, 1, 0)
    project(down)
    half_wait(up, 0, 1)
    project(up)

    def wait_t(o, carry):
        src = lax.rem(ctx + 2 * CHIPS - o, 2 * CHIPS)
        remote(tmeta, times.at[src], t_s.at[o], t_r.at[o], dp, src).wait_recv()
        return carry

    lax.fori_loop(1, 2 * CHIPS, wait_t, 0)
    lane = iota((ROWS, 128), 1)

    def times_of(b, carry):
        line = times[b, 0:1, :].astype(F32)
        column = jnp.concatenate(
            [column_of(line[:, 0:128]), column_of(line[:, 128:256])], axis=0
        )
        tcol_s[b] = column
        hot_s[rows_at(b, ROWS), :] = jnp.where(
            (column.astype(jnp.int32) & 15) == lane, 1.0, 0.0
        ).astype(BF)
        return carry

    lax.fori_loop(0, 2 * CHIPS, times_of, 0)
    dk_s[...] = jnp.zeros_like(dk_s)
    dv_s[...] = jnp.zeros_like(dv_s)
    htot_s[...] = jnp.zeros_like(htot_s)
    tot_s[...] = jnp.zeros_like(tot_s)

    for half in range(2):
        here = tok_all.at[rows_at(2 * far + half, half_rows), :]
        remote(here, here, fwd_s.at[half], fwd_r.at[half], dp, sib).wait_recv()
    project(far)
    for d in (1, 3, 2):
        st_copy(d).start()
    for d in (1, 3, 2):
        src = lax.rem(chip + CHIPS - d, CHIPS)
        remote(c_g.at[src], c_g.at[src], c_s.at[d], c_r.at[d], dp, sib).wait_recv()
    for src in range(CHIPS):
        kv_wait(src)

    table = jnp.broadcast_to(tab_s[pl.ds(chip, 1), :], (ROWS, 128))
    length = llen[0]

    def stat_copy(qs, d):
        here = stat_s.at[qs, chip]
        return remote(
            here,
            here,
            stat_ss.at[qs, d],
            stat_sr.at[qs, d],
            dp,
            2 * lax.rem(chip + d, CHIPS) + core,
        )

    def key_times(p):
        return jnp.concatenate(
            [times[2 * p, 0:1, :], times[2 * p + 1, 0:1, :]], axis=1
        ).astype(F32)

    def forward(step, carry):
        qs = CHIPS - 1 - step
        block = 2 * qs + core
        queries = act_s[qs, :, 2 * HEAD : 3 * HEAD]
        tq = tcol_s[block][:, 0:1]
        spot = iota((ROWS, 1), 0) + block * ROWS
        limit = jnp.where(spot < length, spot, -1)
        mixed_s[qs] = jnp.zeros((ROWS, HEAD), F32)

        def tile(p, carry):
            keys = kv[rows_at(p, PAIR), 0:HEAD]
            values = kv[rows_at(p, PAIR), HEAD : 2 * HEAD]
            total = dot_nt(queries, keys) * SCALE + lookup(table, tq - key_times(p))
            sg = sigmoid(total)
            weight = total * sg
            visible = (iota((ROWS, PAIR), 1) + p * PAIR) <= limit
            weight16 = jnp.where(visible, weight, 0.0).astype(BF)
            weight_s[qs, p] = weight16
            slope_s[qs, p] = jnp.where(visible, sg + weight * (1.0 - sg), 0.0)
            mixed_s[qs] += dot_nn(weight16, values)
            return carry

        lax.fori_loop(0, qs + 1, tile, 0)
        mixed = mixed_s[qs]
        q = c_g[qs].astype(F32) * act_s[qs, :, 0:HEAD].astype(F32)
        s1 = jnp.sum(mixed, axis=1, keepdims=True)
        centred = mixed - s1 * (1.0 / HEAD)
        s2 = jnp.sum(centred * centred, axis=1, keepdims=True)
        s3 = jnp.sum(q, axis=1, keepdims=True)
        s4 = jnp.sum(q * centred, axis=1, keepdims=True)
        stats = jnp.where(
            lane == 0, s1, jnp.where(lane == 1, s2, jnp.where(lane == 2, s3, s4))
        )
        stat_s[qs, chip] = jnp.transpose(stats)[0:8, :]
        for d in (1, 3, 2):
            stat_copy(qs, d).start()
        return carry

    lax.fori_loop(0, CHIPS, forward, 0)

    dp_all(cbuf, crecv, s_s, s_r).wait_recv()
    owner = jnp.concatenate([column_of(owner_row)] * (n_dp * SLEN // 128), axis=1)
    shape = (SHORT, n_dp * SLEN)
    same = (iota(shape, 0) & 15) == (iota(shape, 1) & 15)
    chooser = jnp.where(
        same & (owner == (iota(shape, 1) >> 4).astype(F32)), 1.0, 0.0
    ).astype(BF)
    c_home[...] = dot_nn(chooser, crecv[...].reshape(n_dp * SLEN, BLOCK))
    scale = sscale_s[:, 0:1]
    mean_q = jnp.zeros((SHORT, 1), F32)
    mean_qn = jnp.zeros((SHORT, 1), F32)
    for h in range(4):
        q = c_home[:, h * HEAD : (h + 1) * HEAD] * sact_s[h, :, 0:HEAD].astype(F32)
        mean_q = mean_q + jnp.sum(q, axis=1, keepdims=True)
        mean_qn = mean_qn + jnp.sum(q * snorm_s[h], axis=1, keepdims=True)
    mean_q = mean_q * (1.0 / BLOCK)
    mean_qn = mean_qn * (1.0 / BLOCK)
    bucket = jnp.clip(stime_diff, 0.0, LEVELS - 1.0).astype(jnp.int32)
    level_lane = iota((LEVELS, 128), 1)
    sums = jnp.zeros((LEVELS, 128), F32)
    outs = []
    for h in range(4):
        act = sact_s[h]
        gates = act[:, 0:HEAD].astype(F32)
        values = act[:, HEAD : 2 * HEAD]
        queries = act[:, 2 * HEAD : 3 * HEAD]
        keys = act[:, 3 * HEAD : 4 * HEAD]
        normed = snorm_s[h]
        cot = c_home[:, h * HEAD : (h + 1) * HEAD]
        outs.append((normed * gates).astype(BF))
        mixed_grad = ((cot * gates - mean_q - normed * mean_qn) * scale).astype(BF)
        score = dot_nt(mixed_grad, values) * sslope_s[h]
        rows = [
            jnp.sum(jnp.where(bucket == b, score, 0.0), axis=0, keepdims=True)
            for b in range(LEVELS)
        ]
        per_level = jnp.sum(jnp.concatenate(rows, axis=0), axis=1, keepdims=True)
        sums = sums + jnp.where(level_lane == h, per_level, 0.0)
        half = score.astype(BF)
        grads = [
            cot * normed,
            dot_tn(sweight_s[h], mixed_grad),
            dot_nn(half, keys) * SCALE,
            dot_tn(half, queries) * SCALE,
        ]
        for k in range(4):
            lanes = slice(k * HEAD, (k + 1) * HEAD)
            sgrad_s[h, :, lanes] = (grads[k] * silu_grad(sp_s[h, :, lanes])).astype(BF)
    sbias_s[...] = sums
    shape = (n_dp * SLEN, SHORT)
    same = (iota(shape, 0) & 15) == (iota(shape, 1) & 15)
    sender = jnp.where(
        same & (owner_row == (iota(shape, 0) >> 4).astype(F32)), 1.0, 0.0
    ).astype(BF)
    obuf[...] = dot_nn(sender, jnp.concatenate(outs, axis=1)).astype(BF).reshape(obuf.shape)
    for d in (1, 3, 2):
        sg_copy(d).start()
    grad_all[pl.ds(pl.multiple_of(LONG_ROWS + chip * SHORT, SHORT), SHORT), :] = sgrad_s[chip]
    dp_start(obuf, orecv, o_s, o_r)
    orecv[dp] = obuf[dp]

    def sib_copy(qs):
        return remote(
            sib_send.at[qs], sib_recv.at[qs], sib_s.at[qs], sib_r.at[qs], dp, sib
        )

    def g_copy(k, qs):
        return remote(
            grad_all.at[rows_at(qs, ROWS), k * HEAD : (k + 1) * HEAD],
            grad_h.at[chip, :, k * HEAD : (k + 1) * HEAD],
            g_s.at[k, qs],
            g_r.at[k, chip],
            dp,
            2 * qs + core,
        )

    def l_copy(qs):
        return remote(
            out_s.at[qs], long_out.at[:, lanes_at(chip)], l_s.at[qs], l_r.at[chip], dp, 2 * qs + core
        )

    def backward(step, carry):
        qs = CHIPS - 1 - step
        block = 2 * qs + core
        mine = rows_at(qs, ROWS)
        for d in (1, 3, 2):
            here = stat_s.at[qs, lax.rem(chip + CHIPS - d, CHIPS)]
            remote(here, here, stat_ss.at[qs, d], stat_sr.at[qs, d], dp, sib).wait_recv()
        stats = [stat_s[qs, h] for h in range(4)]
        mean = sum(s[0:1, :] for s in stats) * (1.0 / BLOCK)
        gaps = [s[0:1, :] * (1.0 / HEAD) - mean for s in stats]
        spread = sum(s[1:2, :] + HEAD * g * g for s, g in zip(stats, gaps)) * (1.0 / BLOCK)
        scale = lax.rsqrt(spread + epsilon)
        mean_q = sum(s[2:3, :] for s in stats) * (1.0 / BLOCK)
        mean_qn = sum(s[3:4, :] + g * s[2:3, :] for s, g in zip(stats, gaps))
        mean_qn = mean_qn * scale * (1.0 / BLOCK)
        whole = jnp.concatenate(
            [mean, scale, mean_q, mean_qn, jnp.zeros((124, ROWS), F32)], axis=0
        )
        cols = jnp.transpose(whole)
        mean, scale = cols[:, 0:1], cols[:, 1:2]
        mean_q, mean_qn = cols[:, 2:3], cols[:, 3:4]
        normed = (mixed_s[qs] - mean) * scale
        gates = act_s[qs, :, 0:HEAD].astype(F32)
        cotangent = c_g[qs].astype(F32)
        out_s[qs] = (normed * gates).astype(BF)
        mixed_grad = ((cotangent * gates - mean_q - normed * mean_qn) * scale).astype(BF)
        grad_all[mine, 0:HEAD] = (cotangent * normed * silu_grad(p_s[qs, :, 0:HEAD])).astype(BF)

        @pl.when(qs != chip)
        def _():
            l_copy(qs).start()
            g_copy(0, qs).start()

        queries = act_s[qs, :, 2 * HEAD : 3 * HEAD]
        tq = tcol_s[block][:, 0:1]
        dq_s[...] = jnp.zeros_like(dq_s)
        hist_s[...] = jnp.zeros_like(hist_s)

        def tile(p, carry):
            span = rows_at(p, PAIR)
            keys = kv[span, 0:HEAD]
            values = kv[span, HEAD : 2 * HEAD]
            score = dot_nt(mixed_grad, values) * slope_s[qs, p]
            near = jnp.where(tq - key_times(p) < LEVELS - 1.0, score, 0.0).astype(BF)
            half = score.astype(BF)
            tot_s[...] += jnp.sum(score.reshape(ROWS // 8, 8, PAIR), axis=0)
            hist_s[...] += dot_nn(near, hot_s[span, :])
            dq_s[...] += dot_nn(half, keys)
            dk_s[span, :] += dot_tn(half, queries)
            dv_s[span, :] += dot_tn(weight_s[qs, p], mixed_grad)
            return carry

        lax.fori_loop(0, qs + 1, tile, 0)
        htot_s[...] += lax.dot_general(
            hot_s[rows_at(block, ROWS), :].astype(F32),
            hist_s[...],
            (((0,), (0,)), ((), ())),
            precision=lax.Precision.HIGHEST,
            preferred_element_type=F32,
        )
        grad_all[mine, 2 * HEAD : 3 * HEAD] = (
            dq_s[...] * SCALE * silu_grad(p_s[qs, :, 2 * HEAD : 3 * HEAD])
        ).astype(BF)
        other = rows_at(2 * qs + 1 - core, ROWS)
        sib_send[qs, :, 0:HEAD] = dk_s[other, :].astype(BF)
        sib_send[qs, :, HEAD : 2 * HEAD] = dv_s[other, :].astype(BF)
        sib_copy(qs).start()

        @pl.when(qs != chip)
        def _():
            g_copy(2, qs).start()

        return carry

    lax.fori_loop(0, CHIPS, backward, 0)

    def finish(step, carry):
        qs = CHIPS - 1 - step
        sib_copy(qs).wait_recv()
        mine = rows_at(qs, ROWS)
        block = rows_at(2 * qs + core, ROWS)
        dk = (dk_s[block, :] + sib_recv[qs, :, 0:HEAD].astype(F32)) * SCALE
        dv = dv_s[block, :] + sib_recv[qs, :, HEAD : 2 * HEAD].astype(F32)
        grad_all[mine, HEAD : 2 * HEAD] = (
            dv * silu_grad(p_s[qs, :, HEAD : 2 * HEAD])
        ).astype(BF)
        grad_all[mine, 3 * HEAD : 4 * HEAD] = (
            dk * silu_grad(p_s[qs, :, 3 * HEAD : 4 * HEAD])
        ).astype(BF)

        @pl.when(qs != chip)
        def _():
            g_copy(1, qs).start()
            g_copy(3, qs).start()

        return carry

    lax.fori_loop(0, CHIPS, finish, 0)

    for d in (1, 3, 2):
        src = lax.rem(chip + CHIPS - d, CHIPS)
        there = pl.ds(pl.multiple_of(LONG_ROWS + src * SHORT, SHORT), SHORT)
        remote(stok, tok_all.at[there, :], st_s.at[d], st_r.at[d], dp, sib).wait_recv()
        remote(sgrad_s.at[src], grad_all.at[there, :], sg_s.at[d], sg_r.at[d], dp, sib).wait_recv()

    def outer(pair):
        cols = pl.ds(pl.multiple_of(pair * 2 * HEAD, 2 * HEAD), 2 * HEAD)
        return dot_tn(tok_all[...], grad_all[:, cols])

    half_send[...] = outer(1 - core).astype(BF)
    swap = remote(half_send, half_recv, p_ss, p_sr, dp, sib)
    swap.start()
    own[...] = outer(core)
    swap.wait_recv()
    rs_send[...] = (own[...] + half_recv[...].astype(F32)).astype(BF).reshape(rs_send.shape)
    dp_start(rs_send, rs_recv, rs_s, rs_r)
    rs_recv[dp] = rs_send[dp]

    shape = (128, 128)
    gap = (iota(shape, 0) - iota(shape, 1)) & 15
    hist = htot_s[...]
    rows = [
        jnp.sum(jnp.where(gap == b, hist, 0.0), axis=0, keepdims=True) for b in range(LEVELS - 1)
    ]
    total = jnp.sum(tot_s[...], axis=0, keepdims=True)
    total = sum(total[:, i : i + 128] for i in range(0, PAIR, 128))
    rows.append(total - sum(rows))
    levels = jnp.sum(jnp.concatenate(rows, axis=0), axis=1, keepdims=True)
    levels = sbias_s[...] + jnp.where(level_lane == chip, levels, 0.0)
    levels = jnp.concatenate([levels, jnp.zeros((128 - LEVELS, 128), F32)], axis=0)
    b_send[...] = jnp.transpose(levels)[0:8, :]
    one_start(b_send, b_dp, b1_s, b1_r)
    b_dp[dp] = b_send[...]

    dp_all(obuf, orecv, o_s, o_r).wait_recv()
    short_out[...] = dot_tn(place_s[...], orecv[...].reshape(n_dp * SLEN, BLOCK)).astype(BF)
    total = dot_nt(sgrad_s[0], wh[0])
    for h in range(1, 4):
        total = total + dot_nt(sgrad_s[h], wh[h])
    short_grad[...] = total.astype(BF)

    one_all(b_dp, b1_s, b1_r).wait_recv()
    b_mid[...] = jnp.sum(b_dp[...], axis=0)

    def b2_copy(o):
        return remote(
            b_mid, b_ctx.at[ctx], b2_s.at[o], b2_r.at[o], dp, lax.rem(ctx + o, 2 * CHIPS)
        )

    def start_b2(o, carry):
        b2_copy(o).start()
        return carry

    lax.fori_loop(1, 2 * CHIPS, start_b2, 0)
    b_ctx[ctx] = b_mid[...]

    long_out[:, lanes_at(chip)] = out_s[chip]
    grad_h[chip] = grad_all[rows_at(chip, ROWS), :]
    total = dot_nt(grad_h[chip], wh[chip])
    for d in (1, 3, 2):
        src = lax.rem(chip + CHIPS - d, CHIPS)
        for k in range(4):
            here = grad_h.at[src, :, k * HEAD : (k + 1) * HEAD]
            remote(here, here, g_s.at[k, src], g_r.at[k, src], dp, sib).wait_recv()
        here = long_out.at[:, lanes_at(src)]
        remote(out_s.at[src], here, l_s.at[src], l_r.at[src], dp, sib).wait_recv()
        total = total + dot_nt(grad_h[src], wh[src])
    token_grad[...] = total.astype(BF)

    def wait_b2(o, carry):
        src = lax.rem(ctx + 2 * CHIPS - o, 2 * CHIPS)
        remote(b_mid, b_ctx.at[src], b2_s.at[o], b2_r.at[o], dp, src).wait_recv()
        return carry

    lax.fori_loop(1, 2 * CHIPS, wait_b2, 0)
    bias_out[...] = jnp.sum(b_ctx[...], axis=0)[0:4, 0:LEVELS]

    half_copy(up, 0, 0).wait_send()
    half_copy(up, 1, 0).wait_send()
    half_copy(down, 0, 1).wait_send()
    half_copy(down, 1, 1).wait_send()
    pass_copy(down, 0, up).wait_send()
    pass_copy(up, 1, down).wait_send()
    for d in (1, 3, 2):
        c_copy(d).wait_send()
        st_copy(d).wait_send()
        sg_copy(d).wait_send()
    one_all(dest_g, d_s, d_r).wait_send()
    dp_all(cbuf, crecv, s_s, s_r).wait_send()
    dp_all(obuf, orecv, o_s, o_r).wait_send()
    one_all(b_dp, b1_s, b1_r).wait_send()

    def ended_o(o, carry):
        t_copy(o).wait_send()
        b2_copy(o).wait_send()
        return carry

    lax.fori_loop(1, 2 * CHIPS, ended_o, 0)

    def ended_q(qs, carry):
        kv_copy(qs).wait_send()
        sib_copy(qs).wait_send()
        for d in (1, 3, 2):
            stat_copy(qs, d).wait_send()

        @pl.when(qs != chip)
        def _():
            l_copy(qs).wait_send()
            for k in range(4):
                g_copy(k, qs).wait_send()

        return carry

    lax.fori_loop(0, CHIPS, ended_q, 0)
    swap.wait_send()

    dp_all(rs_send, rs_recv, rs_s, rs_r).wait_recv()
    piece[...] = jnp.sum(rs_recv[...].astype(F32), axis=0)
    mine = lax.rem(chip, 2)

    def f_copy(i):
        target = 2 * (2 * core + i) + lax.div(chip, 2)
        return target, remote(
            piece.at[:, i * HEAD : (i + 1) * HEAD],
            proj_grad.at[:, lanes_at(mine)],
            f_s.at[i],
            f_r.at[mine],
            dp,
            target,
        )

    for i in range(2):
        target, copy = f_copy(i)

        @pl.when(target != ctx)
        def _():
            copy.start()

        @pl.when(target == ctx)
        def _():
            proj_grad[:, lanes_at(mine)] = piece[:, i * HEAD : (i + 1) * HEAD]

    for half in range(2):
        source = 2 * (2 * core + half) + lax.div(chip, 2)

        @pl.when(source != ctx)
        def _():
            remote(
                piece.at[:, 0:HEAD],
                proj_grad.at[:, half * HEAD : (half + 1) * HEAD],
                f_s.at[half],
                f_r.at[half],
                dp,
                source,
            ).wait_recv()

    for i in range(2):
        target, copy = f_copy(i)

        @pl.when(target != ctx)
        def _():
            copy.wait_send()

    dp_all(rs_send, rs_recv, rs_s, rs_r).wait_send()


def output_kernel(count, *refs):
    for i in range(count):
        refs[count + i][...] = refs[i][...]


VM = pl.BlockSpec(memory_space=pltpu.VMEM)
SM = pl.BlockSpec(memory_space=pltpu.SMEM)
ANY = pl.BlockSpec(memory_space=pl.ANY)
DMA = pltpu.SemaphoreType.DMA
VMEM = pltpu.VMEM


def shaped(shape, dtype):
    return jax.ShapeDtypeStruct(shape, dtype)


def per_device(
    n_dp,
    long_tokens,
    short_tokens,
    projection,
    time_bias,
    long_length,
    short_length,
    long_time,
    short_time,
    destination,
    long_cotangent,
    short_cotangent,
):
    part = MODEL // n_dp
    spread = (n_dp, SLEN, BLOCK)
    scratch = [
        VMEM((CHIPS, MODEL, BLOCK), BF),
        VMEM((ALL_ROWS, MODEL), BF),
        VMEM((ALL_ROWS, BLOCK), BF),
        VMEM((CHIPS, ROWS, BLOCK), F32),
        VMEM((CHIPS, ROWS, BLOCK), BF),
        VMEM((2 * CHIPS * ROWS, 2 * HEAD), BF),
        VMEM((CHIPS, ROWS, HEAD), BF),
        VMEM((8, ROWS), jnp.int32),
        VMEM((2 * CHIPS, 8, ROWS), jnp.int32),
        VMEM((8, 128), F32),
        VMEM((8, 128), jnp.int32),
        VMEM((8, 128), jnp.int32),
        VMEM((n_dp, 8, 128), jnp.int32),
        VMEM((n_dp * SLEN, 128), BF),
        VMEM(spread, BF),
        VMEM(spread, BF),
        VMEM((4, SHORT, BLOCK), F32),
        VMEM((4, SHORT, BLOCK), BF),
        VMEM((4, SHORT, SHORT), BF),
        VMEM((4, SHORT, SHORT), F32),
        VMEM((4, SHORT, HEAD), F32),
        VMEM((SHORT, 128), F32),
        VMEM((SHORT, BLOCK), F32),
        VMEM((4, SHORT, BLOCK), BF),
        VMEM(spread, BF),
        VMEM(spread, BF),
        VMEM((LEVELS, 128), F32),
        VMEM((CHIPS, CHIPS, ROWS, PAIR), BF),
        VMEM((CHIPS, CHIPS, ROWS, PAIR), F32),
        VMEM((CHIPS, ROWS, HEAD), F32),
        VMEM((CHIPS, ROWS, HEAD), BF),
        VMEM((2 * CHIPS * ROWS, 128), BF),
        VMEM((2 * CHIPS, ROWS, 128), F32),
        VMEM((CHIPS, CHIPS, 8, ROWS), F32),
        VMEM((2 * CHIPS * ROWS, HEAD), F32),
        VMEM((2 * CHIPS * ROWS, HEAD), F32),
        VMEM((ROWS, HEAD), F32),
        VMEM((ROWS, 128), F32),
        VMEM((128, 128), F32),
        VMEM((8, PAIR), F32),
        VMEM((CHIPS, ROWS, 2 * HEAD), BF),
        VMEM((CHIPS, ROWS, 2 * HEAD), BF),
        VMEM((CHIPS, ROWS, BLOCK), BF),
        VMEM((MODEL, 2 * HEAD), BF),
        VMEM((MODEL, 2 * HEAD), BF),
        VMEM((MODEL, 2 * HEAD), F32),
        VMEM((n_dp, part, 2 * HEAD), BF),
        VMEM((n_dp, part, 2 * HEAD), BF),
        VMEM((8, 128), F32),
        VMEM((n_dp, 8, 128), F32),
        VMEM((8, 128), F32),
        VMEM((2 * CHIPS, 8, 128), F32),
        VMEM((part, 2 * HEAD), F32),
        DMA((4, 4)),
        DMA((2, 2)),
        DMA((2, 2)),
        DMA((2,)),
        DMA((2,)),
        DMA((CHIPS,)),
        DMA((CHIPS,)),
        DMA((2 * CHIPS,)),
        DMA((2 * CHIPS,)),
        DMA((CHIPS,)),
        DMA((CHIPS,)),
        DMA((CHIPS,)),
        DMA((CHIPS,)),
        DMA((CHIPS,)),
        DMA((CHIPS,)),
        DMA,
        DMA,
        DMA,
        DMA,
        DMA,
        DMA,
        DMA((CHIPS, CHIPS)),
        DMA((CHIPS, CHIPS)),
        DMA((CHIPS,)),
        DMA((CHIPS,)),
        DMA((4, CHIPS)),
        DMA((4, CHIPS)),
        DMA((CHIPS,)),
        DMA((CHIPS,)),
        DMA,
        DMA,
        DMA,
        DMA,
        DMA,
        DMA,
        DMA((2 * CHIPS,)),
        DMA((2 * CHIPS,)),
        DMA((2,)),
        DMA((2,)),
    ]
    results = pl.pallas_call(
        functools.partial(layer_kernel, n_dp),
        out_shape=(
            shaped((ROWS, BLOCK), BF),
            shaped((SHORT, BLOCK), BF),
            shaped((ROWS, MODEL), BF),
            shaped((SHORT, MODEL), BF),
            shaped((part, 2 * HEAD), F32),
            shaped(time_bias.shape, F32),
        ),
        in_specs=[VM, VM, ANY, VM, VM, VM, VM, VM, VM, SM, VM],
        out_specs=(VM,) * 6,
        scratch_shapes=scratch,
        compiler_params=pltpu.CompilerParams(
            vmem_limit_bytes=VMEM_LIMIT, collective_id=0, has_side_effects=True
        ),
        name="layer",
    )(
        long_tokens[0],
        short_tokens.reshape(SHORT, MODEL),
        projection,
        long_cotangent[0],
        short_cotangent.reshape(SHORT, BLOCK),
        long_time,
        short_time,
        short_length,
        destination,
        long_length,
        time_bias,
    )
    results = pl.pallas_call(
        functools.partial(output_kernel, len(results)),
        out_shape=tuple(shaped(r.shape, r.dtype) for r in results),
        in_specs=[VM] * len(results),
        out_specs=(VM,) * len(results),
        compiler_params=pltpu.CompilerParams(vmem_limit_bytes=VMEM_LIMIT),
        name="output",
    )(*results)
    long_out, short_out, token_grad, short_grad, proj_grad, bias_out = results
    return (
        long_out[None],
        short_out.reshape(short_cotangent.shape),
        token_grad[None],
        short_grad.reshape(short_tokens.shape),
        proj_grad,
        bias_out,
    )


def solution(mesh):
    return jax.shard_map(
        functools.partial(per_device, mesh.shape["dp"]),
        mesh=mesh,
        in_specs=(
            P("dp", "ctx", None),
            P("dp", "ctx", None, None),
            P(),
            P(),
            P("dp"),
            P("dp", "ctx"),
            P("dp", "ctx"),
            P("dp", "ctx", None),
            P("dp", "ctx"),
            P("dp", "ctx", None),
            P("dp", "ctx", None, None),
        ),
        out_specs=(
            P("dp", "ctx", None),
            P("dp", "ctx", None, None),
            P("dp", "ctx", None),
            P("dp", "ctx", None, None),
            P("dp", "ctx"),
            P(),
        ),
        check_vma=False,
    )
```

```python
import functools

import jax
import jax.numpy as jnp
from jax import lax
from jax.experimental import pallas as pl
from jax.experimental.pallas import tpu as pltpu
from jax.sharding import PartitionSpec as P

epsilon = 1e-05
MESH = pl.DeviceIdType.MESH
BF = jnp.bfloat16
F32 = jnp.float32
CHIPS = 4
ROWS = 256
HEAD = 128
LEVELS = 16
SLEN = 16
SHORT = 128
LONG_ROWS = CHIPS * ROWS
ALL_ROWS = CHIPS * (ROWS + SHORT)
PAIR = 2 * ROWS
MODEL = 1024
BLOCK = 512
SCALE = HEAD ** (-0.5)
VMEM_LIMIT = 56 * 1024 * 1024


def sigmoid(value):
    return 0.5 * jnp.tanh(0.5 * value) + 0.5


def silu_and_grad(value):
    sigma = sigmoid(value)
    silu = value * sigma
    return silu.astype(BF), sigma + silu * (1.0 - sigma)


def dot_nn(a, b):
    return jnp.dot(a, b, preferred_element_type=F32)


def dot_nt(a, b):
    return lax.dot_general(a, b, (((1,), (1,)), ((), ())), preferred_element_type=F32)


def dot_tn(a, b):
    return lax.dot_general(a, b, (((0,), (0,)), ((), ())), preferred_element_type=F32)


def column_of(row):
    return jnp.transpose(jnp.broadcast_to(row, (128, 128)))


def iota(shape, axis):
    return lax.broadcasted_iota(jnp.int32, shape, axis)


def remote(src, dst, send_sem, recv_sem, dp, ctx):
    return pltpu.make_async_remote_copy(
        src_ref=src,
        dst_ref=dst,
        send_sem=send_sem,
        recv_sem=recv_sem,
        device_id=(dp, ctx),
        device_id_type=MESH,
    )


def place():
    dp = lax.axis_index("dp")
    ctx = lax.axis_index("ctx")
    return dp, ctx, lax.div(ctx, 2), lax.rem(ctx, 2)


def lookup(table, diff):
    index = jnp.clip(diff, 0.0, LEVELS - 1.0).astype(jnp.int32)
    parts = [
        jnp.take_along_axis(table, index[:, i : i + 128], axis=1)
        for i in range(0, index.shape[1], 128)
    ]
    return parts[0] if len(parts) == 1 else jnp.concatenate(parts, axis=1)


def exact_dot(a, b):
    return lax.dot_general(
        a,
        b,
        (((1,), (0,)), ((), ())),
        precision=lax.Precision.HIGHEST,
        preferred_element_type=F32,
    )


def rows_at(block, rows):
    return pl.ds(pl.multiple_of(block * rows, rows), rows)


def lanes_at(block):
    return pl.ds(pl.multiple_of(block * HEAD, HEAD), HEAD)


def layer_kernel(
    n_dp,
    tok,
    stok,
    w,
    lcot,
    scot,
    ltime,
    stime,
    slen,
    dest_in,
    llen,
    tbias,
    long_out,
    short_out,
    token_grad,
    short_grad,
    proj_grad,
    bias_out,
    wh,
    tok_all,
    grad_all,
    p_s,
    act_s,
    kv,
    c_g,
    tmeta,
    times,
    tab_s,
    ints,
    dtile,
    dest_g,
    place_s,
    cbuf,
    crecv,
    sp_s,
    sact_s,
    sweight_s,
    sslope_s,
    snorm_s,
    sscale_s,
    c_home,
    sgrad_s,
    obuf,
    orecv,
    sbias_s,
    weight_s,
    slope_s,
    mixed_s,
    out_s,
    hot_s,
    tcol_s,
    stat_s,
    dk_s,
    dv_s,
    dq_s,
    hist_s,
    htot_s,
    tot_s,
    sib_send,
    sib_recv,
    grad_h,
    half_send,
    half_recv,
    own,
    rs_send,
    rs_recv,
    b_send,
    b_dp,
    b_mid,
    b_ctx,
    piece,
    lo_v,
    so_v,
    tg_v,
    sg_v,
    w_sem,
    in_sem,
    out_sem,
    tok_s,
    tok_r,
    fwd_s,
    fwd_r,
    c_s,
    c_r,
    t_s,
    t_r,
    kv_s,
    kv_r,
    st_s,
    st_r,
    sg_s,
    sg_r,
    d_s,
    d_r,
    s_s,
    s_r,
    o_s,
    o_r,
    stat_ss,
    stat_sr,
    sib_s,
    sib_r,
    g_s,
    g_r,
    l_s,
    l_r,
    p_ss,
    p_sr,
    rs_s,
    rs_r,
    b1_s,
    b1_r,
    b2_s,
    b2_r,
    f_s,
    f_r,
):
    dp, ctx, chip, core = place()
    sib = ctx + 1 - 2 * core
    up = lax.rem(chip + 1, CHIPS)
    down = lax.rem(chip + CHIPS - 1, CHIPS)
    far = lax.rem(chip + 2, CHIPS)
    half_rows = ROWS // 2
    barrier = pltpu.get_barrier_semaphore()

    def greet_ctx(o, carry):
        pl.semaphore_signal(
            barrier, inc=1, device_id=(dp, lax.rem(ctx + o, 2 * CHIPS)), device_id_type=MESH
        )
        return carry

    def greet_dp(o, carry):
        pl.semaphore_signal(
            barrier, inc=1, device_id=(lax.rem(dp + o, n_dp), ctx), device_id_type=MESH
        )
        return carry

    lax.fori_loop(1, 2 * CHIPS, greet_ctx, 0)
    lax.fori_loop(1, n_dp, greet_dp, 0)

    def w_copy(h, k):
        return pltpu.make_async_copy(
            w.at[:, k * BLOCK + h * HEAD : k * BLOCK + (h + 1) * HEAD],
            wh.at[h, :, k * HEAD : (k + 1) * HEAD],
            w_sem.at[h, k],
        )

    for h in range(4):
        for k in range(4):
            w_copy(h, k).start()
    tmeta[...] = jnp.broadcast_to(ltime[...], (8, ROWS))
    ints[...] = jnp.zeros((8, 128), jnp.int32) - 1
    ints[0:1, 0:8] = slen[...]
    ints[1:2, 0:8] = dest_in[...]
    dtile[...] = jnp.broadcast_to(ints[1:2, :], (8, 128))
    tab_s[...] = jnp.zeros_like(tab_s)
    tab_s[0:4, 0:LEVELS] = tbias[...]

    def half_copy(peer, half, index):
        return remote(
            tok.at[half * half_rows : (half + 1) * half_rows, :],
            tok_all.at[rows_at(2 * chip + half, half_rows), :],
            tok_s.at[index, half],
            tok_r.at[index, half],
            dp,
            2 * peer + core,
        )

    def half_wait(src, half, index):
        here = tok_all.at[rows_at(2 * src + half, half_rows), :]
        remote(here, here, tok_s.at[index, half], tok_r.at[index, half], dp, sib).wait_recv()

    def pass_copy(src, half, peer):
        here = tok_all.at[rows_at(2 * src + half, half_rows), :]
        return remote(here, here, fwd_s.at[half], fwd_r.at[half], dp, 2 * peer + core)

    def c_copy(d):
        peer = lax.rem(chip + d, CHIPS)
        return remote(
            lcot.at[:, lanes_at(peer)], c_g.at[chip], c_s.at[d], c_r.at[d], dp, 2 * peer + core
        )

    def t_copy(o):
        return remote(
            tmeta, times.at[ctx], t_s.at[o], t_r.at[o], dp, lax.rem(ctx + o, 2 * CHIPS)
        )

    def kv_copy(src):
        here = kv.at[rows_at(2 * src + core, ROWS), :]
        return remote(here, here, kv_s.at[src], kv_r.at[src], dp, sib)

    def kv_wait(src):
        here = kv.at[rows_at(2 * src + 1 - core, ROWS), :]
        remote(here, here, kv_s.at[src], kv_r.at[src], dp, sib).wait_recv()

    def st_copy(d):
        return remote(
            stok,
            tok_all.at[pl.ds(pl.multiple_of(LONG_ROWS + chip * SHORT, SHORT), SHORT), :],
            st_s.at[d],
            st_r.at[d],
            dp,
            2 * lax.rem(chip + d, CHIPS) + core,
        )

    def sg_copy(d):
        peer = lax.rem(chip + d, CHIPS)
        return remote(
            sgrad_s.at[peer],
            grad_all.at[pl.ds(pl.multiple_of(LONG_ROWS + chip * SHORT, SHORT), SHORT), :],
            sg_s.at[d],
            sg_r.at[d],
            dp,
            2 * peer + core,
        )

    def dp_start(source, target, send, recv):
        def one(o, carry):
            peer = lax.rem(dp + o, n_dp)
            remote(source.at[peer], target.at[dp], send, recv, peer, ctx).start()
            return carry

        lax.fori_loop(1, n_dp, one, 0)

    def dp_all(source, target, send, recv):
        return remote(
            source.at[0 : n_dp - 1], target.at[0 : n_dp - 1], send, recv, dp, sib
        )

    def one_start(source, target, send, recv):
        def one(o, carry):
            remote(source, target.at[dp], send, recv, lax.rem(dp + o, n_dp), ctx).start()
            return carry

        lax.fori_loop(1, n_dp, one, 0)

    def one_all(target, send, recv):
        here = target.at[0 : n_dp - 1]
        return remote(here, here, send, recv, dp, sib)

    home_rows = pl.ds(pl.multiple_of(LONG_ROWS + chip * SHORT, SHORT), SHORT)
    loads = [
        pltpu.make_async_copy(tok, tok_all.at[rows_at(chip, ROWS), :], in_sem.at[0]),
        pltpu.make_async_copy(stok, tok_all.at[home_rows, :], in_sem.at[1]),
        pltpu.make_async_copy(lcot.at[:, lanes_at(chip)], c_g.at[chip], in_sem.at[2]),
    ]
    for load in loads:
        load.start()
    pl.semaphore_wait(barrier, n_dp - 1 + 2 * CHIPS - 1)
    half_copy(up, 0, 0).start()
    half_copy(down, 1, 1).start()
    half_copy(up, 1, 0).start()
    half_copy(down, 0, 1).start()
    one_start(dtile, dest_g, d_s, d_r)

    def start_t(o, carry):
        t_copy(o).start()
        return carry

    lax.fori_loop(1, 2 * CHIPS, start_t, 0)
    times[ctx] = tmeta[...]
    dest_g[dp] = dtile[...]
    for h in range(4):
        for k in range(4):
            w_copy(h, k).wait()
    for load in loads:
        load.wait()

    def project(src):
        projected = dot_nn(tok_all[rows_at(src, ROWS), :], wh[chip])
        act, p_s[src] = silu_and_grad(projected)
        act_s[src] = act
        kv[rows_at(2 * src + core, ROWS), 0:HEAD] = act[:, 3 * HEAD : 4 * HEAD]
        kv[rows_at(2 * src + core, ROWS), HEAD : 2 * HEAD] = act[:, HEAD : 2 * HEAD]
        kv_copy(src).start()

    project(chip)

    lane16 = iota((16, 128), 1)
    spread_time = exact_dot(
        stime[0].astype(F32), jnp.where((lane16 & 15) == iota((16, 128), 0), 1.0, 0.0)
    )
    pick = (iota((8, 128), 1) >> 4) == iota((8, 128), 0)
    stime_row = jnp.sum(jnp.where(pick, spread_time, 0.0), axis=0, keepdims=True)
    repeat = jnp.where((iota((128, 128), 1) >> 4) == iota((128, 128), 0), 1.0, 0.0)
    rep_rows = exact_dot(ints[...].astype(F32), repeat)
    slen_row, home_row = rep_rows[0:1, :], rep_rows[1:2, :]
    owner_row = (home_row.astype(jnp.int32) >> 3).astype(F32)
    shape = (SHORT, SHORT)
    row = iota(shape, 0)
    col = iota(shape, 1)
    stime_diff = column_of(stime_row) - stime_row
    inside = (row & 15).astype(F32) < column_of(slen_row)
    svisible = ((row >> 4) == (col >> 4)) & (col <= row) & inside

    short_tokens = tok_all[home_rows, :]
    mixes = []
    for h in range(4):
        act, sp_s[h] = silu_and_grad(dot_nn(short_tokens, wh[h]))
        sact_s[h] = act
        queries, keys = act[:, 2 * HEAD : 3 * HEAD], act[:, 3 * HEAD : 4 * HEAD]
        tab = jnp.broadcast_to(tab_s[h : h + 1, :], (SHORT, 128))
        total = dot_nt(queries, keys) * SCALE + lookup(tab, stime_diff)
        sg = sigmoid(total)
        weight = total * sg
        weight16 = jnp.where(svisible, weight, 0.0).astype(BF)
        sweight_s[h] = weight16
        sslope_s[h] = jnp.where(svisible, sg + weight * (1.0 - sg), 0.0)
        mixes.append(dot_nn(weight16, act[:, HEAD : 2 * HEAD]))
    mean = sum(jnp.sum(m, axis=1, keepdims=True) for m in mixes) * (1.0 / BLOCK)
    centred = [m - mean for m in mixes]
    spread = sum(jnp.sum(m * m, axis=1, keepdims=True) for m in centred) * (1.0 / BLOCK)
    scale = lax.rsqrt(spread + epsilon)
    sscale_s[...] = jnp.broadcast_to(scale, sscale_s.shape)
    for h in range(4):
        snorm_s[h] = centred[h] * scale

    one_all(dest_g, d_s, d_r).wait_recv()
    dest = dest_g[...]
    code = jnp.sum(
        jnp.where((dest >> 3) == dp, ((dest & 7) + 1).astype(F32), 0.0), axis=2, keepdims=True
    )
    code = jnp.broadcast_to(code, (n_dp, 8, 128))
    code = jnp.concatenate([code, code], axis=1).reshape(n_dp * SLEN, 128)
    shape = (n_dp * SLEN, 128)
    same = (iota(shape, 0) & 15) == (iota(shape, 1) & 15)
    slot = ((iota(shape, 1) >> 4) + 1).astype(F32)
    placer = jnp.where(same & (code == slot), 1.0, 0.0).astype(BF)
    place_s[...] = placer
    cbuf[...] = dot_nn(placer, scot[...]).astype(BF).reshape(cbuf.shape)
    dp_start(cbuf, crecv, s_s, s_r)
    crecv[dp] = cbuf[dp]

    half_wait(down, 0, 0)
    pass_copy(down, 0, up).start()
    half_wait(up, 1, 1)
    pass_copy(up, 1, down).start()
    for d in (1, 3, 2):
        c_copy(d).start()

    def wait_t(o, carry):
        src = lax.rem(ctx + 2 * CHIPS - o, 2 * CHIPS)
        remote(tmeta, times.at[src], t_s.at[o], t_r.at[o], dp, src).wait_recv()
        return carry

    lax.fori_loop(1, 2 * CHIPS, wait_t, 0)
    lane = iota((ROWS, 128), 1)

    def times_of(b, carry):
        line = times[b, 0:1, :].astype(F32)
        column = jnp.concatenate(
            [column_of(line[:, 0:128]), column_of(line[:, 128:256])], axis=0
        )
        tcol_s[b] = column
        hot_s[rows_at(b, ROWS), :] = jnp.where(
            (column.astype(jnp.int32) & 15) == lane, 1.0, 0.0
        ).astype(BF)
        return carry

    lax.fori_loop(0, 2 * CHIPS, times_of, 0)
    dk_s[...] = jnp.zeros_like(dk_s)
    dv_s[...] = jnp.zeros_like(dv_s)
    htot_s[...] = jnp.zeros_like(htot_s)
    tot_s[...] = jnp.zeros_like(tot_s)
    mixed_s[...] = jnp.zeros_like(mixed_s)

    half_wait(down, 1, 0)
    project(down)
    half_wait(up, 0, 1)
    project(up)

    table = jnp.broadcast_to(tab_s[pl.ds(chip, 1), :], (ROWS, 128))
    length = llen[0]

    def key_times(p):
        return jnp.concatenate(
            [times[2 * p, 0:1, :], times[2 * p + 1, 0:1, :]], axis=1
        ).astype(F32)

    def forward_tile(qs, p):
        block = 2 * qs + core
        queries = act_s[qs, :, 2 * HEAD : 3 * HEAD]
        tq = tcol_s[block][:, 0:1]
        spot = iota((ROWS, 1), 0) + block * ROWS
        limit = jnp.where(spot < length, spot, -1)
        keys = kv[rows_at(p, PAIR), 0:HEAD]
        values = kv[rows_at(p, PAIR), HEAD : 2 * HEAD]
        total = dot_nt(queries, keys) * SCALE + lookup(table, tq - key_times(p))
        sg = sigmoid(total)
        weight = total * sg
        visible = (iota((ROWS, PAIR), 1) + p * PAIR) <= limit
        weight16 = jnp.where(visible, weight, 0.0).astype(BF)
        weight_s[qs, p] = weight16
        slope_s[qs, p] = jnp.where(visible, sg + weight * (1.0 - sg), 0.0)
        mixed_s[qs] += dot_nn(weight16, values)

    for d in (0, 1, 3):
        kv_wait(lax.rem(chip + CHIPS - d, CHIPS))

    def near_block(step, carry):
        qs = CHIPS - 1 - step

        def one(p, carry):
            @pl.when(p != far)
            def _():
                forward_tile(qs, p)

            return carry

        lax.fori_loop(0, jnp.where(qs == far, 0, qs + 1), one, 0)
        return carry

    lax.fori_loop(0, CHIPS, near_block, 0)

    for half in range(2):
        here = tok_all.at[rows_at(2 * far + half, half_rows), :]
        remote(here, here, fwd_s.at[half], fwd_r.at[half], dp, sib).wait_recv()
    project(far)
    for d in (1, 3, 2):
        st_copy(d).start()
    for d in (1, 3, 2):
        src = lax.rem(chip + CHIPS - d, CHIPS)
        remote(c_g.at[src], c_g.at[src], c_s.at[d], c_r.at[d], dp, sib).wait_recv()
    kv_wait(far)

    def stat_copy(qs, d):
        here = stat_s.at[qs, chip]
        return remote(
            here,
            here,
            stat_ss.at[qs, d],
            stat_sr.at[qs, d],
            dp,
            2 * lax.rem(chip + d, CHIPS) + core,
        )

    def far_block(step, carry):
        qs = CHIPS - 1 - step

        def one(p, carry):
            forward_tile(qs, p)
            return carry

        first = jnp.where(qs == far, 0, far)
        last = jnp.where(qs >= far, jnp.where(qs == far, qs, far) + 1, first)
        lax.fori_loop(first, last, one, 0)
        mixed = mixed_s[qs]
        q = c_g[qs].astype(F32) * act_s[qs, :, 0:HEAD].astype(F32)
        s1 = jnp.sum(mixed, axis=1, keepdims=True)
        centred = mixed - s1 * (1.0 / HEAD)
        s2 = jnp.sum(centred * centred, axis=1, keepdims=True)
        s3 = jnp.sum(q, axis=1, keepdims=True)
        s4 = jnp.sum(q * centred, axis=1, keepdims=True)
        stats = jnp.where(
            lane == 0, s1, jnp.where(lane == 1, s2, jnp.where(lane == 2, s3, s4))
        )
        stat_s[qs, chip] = jnp.transpose(stats)[0:8, :]
        for d in (1, 3, 2):
            stat_copy(qs, d).start()
        return carry

    lax.fori_loop(0, CHIPS, far_block, 0)

    dp_all(cbuf, crecv, s_s, s_r).wait_recv()
    owner = jnp.concatenate([column_of(owner_row)] * (n_dp * SLEN // 128), axis=1)
    shape = (SHORT, n_dp * SLEN)
    same = (iota(shape, 0) & 15) == (iota(shape, 1) & 15)
    chooser = jnp.where(
        same & (owner == (iota(shape, 1) >> 4).astype(F32)), 1.0, 0.0
    ).astype(BF)
    c_home[...] = dot_nn(chooser, crecv[...].reshape(n_dp * SLEN, BLOCK))
    scale = sscale_s[:, 0:1]
    mean_q = jnp.zeros((SHORT, 1), F32)
    mean_qn = jnp.zeros((SHORT, 1), F32)
    for h in range(4):
        q = c_home[:, h * HEAD : (h + 1) * HEAD] * sact_s[h, :, 0:HEAD].astype(F32)
        mean_q = mean_q + jnp.sum(q, axis=1, keepdims=True)
        mean_qn = mean_qn + jnp.sum(q * snorm_s[h], axis=1, keepdims=True)
    mean_q = mean_q * (1.0 / BLOCK)
    mean_qn = mean_qn * (1.0 / BLOCK)
    bucket = jnp.clip(stime_diff, 0.0, LEVELS - 1.0).astype(jnp.int32)
    level_lane = iota((LEVELS, 128), 1)
    sums = jnp.zeros((LEVELS, 128), F32)
    outs = []
    for h in range(4):
        act = sact_s[h]
        gates = act[:, 0:HEAD].astype(F32)
        values = act[:, HEAD : 2 * HEAD]
        queries = act[:, 2 * HEAD : 3 * HEAD]
        keys = act[:, 3 * HEAD : 4 * HEAD]
        normed = snorm_s[h]
        cot = c_home[:, h * HEAD : (h + 1) * HEAD]
        outs.append((normed * gates).astype(BF))
        mixed_grad = ((cot * gates - mean_q - normed * mean_qn) * scale).astype(BF)
        score = dot_nt(mixed_grad, values) * sslope_s[h]
        rows = [
            jnp.sum(jnp.where(bucket == b, score, 0.0), axis=0, keepdims=True)
            for b in range(LEVELS)
        ]
        per_level = jnp.sum(jnp.concatenate(rows, axis=0), axis=1, keepdims=True)
        sums = sums + jnp.where(level_lane == h, per_level, 0.0)
        half = score.astype(BF)
        grads = [
            cot * normed,
            dot_tn(sweight_s[h], mixed_grad),
            dot_nn(half, keys) * SCALE,
            dot_tn(half, queries) * SCALE,
        ]
        for k in range(4):
            lanes = slice(k * HEAD, (k + 1) * HEAD)
            sgrad_s[h, :, lanes] = (grads[k] * sp_s[h, :, lanes]).astype(BF)
    sbias_s[...] = sums
    shape = (n_dp * SLEN, SHORT)
    same = (iota(shape, 0) & 15) == (iota(shape, 1) & 15)
    sender = jnp.where(
        same & (owner_row == (iota(shape, 0) >> 4).astype(F32)), 1.0, 0.0
    ).astype(BF)
    obuf[...] = dot_nn(sender, jnp.concatenate(outs, axis=1)).astype(BF).reshape(obuf.shape)
    for d in (1, 3, 2):
        sg_copy(d).start()
    grad_all[pl.ds(pl.multiple_of(LONG_ROWS + chip * SHORT, SHORT), SHORT), :] = sgrad_s[chip]
    dp_start(obuf, orecv, o_s, o_r)
    orecv[dp] = obuf[dp]

    def sib_copy(qs):
        return remote(
            sib_send.at[qs], sib_recv.at[qs], sib_s.at[qs], sib_r.at[qs], dp, sib
        )

    def g_copy(k, qs):
        return remote(
            grad_all.at[rows_at(qs, ROWS), k * HEAD : (k + 1) * HEAD],
            grad_h.at[chip, :, k * HEAD : (k + 1) * HEAD],
            g_s.at[k, qs],
            g_r.at[k, chip],
            dp,
            2 * qs + core,
        )

    def l_copy(qs):
        return remote(
            out_s.at[qs], lo_v.at[:, lanes_at(chip)], l_s.at[qs], l_r.at[chip], dp, 2 * qs + core
        )

    def backward(step, carry):
        qs = CHIPS - 1 - step
        block = 2 * qs + core
        mine = rows_at(qs, ROWS)
        for d in (1, 3, 2):
            here = stat_s.at[qs, lax.rem(chip + CHIPS - d, CHIPS)]
            remote(here, here, stat_ss.at[qs, d], stat_sr.at[qs, d], dp, sib).wait_recv()
        stats = [stat_s[qs, h] for h in range(4)]
        mean = sum(s[0:1, :] for s in stats) * (1.0 / BLOCK)
        gaps = [s[0:1, :] * (1.0 / HEAD) - mean for s in stats]
        spread = sum(s[1:2, :] + HEAD * g * g for s, g in zip(stats, gaps)) * (1.0 / BLOCK)
        scale = lax.rsqrt(spread + epsilon)
        mean_q = sum(s[2:3, :] for s in stats) * (1.0 / BLOCK)
        mean_qn = sum(s[3:4, :] + g * s[2:3, :] for s, g in zip(stats, gaps))
        mean_qn = mean_qn * scale * (1.0 / BLOCK)
        whole = jnp.concatenate(
            [mean, scale, mean_q, mean_qn, jnp.zeros((124, ROWS), F32)], axis=0
        )
        cols = jnp.transpose(whole)
        mean, scale = cols[:, 0:1], cols[:, 1:2]
        mean_q, mean_qn = cols[:, 2:3], cols[:, 3:4]
        normed = (mixed_s[qs] - mean) * scale
        gates = act_s[qs, :, 0:HEAD].astype(F32)
        cotangent = c_g[qs].astype(F32)
        out_s[qs] = (normed * gates).astype(BF)
        mixed_grad = ((cotangent * gates - mean_q - normed * mean_qn) * scale).astype(BF)
        grad_all[mine, 0:HEAD] = (cotangent * normed * p_s[qs, :, 0:HEAD]).astype(BF)

        @pl.when(qs != chip)
        def _():
            l_copy(qs).start()
            g_copy(0, qs).start()

        queries = act_s[qs, :, 2 * HEAD : 3 * HEAD]
        tq = tcol_s[block][:, 0:1]
        dq_s[...] = jnp.zeros_like(dq_s)
        hist_s[...] = jnp.zeros_like(hist_s)

        def tile(p, carry):
            span = rows_at(p, PAIR)
            keys = kv[span, 0:HEAD]
            values = kv[span, HEAD : 2 * HEAD]
            score = dot_nt(mixed_grad, values) * slope_s[qs, p]
            near = jnp.where(tq - key_times(p) < LEVELS - 1.0, score, 0.0).astype(BF)
            half = score.astype(BF)
            tot_s[...] += jnp.sum(score.reshape(ROWS // 8, 8, PAIR), axis=0)
            hist_s[...] += dot_nn(near, hot_s[span, :])
            dq_s[...] += dot_nn(half, keys)
            dk_s[span, :] += dot_tn(half, queries)
            dv_s[span, :] += dot_tn(weight_s[qs, p], mixed_grad)
            return carry

        lax.fori_loop(0, qs + 1, tile, 0)
        hot = hot_s[rows_at(block, ROWS), :]
        high = hist_s[...].astype(BF)
        low = (hist_s[...] - high.astype(F32)).astype(BF)
        htot_s[...] += dot_tn(hot, high) + dot_tn(hot, low)
        grad_all[mine, 2 * HEAD : 3 * HEAD] = (
            dq_s[...] * SCALE * p_s[qs, :, 2 * HEAD : 3 * HEAD]
        ).astype(BF)
        other = rows_at(2 * qs + 1 - core, ROWS)
        sib_send[qs, :, 0:HEAD] = dk_s[other, :].astype(BF)
        sib_send[qs, :, HEAD : 2 * HEAD] = dv_s[other, :].astype(BF)
        sib_copy(qs).start()

        @pl.when(qs != chip)
        def _():
            g_copy(2, qs).start()

        return carry

    lax.fori_loop(0, CHIPS, backward, 0)

    shape = (128, 128)
    gap = (iota(shape, 0) - iota(shape, 1)) & 15
    hist = htot_s[...]
    rows = [
        jnp.sum(jnp.where(gap == b, hist, 0.0), axis=0, keepdims=True) for b in range(LEVELS - 1)
    ]
    total = jnp.sum(tot_s[...], axis=0, keepdims=True)
    total = sum(total[:, i : i + 128] for i in range(0, PAIR, 128))
    rows.append(total - sum(rows))
    levels = jnp.sum(jnp.concatenate(rows, axis=0), axis=1, keepdims=True)
    levels = sbias_s[...] + jnp.where(level_lane == chip, levels, 0.0)
    levels = jnp.concatenate([levels, jnp.zeros((128 - LEVELS, 128), F32)], axis=0)
    b_send[...] = jnp.transpose(levels)[0:8, :]

    def b2_copy(o):
        return remote(
            b_send, b_ctx.at[ctx], b2_s.at[o], b2_r.at[o], dp, lax.rem(ctx + o, 2 * CHIPS)
        )

    def start_b2(o, carry):
        b2_copy(o).start()
        return carry

    lax.fori_loop(1, 2 * CHIPS, start_b2, 0)
    b_ctx[ctx] = b_send[...]

    def finish(step, carry):
        qs = CHIPS - 1 - step
        sib_copy(qs).wait_recv()
        mine = rows_at(qs, ROWS)
        block = rows_at(2 * qs + core, ROWS)
        dk = (dk_s[block, :] + sib_recv[qs, :, 0:HEAD].astype(F32)) * SCALE
        dv = dv_s[block, :] + sib_recv[qs, :, HEAD : 2 * HEAD].astype(F32)
        grad_all[mine, HEAD : 2 * HEAD] = (
            dv * p_s[qs, :, HEAD : 2 * HEAD]
        ).astype(BF)
        grad_all[mine, 3 * HEAD : 4 * HEAD] = (
            dk * p_s[qs, :, 3 * HEAD : 4 * HEAD]
        ).astype(BF)

        @pl.when(qs != chip)
        def _():
            g_copy(1, qs).start()
            g_copy(3, qs).start()

        return carry

    lax.fori_loop(0, CHIPS, finish, 0)

    for d in (1, 3, 2):
        src = lax.rem(chip + CHIPS - d, CHIPS)
        there = pl.ds(pl.multiple_of(LONG_ROWS + src * SHORT, SHORT), SHORT)
        remote(stok, tok_all.at[there, :], st_s.at[d], st_r.at[d], dp, sib).wait_recv()
        remote(sgrad_s.at[src], grad_all.at[there, :], sg_s.at[d], sg_r.at[d], dp, sib).wait_recv()

    half_dp = n_dp // 2
    half_model = MODEL // 2
    my_half = lax.div(dp, half_dp)
    halves = (my_half, 1 - my_half)

    def outer(pair, half):
        cols = pl.ds(pl.multiple_of(pair * 2 * HEAD, 2 * HEAD), 2 * HEAD)
        rows = pl.ds(pl.multiple_of(half * half_model, half_model), half_model)
        return dot_tn(tok_all[:, rows], grad_all[:, cols])

    def swap(j):
        return remote(half_send.at[j], half_recv.at[j], p_ss.at[j], p_sr.at[j], dp, sib)

    for j in range(2):
        half_send[j] = outer(1 - core, halves[j]).astype(BF)
        swap(j).start()
    for j in range(2):
        own[...] = outer(core, halves[j])
        swap(j).wait_recv()
        total = (own[...] + half_recv[j].astype(F32)).astype(BF)
        first = halves[j] * half_dp
        rs_send[pl.ds(first, half_dp)] = total.reshape((half_dp,) + rs_send.shape[1:])

        def start_rs(o, carry):
            peer = first + lax.rem(dp + o, half_dp)
            remote(rs_send.at[peer], rs_recv.at[dp], rs_s, rs_r, peer, ctx).start()
            return carry

        lax.fori_loop(1 - j, half_dp, start_rs, 0)
    rs_recv[dp] = rs_send[dp]

    def wait_b2(o, carry):
        src = lax.rem(ctx + 2 * CHIPS - o, 2 * CHIPS)
        remote(b_send, b_ctx.at[src], b2_s.at[o], b2_r.at[o], dp, src).wait_recv()
        return carry

    lax.fori_loop(1, 2 * CHIPS, wait_b2, 0)
    b_mid[...] = jnp.sum(b_ctx[...], axis=0)
    one_start(b_mid, b_dp, b1_s, b1_r)
    b_dp[dp] = b_mid[...]

    def write(source, target, index):
        return pltpu.make_async_copy(source, target, out_sem.at[index])

    dp_all(obuf, orecv, o_s, o_r).wait_recv()
    so_v[...] = dot_tn(place_s[...], orecv[...].reshape(n_dp * SLEN, BLOCK)).astype(BF)
    write(so_v, short_out, 1).start()
    total = dot_nt(sgrad_s[0], wh[0])
    for h in range(1, 4):
        total = total + dot_nt(sgrad_s[h], wh[h])
    sg_v[...] = total.astype(BF)
    write(sg_v, short_grad, 3).start()

    lo_v[:, lanes_at(chip)] = out_s[chip]
    grad_h[chip] = grad_all[rows_at(chip, ROWS), :]
    total = dot_nt(grad_h[chip], wh[chip])
    for d in (1, 3, 2):
        src = lax.rem(chip + CHIPS - d, CHIPS)
        for k in range(4):
            here = grad_h.at[src, :, k * HEAD : (k + 1) * HEAD]
            remote(here, here, g_s.at[k, src], g_r.at[k, src], dp, sib).wait_recv()
        here = lo_v.at[:, lanes_at(src)]
        remote(out_s.at[src], here, l_s.at[src], l_r.at[src], dp, sib).wait_recv()
        total = total + dot_nt(grad_h[src], wh[src])
    tg_v[...] = total.astype(BF)
    write(tg_v, token_grad, 2).start()
    write(lo_v, long_out, 0).start()

    half_copy(up, 0, 0).wait_send()
    half_copy(up, 1, 0).wait_send()
    half_copy(down, 0, 1).wait_send()
    half_copy(down, 1, 1).wait_send()
    pass_copy(down, 0, up).wait_send()
    pass_copy(up, 1, down).wait_send()
    for d in (1, 3, 2):
        c_copy(d).wait_send()
        st_copy(d).wait_send()
        sg_copy(d).wait_send()
    one_all(dest_g, d_s, d_r).wait_send()
    dp_all(cbuf, crecv, s_s, s_r).wait_send()
    dp_all(obuf, orecv, o_s, o_r).wait_send()

    def ended_o(o, carry):
        t_copy(o).wait_send()
        b2_copy(o).wait_send()
        return carry

    lax.fori_loop(1, 2 * CHIPS, ended_o, 0)

    def ended_q(qs, carry):
        kv_copy(qs).wait_send()
        sib_copy(qs).wait_send()
        for d in (1, 3, 2):
            stat_copy(qs, d).wait_send()

        @pl.when(qs != chip)
        def _():
            l_copy(qs).wait_send()
            for k in range(4):
                g_copy(k, qs).wait_send()

        return carry

    lax.fori_loop(0, CHIPS, ended_q, 0)
    for j in range(2):
        swap(j).wait_send()

    dp_all(rs_send, rs_recv, rs_s, rs_r).wait_recv()
    piece[...] = jnp.sum(rs_recv[...].astype(F32), axis=0)
    mine = lax.rem(chip, 2)

    def f_copy(i):
        target = 2 * (2 * core + i) + lax.div(chip, 2)
        return target, remote(
            piece.at[:, i * HEAD : (i + 1) * HEAD],
            proj_grad.at[:, lanes_at(mine)],
            f_s.at[i],
            f_r.at[mine],
            dp,
            target,
        )

    for i in range(2):
        target, copy = f_copy(i)

        @pl.when(target != ctx)
        def _():
            copy.start()

        @pl.when(target == ctx)
        def _():
            proj_grad[:, lanes_at(mine)] = piece[:, i * HEAD : (i + 1) * HEAD]

    one_all(b_dp, b1_s, b1_r).wait_recv()
    bias_out[...] = jnp.sum(b_dp[...], axis=0)[0:4, 0:LEVELS]

    for half in range(2):
        source = 2 * (2 * core + half) + lax.div(chip, 2)

        @pl.when(source != ctx)
        def _():
            remote(
                piece.at[:, 0:HEAD],
                proj_grad.at[:, half * HEAD : (half + 1) * HEAD],
                f_s.at[half],
                f_r.at[half],
                dp,
                source,
            ).wait_recv()

    for i in range(2):
        target, copy = f_copy(i)

        @pl.when(target != ctx)
        def _():
            copy.wait_send()

    dp_all(rs_send, rs_recv, rs_s, rs_r).wait_send()
    one_all(b_dp, b1_s, b1_r).wait_send()
    write(lo_v, long_out, 0).wait()
    write(so_v, short_out, 1).wait()
    write(tg_v, token_grad, 2).wait()
    write(sg_v, short_grad, 3).wait()


def output_kernel(count, *refs):
    for i in range(count):
        refs[count + i][...] = refs[i][...]


VM = pl.BlockSpec(memory_space=pltpu.VMEM)
SM = pl.BlockSpec(memory_space=pltpu.SMEM)
ANY = pl.BlockSpec(memory_space=pl.ANY)
DMA = pltpu.SemaphoreType.DMA
VMEM = pltpu.VMEM


def shaped(shape, dtype):
    return jax.ShapeDtypeStruct(shape, dtype)


def per_device(
    n_dp,
    long_tokens,
    short_tokens,
    projection,
    time_bias,
    long_length,
    short_length,
    long_time,
    short_time,
    destination,
    long_cotangent,
    short_cotangent,
):
    part = MODEL // n_dp
    spread = (n_dp, SLEN, BLOCK)
    scratch = [
        VMEM((CHIPS, MODEL, BLOCK), BF),
        VMEM((ALL_ROWS, MODEL), BF),
        VMEM((ALL_ROWS, BLOCK), BF),
        VMEM((CHIPS, ROWS, BLOCK), F32),
        VMEM((CHIPS, ROWS, BLOCK), BF),
        VMEM((2 * CHIPS * ROWS, 2 * HEAD), BF),
        VMEM((CHIPS, ROWS, HEAD), BF),
        VMEM((8, ROWS), jnp.int32),
        VMEM((2 * CHIPS, 8, ROWS), jnp.int32),
        VMEM((8, 128), F32),
        VMEM((8, 128), jnp.int32),
        VMEM((8, 128), jnp.int32),
        VMEM((n_dp, 8, 128), jnp.int32),
        VMEM((n_dp * SLEN, 128), BF),
        VMEM(spread, BF),
        VMEM(spread, BF),
        VMEM((4, SHORT, BLOCK), F32),
        VMEM((4, SHORT, BLOCK), BF),
        VMEM((4, SHORT, SHORT), BF),
        VMEM((4, SHORT, SHORT), F32),
        VMEM((4, SHORT, HEAD), F32),
        VMEM((SHORT, 128), F32),
        VMEM((SHORT, BLOCK), F32),
        VMEM((4, SHORT, BLOCK), BF),
        VMEM(spread, BF),
        VMEM(spread, BF),
        VMEM((LEVELS, 128), F32),
        VMEM((CHIPS, CHIPS, ROWS, PAIR), BF),
        VMEM((CHIPS, CHIPS, ROWS, PAIR), F32),
        VMEM((CHIPS, ROWS, HEAD), F32),
        VMEM((CHIPS, ROWS, HEAD), BF),
        VMEM((2 * CHIPS * ROWS, 128), BF),
        VMEM((2 * CHIPS, ROWS, 128), F32),
        VMEM((CHIPS, CHIPS, 8, ROWS), F32),
        VMEM((2 * CHIPS * ROWS, HEAD), F32),
        VMEM((2 * CHIPS * ROWS, HEAD), F32),
        VMEM((ROWS, HEAD), F32),
        VMEM((ROWS, 128), F32),
        VMEM((128, 128), F32),
        VMEM((8, PAIR), F32),
        VMEM((CHIPS, ROWS, 2 * HEAD), BF),
        VMEM((CHIPS, ROWS, 2 * HEAD), BF),
        VMEM((CHIPS, ROWS, BLOCK), BF),
        VMEM((2, MODEL // 2, 2 * HEAD), BF),
        VMEM((2, MODEL // 2, 2 * HEAD), BF),
        VMEM((MODEL // 2, 2 * HEAD), F32),
        VMEM((n_dp, part, 2 * HEAD), BF),
        VMEM((n_dp, part, 2 * HEAD), BF),
        VMEM((8, 128), F32),
        VMEM((n_dp, 8, 128), F32),
        VMEM((8, 128), F32),
        VMEM((2 * CHIPS, 8, 128), F32),
        VMEM((part, 2 * HEAD), F32),
        VMEM((ROWS, BLOCK), BF),
        VMEM((SHORT, BLOCK), BF),
        VMEM((ROWS, MODEL), BF),
        VMEM((SHORT, MODEL), BF),
        DMA((4, 4)),
        DMA((3,)),
        DMA((4,)),
        DMA((2, 2)),
        DMA((2, 2)),
        DMA((2,)),
        DMA((2,)),
        DMA((CHIPS,)),
        DMA((CHIPS,)),
        DMA((2 * CHIPS,)),
        DMA((2 * CHIPS,)),
        DMA((CHIPS,)),
        DMA((CHIPS,)),
        DMA((CHIPS,)),
        DMA((CHIPS,)),
        DMA((CHIPS,)),
        DMA((CHIPS,)),
        DMA,
        DMA,
        DMA,
        DMA,
        DMA,
        DMA,
        DMA((CHIPS, CHIPS)),
        DMA((CHIPS, CHIPS)),
        DMA((CHIPS,)),
        DMA((CHIPS,)),
        DMA((4, CHIPS)),
        DMA((4, CHIPS)),
        DMA((CHIPS,)),
        DMA((CHIPS,)),
        DMA((2,)),
        DMA((2,)),
        DMA,
        DMA,
        DMA,
        DMA,
        DMA((2 * CHIPS,)),
        DMA((2 * CHIPS,)),
        DMA((2,)),
        DMA((2,)),
    ]
    results = pl.pallas_call(
        functools.partial(layer_kernel, n_dp),
        out_shape=(
            shaped((ROWS, BLOCK), BF),
            shaped((SHORT, BLOCK), BF),
            shaped((ROWS, MODEL), BF),
            shaped((SHORT, MODEL), BF),
            shaped((part, 2 * HEAD), F32),
            shaped(time_bias.shape, F32),
        ),
        in_specs=[ANY, ANY, ANY, ANY, VM, VM, VM, VM, VM, SM, VM],
        out_specs=(ANY,) * 4 + (VM,) * 2,
        scratch_shapes=scratch,
        compiler_params=pltpu.CompilerParams(
            vmem_limit_bytes=VMEM_LIMIT, collective_id=0, has_side_effects=True
        ),
        name="layer",
    )(
        long_tokens[0],
        short_tokens.reshape(SHORT, MODEL),
        projection,
        long_cotangent[0],
        short_cotangent.reshape(SHORT, BLOCK),
        long_time,
        short_time,
        short_length,
        destination,
        long_length,
        time_bias,
    )
    results = pl.pallas_call(
        functools.partial(output_kernel, len(results)),
        out_shape=tuple(shaped(r.shape, r.dtype) for r in results),
        in_specs=[VM] * len(results),
        out_specs=(VM,) * len(results),
        compiler_params=pltpu.CompilerParams(vmem_limit_bytes=VMEM_LIMIT),
        name="output",
    )(*results)
    long_out, short_out, token_grad, short_grad, proj_grad, bias_out = results
    return (
        long_out[None],
        short_out.reshape(short_cotangent.shape),
        token_grad[None],
        short_grad.reshape(short_tokens.shape),
        proj_grad,
        bias_out,
    )


def solution(mesh):
    return jax.shard_map(
        functools.partial(per_device, mesh.shape["dp"]),
        mesh=mesh,
        in_specs=(
            P("dp", "ctx", None),
            P("dp", "ctx", None, None),
            P(),
            P(),
            P("dp"),
            P("dp", "ctx"),
            P("dp", "ctx"),
            P("dp", "ctx", None),
            P("dp", "ctx"),
            P("dp", "ctx", None),
            P("dp", "ctx", None, None),
        ),
        out_specs=(
            P("dp", "ctx", None),
            P("dp", "ctx", None, None),
            P("dp", "ctx", None),
            P("dp", "ctx", None, None),
            P("dp", "ctx"),
            P(),
        ),
        check_vma=False,
    )
```

```python
import functools

import jax
import jax.numpy as jnp
from jax import lax
from jax.experimental import pallas as pl
from jax.experimental.pallas import tpu as pltpu
from jax.sharding import PartitionSpec as P

epsilon = 1e-05
MESH = pl.DeviceIdType.MESH
BF = jnp.bfloat16
F32 = jnp.float32
CHIPS = 4
NZ = 8
ROWS = 256
HEAD = 128
LEVELS = 16
SLEN = 16
SHORT = 128
LONG_ROWS = CHIPS * ROWS
ALL_ROWS = CHIPS * (ROWS + SHORT)
PAIR = 2 * ROWS
MODEL = 1024
BLOCK = 512
SCALE = HEAD ** (-0.5)
VMEM_LIMIT = 56 * 1024 * 1024


def sigmoid(value):
    return 0.5 * jnp.tanh(0.5 * value) + 0.5


def silu_and_grad(value):
    sigma = sigmoid(value)
    silu = value * sigma
    return silu.astype(BF), sigma + silu * (1.0 - sigma)


def dot_nn(a, b):
    return jnp.dot(a, b, preferred_element_type=F32)


def dot_nt(a, b):
    return lax.dot_general(a, b, (((1,), (1,)), ((), ())), preferred_element_type=F32)


def dot_tn(a, b):
    return lax.dot_general(a, b, (((0,), (0,)), ((), ())), preferred_element_type=F32)


def column_of(row):
    return jnp.transpose(jnp.broadcast_to(row, (128, 128)))


def iota(shape, axis):
    return lax.broadcasted_iota(jnp.int32, shape, axis)


def remote(src, dst, send_sem, recv_sem, dp, ctx):
    return pltpu.make_async_remote_copy(
        src_ref=src,
        dst_ref=dst,
        send_sem=send_sem,
        recv_sem=recv_sem,
        device_id=(dp, ctx),
        device_id_type=MESH,
    )


def place():
    dp = lax.axis_index("dp")
    ctx = lax.axis_index("ctx")
    return dp, ctx, lax.div(ctx, 2), lax.rem(ctx, 2)


def lookup(table, diff):
    index = jnp.clip(diff, 0.0, LEVELS - 1.0).astype(jnp.int32)
    parts = [
        jnp.take_along_axis(table, index[:, i : i + 128], axis=1)
        for i in range(0, index.shape[1], 128)
    ]
    return parts[0] if len(parts) == 1 else jnp.concatenate(parts, axis=1)


def exact_dot(a, b):
    return lax.dot_general(
        a,
        b,
        (((1,), (0,)), ((), ())),
        precision=lax.Precision.HIGHEST,
        preferred_element_type=F32,
    )


def rows_at(block, rows):
    return pl.ds(pl.multiple_of(block * rows, rows), rows)


def lanes_at(block):
    return pl.ds(pl.multiple_of(block * HEAD, HEAD), HEAD)


def layer_kernel(
    n_dp,
    tok,
    stok,
    w,
    lcot,
    scot,
    ltime,
    stime,
    slen,
    dest_in,
    llen,
    tbias,
    long_out,
    short_out,
    token_grad,
    short_grad,
    proj_grad,
    bias_out,
    wh,
    tok_all,
    grad_all,
    p_s,
    act_s,
    kv,
    c_g,
    tmeta,
    times,
    tab_s,
    ints,
    dtile,
    dest_g,
    place_s,
    cbuf,
    crecv,
    sp_s,
    sact_s,
    sweight_s,
    sslope_s,
    snorm_s,
    sscale_s,
    c_home,
    sgrad_s,
    obuf,
    omid,
    orecv,
    sbias_s,
    weight_s,
    slope_s,
    mixed_s,
    out_s,
    hot_s,
    tcol_s,
    stat_s,
    dk_s,
    dv_s,
    dq_s,
    hist_s,
    htot_s,
    tot_s,
    sib_send,
    sib_recv,
    grad_h,
    half_send,
    half_recv,
    own,
    rs_send,
    rs_mid,
    rs_sum,
    rs_fin,
    b_send,
    b_dp,
    b_mid,
    b_ctx,
    piece,
    lo_v,
    so_v,
    tg_v,
    sg_v,
    w_sem,
    in_sem,
    out_sem,
    tok_s,
    tok_r,
    fwd_s,
    fwd_r,
    c_s,
    c_r,
    t_s,
    t_r,
    kv_s,
    kv_r,
    st_s,
    st_r,
    sg_s,
    sg_r,
    d_s,
    d_r,
    s_s,
    s_r,
    oy_s,
    oy_r,
    oz_s,
    oz_r,
    stat_ss,
    stat_sr,
    sib_s,
    sib_r,
    g_s,
    g_r,
    l_s,
    l_r,
    p_ss,
    p_sr,
    ry_s,
    ry_r,
    rz_s,
    rz_r,
    b1_s,
    b1_r,
    b2_s,
    b2_r,
    f_s,
    f_r,
):
    dp, ctx, chip, core = place()
    sib = ctx + 1 - 2 * core
    up = lax.rem(chip + 1, CHIPS)
    down = lax.rem(chip + CHIPS - 1, CHIPS)
    far = lax.rem(chip + 2, CHIPS)
    half_rows = ROWS // 2
    ny = n_dp // NZ
    y, z = lax.div(dp, NZ), lax.rem(dp, NZ)
    barrier = pltpu.get_barrier_semaphore()

    def greet_ctx(o, carry):
        pl.semaphore_signal(
            barrier, inc=1, device_id=(dp, lax.rem(ctx + o, 2 * CHIPS)), device_id_type=MESH
        )
        return carry

    def greet_dp(o, carry):
        pl.semaphore_signal(
            barrier, inc=1, device_id=(lax.rem(dp + o, n_dp), ctx), device_id_type=MESH
        )
        return carry

    lax.fori_loop(1, 2 * CHIPS, greet_ctx, 0)
    lax.fori_loop(1, n_dp, greet_dp, 0)

    def w_copy(h, k):
        return pltpu.make_async_copy(
            w.at[:, k * BLOCK + h * HEAD : k * BLOCK + (h + 1) * HEAD],
            wh.at[h, :, k * HEAD : (k + 1) * HEAD],
            w_sem.at[h, k],
        )

    for h in range(4):
        for k in range(4):
            w_copy(h, k).start()
    tmeta[...] = jnp.broadcast_to(ltime[...], (8, ROWS))
    ints[...] = jnp.zeros((8, 128), jnp.int32) - 1
    ints[0:1, 0:8] = slen[...]
    ints[1:2, 0:8] = dest_in[...]
    dtile[...] = jnp.broadcast_to(ints[1:2, :], (8, 128))
    tab_s[...] = jnp.zeros_like(tab_s)
    tab_s[0:4, 0:LEVELS] = tbias[...]

    def half_copy(peer, half, index):
        return remote(
            tok.at[half * half_rows : (half + 1) * half_rows, :],
            tok_all.at[rows_at(2 * chip + half, half_rows), :],
            tok_s.at[index, half],
            tok_r.at[index, half],
            dp,
            2 * peer + core,
        )

    def half_wait(src, half, index):
        here = tok_all.at[rows_at(2 * src + half, half_rows), :]
        remote(here, here, tok_s.at[index, half], tok_r.at[index, half], dp, sib).wait_recv()

    def pass_copy(src, half, peer):
        here = tok_all.at[rows_at(2 * src + half, half_rows), :]
        return remote(here, here, fwd_s.at[half], fwd_r.at[half], dp, 2 * peer + core)

    def c_copy(d):
        peer = lax.rem(chip + d, CHIPS)
        return remote(
            lcot.at[:, lanes_at(peer)], c_g.at[chip], c_s.at[d], c_r.at[d], dp, 2 * peer + core
        )

    def t_copy(o):
        return remote(
            tmeta, times.at[ctx], t_s.at[o], t_r.at[o], dp, lax.rem(ctx + o, 2 * CHIPS)
        )

    def kv_copy(src):
        here = kv.at[rows_at(2 * src + core, ROWS), :]
        return remote(here, here, kv_s.at[src], kv_r.at[src], dp, sib)

    def kv_wait(src):
        here = kv.at[rows_at(2 * src + 1 - core, ROWS), :]
        remote(here, here, kv_s.at[src], kv_r.at[src], dp, sib).wait_recv()

    def st_copy(d):
        return remote(
            stok,
            tok_all.at[pl.ds(pl.multiple_of(LONG_ROWS + chip * SHORT, SHORT), SHORT), :],
            st_s.at[d],
            st_r.at[d],
            dp,
            2 * lax.rem(chip + d, CHIPS) + core,
        )

    def sg_copy(d):
        peer = lax.rem(chip + d, CHIPS)
        return remote(
            sgrad_s.at[peer],
            grad_all.at[pl.ds(pl.multiple_of(LONG_ROWS + chip * SHORT, SHORT), SHORT), :],
            sg_s.at[d],
            sg_r.at[d],
            dp,
            2 * peer + core,
        )

    def dp_start(source, target, send, recv):
        def one(o, carry):
            peer = lax.rem(dp + o, n_dp)
            remote(source.at[peer], target.at[dp], send, recv, peer, ctx).start()
            return carry

        lax.fori_loop(1, n_dp, one, 0)

    def dp_all(source, target, send, recv):
        return remote(
            source.at[0 : n_dp - 1], target.at[0 : n_dp - 1], send, recv, dp, sib
        )

    def one_start(source, target, send, recv):
        def one(o, carry):
            remote(source, target.at[dp], send, recv, lax.rem(dp + o, n_dp), ctx).start()
            return carry

        lax.fori_loop(1, n_dp, one, 0)

    def one_all(target, send, recv):
        here = target.at[0 : n_dp - 1]
        return remote(here, here, send, recv, dp, sib)

    home_rows = pl.ds(pl.multiple_of(LONG_ROWS + chip * SHORT, SHORT), SHORT)
    loads = [
        pltpu.make_async_copy(tok, tok_all.at[rows_at(chip, ROWS), :], in_sem.at[0]),
        pltpu.make_async_copy(stok, tok_all.at[home_rows, :], in_sem.at[1]),
        pltpu.make_async_copy(lcot.at[:, lanes_at(chip)], c_g.at[chip], in_sem.at[2]),
    ]
    for load in loads:
        load.start()
    pl.semaphore_wait(barrier, n_dp - 1 + 2 * CHIPS - 1)
    half_copy(up, 0, 0).start()
    half_copy(down, 1, 1).start()
    half_copy(up, 1, 0).start()
    half_copy(down, 0, 1).start()
    one_start(dtile, dest_g, d_s, d_r)

    def start_t(o, carry):
        t_copy(o).start()
        return carry

    lax.fori_loop(1, 2 * CHIPS, start_t, 0)
    times[ctx] = tmeta[...]
    dest_g[dp] = dtile[...]
    for h in range(4):
        for k in range(4):
            w_copy(h, k).wait()
    for load in loads:
        load.wait()

    def project(src):
        projected = dot_nn(tok_all[rows_at(src, ROWS), :], wh[chip])
        act, p_s[src] = silu_and_grad(projected)
        act_s[src] = act
        kv[rows_at(2 * src + core, ROWS), 0:HEAD] = act[:, 3 * HEAD : 4 * HEAD]
        kv[rows_at(2 * src + core, ROWS), HEAD : 2 * HEAD] = act[:, HEAD : 2 * HEAD]
        kv_copy(src).start()

    project(chip)

    lane16 = iota((16, 128), 1)
    spread_time = exact_dot(
        stime[0].astype(F32), jnp.where((lane16 & 15) == iota((16, 128), 0), 1.0, 0.0)
    )
    pick = (iota((8, 128), 1) >> 4) == iota((8, 128), 0)
    stime_row = jnp.sum(jnp.where(pick, spread_time, 0.0), axis=0, keepdims=True)
    repeat = jnp.where((iota((128, 128), 1) >> 4) == iota((128, 128), 0), 1.0, 0.0)
    rep_rows = exact_dot(ints[...].astype(F32), repeat)
    slen_row, home_row = rep_rows[0:1, :], rep_rows[1:2, :]
    owner_row = (home_row.astype(jnp.int32) >> 3).astype(F32)
    shape = (SHORT, SHORT)
    row = iota(shape, 0)
    col = iota(shape, 1)
    stime_diff = column_of(stime_row) - stime_row
    inside = (row & 15).astype(F32) < column_of(slen_row)
    svisible = ((row >> 4) == (col >> 4)) & (col <= row) & inside

    short_tokens = tok_all[home_rows, :]
    mixes = []
    for h in range(4):
        act, sp_s[h] = silu_and_grad(dot_nn(short_tokens, wh[h]))
        sact_s[h] = act
        queries, keys = act[:, 2 * HEAD : 3 * HEAD], act[:, 3 * HEAD : 4 * HEAD]
        tab = jnp.broadcast_to(tab_s[h : h + 1, :], (SHORT, 128))
        total = dot_nt(queries, keys) * SCALE + lookup(tab, stime_diff)
        sg = sigmoid(total)
        weight = total * sg
        weight16 = jnp.where(svisible, weight, 0.0).astype(BF)
        sweight_s[h] = weight16
        sslope_s[h] = jnp.where(svisible, sg + weight * (1.0 - sg), 0.0)
        mixes.append(dot_nn(weight16, act[:, HEAD : 2 * HEAD]))
    mean = sum(jnp.sum(m, axis=1, keepdims=True) for m in mixes) * (1.0 / BLOCK)
    centred = [m - mean for m in mixes]
    spread = sum(jnp.sum(m * m, axis=1, keepdims=True) for m in centred) * (1.0 / BLOCK)
    scale = lax.rsqrt(spread + epsilon)
    sscale_s[...] = jnp.broadcast_to(scale, sscale_s.shape)
    for h in range(4):
        snorm_s[h] = centred[h] * scale

    one_all(dest_g, d_s, d_r).wait_recv()
    dest = dest_g[...]
    code = jnp.sum(
        jnp.where((dest >> 3) == dp, ((dest & 7) + 1).astype(F32), 0.0), axis=2, keepdims=True
    )
    code = jnp.broadcast_to(code, (n_dp, 8, 128))
    code = jnp.concatenate([code, code], axis=1).reshape(n_dp * SLEN, 128)
    shape = (n_dp * SLEN, 128)
    same = (iota(shape, 0) & 15) == (iota(shape, 1) & 15)
    slot = ((iota(shape, 1) >> 4) + 1).astype(F32)
    placer = jnp.where(same & (code == slot), 1.0, 0.0).astype(BF)
    place_s[...] = placer
    cbuf[...] = dot_nn(placer, scot[...]).astype(BF).reshape(cbuf.shape)
    dp_start(cbuf, crecv, s_s, s_r)
    crecv[dp] = cbuf[dp]

    half_wait(down, 0, 0)
    pass_copy(down, 0, up).start()
    half_wait(up, 1, 1)
    pass_copy(up, 1, down).start()
    for d in (1, 3, 2):
        c_copy(d).start()

    def wait_t(o, carry):
        src = lax.rem(ctx + 2 * CHIPS - o, 2 * CHIPS)
        remote(tmeta, times.at[src], t_s.at[o], t_r.at[o], dp, src).wait_recv()
        return carry

    lax.fori_loop(1, 2 * CHIPS, wait_t, 0)
    lane = iota((ROWS, 128), 1)

    def times_of(b, carry):
        line = times[b, 0:1, :].astype(F32)
        column = jnp.concatenate(
            [column_of(line[:, 0:128]), column_of(line[:, 128:256])], axis=0
        )
        tcol_s[b] = column
        hot_s[rows_at(b, ROWS), :] = jnp.where(
            (column.astype(jnp.int32) & 15) == lane, 1.0, 0.0
        ).astype(BF)
        return carry

    lax.fori_loop(0, 2 * CHIPS, times_of, 0)
    dk_s[...] = jnp.zeros_like(dk_s)
    dv_s[...] = jnp.zeros_like(dv_s)
    htot_s[...] = jnp.zeros_like(htot_s)
    tot_s[...] = jnp.zeros_like(tot_s)
    mixed_s[...] = jnp.zeros_like(mixed_s)

    half_wait(down, 1, 0)
    project(down)
    half_wait(up, 0, 1)
    project(up)

    table = jnp.broadcast_to(tab_s[pl.ds(chip, 1), :], (ROWS, 128))
    length = llen[0]

    def key_times(p):
        return jnp.concatenate(
            [times[2 * p, 0:1, :], times[2 * p + 1, 0:1, :]], axis=1
        ).astype(F32)

    def forward_tile(qs, p):
        block = 2 * qs + core
        queries = act_s[qs, :, 2 * HEAD : 3 * HEAD]
        tq = tcol_s[block][:, 0:1]
        spot = iota((ROWS, 1), 0) + block * ROWS
        limit = jnp.where(spot < length, spot, -1)
        keys = kv[rows_at(p, PAIR), 0:HEAD]
        values = kv[rows_at(p, PAIR), HEAD : 2 * HEAD]
        total = dot_nt(queries, keys) * SCALE + lookup(table, tq - key_times(p))
        sg = sigmoid(total)
        weight = total * sg
        visible = (iota((ROWS, PAIR), 1) + p * PAIR) <= limit
        weight16 = jnp.where(visible, weight, 0.0).astype(BF)
        weight_s[qs, p] = weight16
        slope_s[qs, p] = jnp.where(visible, sg + weight * (1.0 - sg), 0.0)
        mixed_s[qs] += dot_nn(weight16, values)

    for d in (0, 1, 3):
        kv_wait(lax.rem(chip + CHIPS - d, CHIPS))

    def near_block(step, carry):
        qs = CHIPS - 1 - step

        def one(p, carry):
            @pl.when(p != far)
            def _():
                forward_tile(qs, p)

            return carry

        lax.fori_loop(0, jnp.where(qs == far, 0, qs + 1), one, 0)
        return carry

    lax.fori_loop(0, CHIPS, near_block, 0)

    for half in range(2):
        here = tok_all.at[rows_at(2 * far + half, half_rows), :]
        remote(here, here, fwd_s.at[half], fwd_r.at[half], dp, sib).wait_recv()
    project(far)
    for d in (1, 3, 2):
        st_copy(d).start()
    for d in (1, 3, 2):
        src = lax.rem(chip + CHIPS - d, CHIPS)
        remote(c_g.at[src], c_g.at[src], c_s.at[d], c_r.at[d], dp, sib).wait_recv()
    kv_wait(far)

    def stat_copy(qs, d):
        here = stat_s.at[qs, chip]
        return remote(
            here,
            here,
            stat_ss.at[qs, d],
            stat_sr.at[qs, d],
            dp,
            2 * lax.rem(chip + d, CHIPS) + core,
        )

    def far_block(step, carry):
        qs = CHIPS - 1 - step

        def one(p, carry):
            forward_tile(qs, p)
            return carry

        first = jnp.where(qs == far, 0, far)
        last = jnp.where(qs >= far, jnp.where(qs == far, qs, far) + 1, first)
        lax.fori_loop(first, last, one, 0)
        mixed = mixed_s[qs]
        q = c_g[qs].astype(F32) * act_s[qs, :, 0:HEAD].astype(F32)
        s1 = jnp.sum(mixed, axis=1, keepdims=True)
        centred = mixed - s1 * (1.0 / HEAD)
        s2 = jnp.sum(centred * centred, axis=1, keepdims=True)
        s3 = jnp.sum(q, axis=1, keepdims=True)
        s4 = jnp.sum(q * centred, axis=1, keepdims=True)
        stats = jnp.where(
            lane == 0, s1, jnp.where(lane == 1, s2, jnp.where(lane == 2, s3, s4))
        )
        stat_s[qs, chip] = jnp.transpose(stats)[0:8, :]
        for d in (1, 3, 2):
            stat_copy(qs, d).start()
        return carry

    lax.fori_loop(0, CHIPS, far_block, 0)

    dp_all(cbuf, crecv, s_s, s_r).wait_recv()
    owner = jnp.concatenate([column_of(owner_row)] * (n_dp * SLEN // 128), axis=1)
    shape = (SHORT, n_dp * SLEN)
    same = (iota(shape, 0) & 15) == (iota(shape, 1) & 15)
    chooser = jnp.where(
        same & (owner == (iota(shape, 1) >> 4).astype(F32)), 1.0, 0.0
    ).astype(BF)
    c_home[...] = dot_nn(chooser, crecv[...].reshape(n_dp * SLEN, BLOCK))
    scale = sscale_s[:, 0:1]
    mean_q = jnp.zeros((SHORT, 1), F32)
    mean_qn = jnp.zeros((SHORT, 1), F32)
    for h in range(4):
        q = c_home[:, h * HEAD : (h + 1) * HEAD] * sact_s[h, :, 0:HEAD].astype(F32)
        mean_q = mean_q + jnp.sum(q, axis=1, keepdims=True)
        mean_qn = mean_qn + jnp.sum(q * snorm_s[h], axis=1, keepdims=True)
    mean_q = mean_q * (1.0 / BLOCK)
    mean_qn = mean_qn * (1.0 / BLOCK)
    bucket = jnp.clip(stime_diff, 0.0, LEVELS - 1.0).astype(jnp.int32)
    level_lane = iota((LEVELS, 128), 1)
    sums = jnp.zeros((LEVELS, 128), F32)
    outs = []
    for h in range(4):
        act = sact_s[h]
        gates = act[:, 0:HEAD].astype(F32)
        values = act[:, HEAD : 2 * HEAD]
        queries = act[:, 2 * HEAD : 3 * HEAD]
        keys = act[:, 3 * HEAD : 4 * HEAD]
        normed = snorm_s[h]
        cot = c_home[:, h * HEAD : (h + 1) * HEAD]
        outs.append((normed * gates).astype(BF))
        mixed_grad = ((cot * gates - mean_q - normed * mean_qn) * scale).astype(BF)
        score = dot_nt(mixed_grad, values) * sslope_s[h]
        rows = [
            jnp.sum(jnp.where(bucket == b, score, 0.0), axis=0, keepdims=True)
            for b in range(LEVELS)
        ]
        per_level = jnp.sum(jnp.concatenate(rows, axis=0), axis=1, keepdims=True)
        sums = sums + jnp.where(level_lane == h, per_level, 0.0)
        half = score.astype(BF)
        grads = [
            cot * normed,
            dot_tn(sweight_s[h], mixed_grad),
            dot_nn(half, keys) * SCALE,
            dot_tn(half, queries) * SCALE,
        ]
        for k in range(4):
            lanes = slice(k * HEAD, (k + 1) * HEAD)
            sgrad_s[h, :, lanes] = (grads[k] * sp_s[h, :, lanes]).astype(BF)
    sbias_s[...] = sums
    shape = (n_dp * SLEN, SHORT)
    same = (iota(shape, 0) & 15) == (iota(shape, 1) & 15)
    sender = jnp.where(
        same & (owner_row == (iota(shape, 0) >> 4).astype(F32)), 1.0, 0.0
    ).astype(BF)
    obuf[...] = dot_nn(sender, jnp.concatenate(outs, axis=1)).astype(BF).reshape(obuf.shape)
    for d in (1, 3, 2):
        sg_copy(d).start()
    grad_all[pl.ds(pl.multiple_of(LONG_ROWS + chip * SHORT, SHORT), SHORT), :] = sgrad_s[chip]

    def oy_copy(o):
        peer = lax.rem(y + o, ny)
        return remote(
            obuf.at[peer], omid.at[y], oy_s.at[o], oy_r.at[o], peer * NZ + z, ctx
        )

    def oz_copy(o):
        peer = lax.rem(z + o, NZ)
        return remote(
            omid.at[:, peer], orecv.at[:, z], oz_s.at[o], oz_r.at[o], y * NZ + peer, ctx
        )

    for o in range(1, ny):
        oy_copy(o).start()
    omid[y] = obuf[y]

    def sib_copy(qs):
        return remote(
            sib_send.at[qs], sib_recv.at[qs], sib_s.at[qs], sib_r.at[qs], dp, sib
        )

    def g_copy(k, qs):
        return remote(
            grad_all.at[rows_at(qs, ROWS), k * HEAD : (k + 1) * HEAD],
            grad_h.at[chip, :, k * HEAD : (k + 1) * HEAD],
            g_s.at[k, qs],
            g_r.at[k, chip],
            dp,
            2 * qs + core,
        )

    def l_copy(qs):
        return remote(
            out_s.at[qs], lo_v.at[:, lanes_at(chip)], l_s.at[qs], l_r.at[chip], dp, 2 * qs + core
        )

    def backward(step, carry):
        qs = CHIPS - 1 - step
        block = 2 * qs + core
        mine = rows_at(qs, ROWS)
        for d in (1, 3, 2):
            here = stat_s.at[qs, lax.rem(chip + CHIPS - d, CHIPS)]
            remote(here, here, stat_ss.at[qs, d], stat_sr.at[qs, d], dp, sib).wait_recv()
        stats = [stat_s[qs, h] for h in range(4)]
        mean = sum(s[0:1, :] for s in stats) * (1.0 / BLOCK)
        gaps = [s[0:1, :] * (1.0 / HEAD) - mean for s in stats]
        spread = sum(s[1:2, :] + HEAD * g * g for s, g in zip(stats, gaps)) * (1.0 / BLOCK)
        scale = lax.rsqrt(spread + epsilon)
        mean_q = sum(s[2:3, :] for s in stats) * (1.0 / BLOCK)
        mean_qn = sum(s[3:4, :] + g * s[2:3, :] for s, g in zip(stats, gaps))
        mean_qn = mean_qn * scale * (1.0 / BLOCK)
        whole = jnp.concatenate(
            [mean, scale, mean_q, mean_qn, jnp.zeros((124, ROWS), F32)], axis=0
        )
        cols = jnp.transpose(whole)
        mean, scale = cols[:, 0:1], cols[:, 1:2]
        mean_q, mean_qn = cols[:, 2:3], cols[:, 3:4]
        normed = (mixed_s[qs] - mean) * scale
        gates = act_s[qs, :, 0:HEAD].astype(F32)
        cotangent = c_g[qs].astype(F32)
        out_s[qs] = (normed * gates).astype(BF)
        mixed_grad = ((cotangent * gates - mean_q - normed * mean_qn) * scale).astype(BF)
        grad_all[mine, 0:HEAD] = (cotangent * normed * p_s[qs, :, 0:HEAD]).astype(BF)

        @pl.when(qs != chip)
        def _():
            l_copy(qs).start()
            g_copy(0, qs).start()

        queries = act_s[qs, :, 2 * HEAD : 3 * HEAD]
        tq = tcol_s[block][:, 0:1]
        dq_s[...] = jnp.zeros_like(dq_s)
        hist_s[...] = jnp.zeros_like(hist_s)

        def tile(p, carry):
            span = rows_at(p, PAIR)
            keys = kv[span, 0:HEAD]
            values = kv[span, HEAD : 2 * HEAD]
            score = dot_nt(mixed_grad, values) * slope_s[qs, p]
            near = jnp.where(tq - key_times(p) < LEVELS - 1.0, score, 0.0).astype(BF)
            half = score.astype(BF)
            tot_s[...] += jnp.sum(score.reshape(ROWS // 8, 8, PAIR), axis=0)
            hist_s[...] += dot_nn(near, hot_s[span, :])
            dq_s[...] += dot_nn(half, keys)
            dk_s[span, :] += dot_tn(half, queries)
            dv_s[span, :] += dot_tn(weight_s[qs, p], mixed_grad)
            return carry

        lax.fori_loop(0, qs + 1, tile, 0)
        hot = hot_s[rows_at(block, ROWS), :]
        high = hist_s[...].astype(BF)
        low = (hist_s[...] - high.astype(F32)).astype(BF)
        htot_s[...] += dot_tn(hot, high) + dot_tn(hot, low)
        grad_all[mine, 2 * HEAD : 3 * HEAD] = (
            dq_s[...] * SCALE * p_s[qs, :, 2 * HEAD : 3 * HEAD]
        ).astype(BF)
        other = rows_at(2 * qs + 1 - core, ROWS)
        sib_send[qs, :, 0:HEAD] = dk_s[other, :].astype(BF)
        sib_send[qs, :, HEAD : 2 * HEAD] = dv_s[other, :].astype(BF)
        sib_copy(qs).start()

        @pl.when(qs != chip)
        def _():
            g_copy(2, qs).start()

        return carry

    lax.fori_loop(0, CHIPS, backward, 0)

    for o in range(1, ny):
        here = omid.at[lax.rem(y + ny - o, ny)]
        remote(here, here, oy_s.at[o], oy_r.at[o], dp, sib).wait_recv()
    for o in range(1, NZ):
        oz_copy(o).start()
    orecv[:, z] = omid[:, z]

    shape = (128, 128)
    gap = (iota(shape, 0) - iota(shape, 1)) & 15
    hist = htot_s[...]
    rows = [
        jnp.sum(jnp.where(gap == b, hist, 0.0), axis=0, keepdims=True) for b in range(LEVELS - 1)
    ]
    total = jnp.sum(tot_s[...], axis=0, keepdims=True)
    total = sum(total[:, i : i + 128] for i in range(0, PAIR, 128))
    rows.append(total - sum(rows))
    levels = jnp.sum(jnp.concatenate(rows, axis=0), axis=1, keepdims=True)
    levels = sbias_s[...] + jnp.where(level_lane == chip, levels, 0.0)
    levels = jnp.concatenate([levels, jnp.zeros((128 - LEVELS, 128), F32)], axis=0)
    b_send[...] = jnp.transpose(levels)[0:8, :]

    def b2_copy(o):
        return remote(
            b_send, b_ctx.at[ctx], b2_s.at[o], b2_r.at[o], dp, lax.rem(ctx + o, 2 * CHIPS)
        )

    def start_b2(o, carry):
        b2_copy(o).start()
        return carry

    lax.fori_loop(1, 2 * CHIPS, start_b2, 0)
    b_ctx[ctx] = b_send[...]

    def finish(step, carry):
        qs = CHIPS - 1 - step
        sib_copy(qs).wait_recv()
        mine = rows_at(qs, ROWS)
        block = rows_at(2 * qs + core, ROWS)
        dk = (dk_s[block, :] + sib_recv[qs, :, 0:HEAD].astype(F32)) * SCALE
        dv = dv_s[block, :] + sib_recv[qs, :, HEAD : 2 * HEAD].astype(F32)
        grad_all[mine, HEAD : 2 * HEAD] = (
            dv * p_s[qs, :, HEAD : 2 * HEAD]
        ).astype(BF)
        grad_all[mine, 3 * HEAD : 4 * HEAD] = (
            dk * p_s[qs, :, 3 * HEAD : 4 * HEAD]
        ).astype(BF)

        @pl.when(qs != chip)
        def _():
            g_copy(1, qs).start()
            g_copy(3, qs).start()

        return carry

    lax.fori_loop(0, CHIPS, finish, 0)

    for d in (1, 3, 2):
        src = lax.rem(chip + CHIPS - d, CHIPS)
        there = pl.ds(pl.multiple_of(LONG_ROWS + src * SHORT, SHORT), SHORT)
        remote(stok, tok_all.at[there, :], st_s.at[d], st_r.at[d], dp, sib).wait_recv()
        remote(sgrad_s.at[src], grad_all.at[there, :], sg_s.at[d], sg_r.at[d], dp, sib).wait_recv()

    half_dp = n_dp // 2
    half_model = MODEL // 2
    my_half = lax.div(dp, half_dp)
    halves = (my_half, 1 - my_half)

    def outer(pair, half):
        cols = pl.ds(pl.multiple_of(pair * 2 * HEAD, 2 * HEAD), 2 * HEAD)
        rows = pl.ds(pl.multiple_of(half * half_model, half_model), half_model)
        return dot_tn(tok_all[:, rows], grad_all[:, cols])

    def swap(j):
        return remote(half_send.at[j], half_recv.at[j], p_ss.at[j], p_sr.at[j], dp, sib)

    def ry_copy(o):
        return remote(
            rs_send.at[y ^ o], rs_mid.at[y], ry_s.at[o], ry_r.at[o], (y ^ o) * NZ + z, ctx
        )

    def rz_copy(o):
        peer = lax.rem(z + o, NZ)
        return remote(
            rs_sum.at[peer], rs_fin.at[z], rz_s.at[o], rz_r.at[o], y * NZ + peer, ctx
        )

    for j in range(2):
        half_send[j] = outer(1 - core, halves[j]).astype(BF)
        swap(j).start()
    for j in range(2):
        own[...] = outer(core, halves[j])
        swap(j).wait_recv()
        total = (own[...] + half_recv[j].astype(F32)).astype(BF)
        rs_send[pl.ds(halves[j] * (ny // 2), ny // 2)] = total.reshape(
            (ny // 2,) + rs_send.shape[1:]
        )
        for o in ((1,), (2, 3))[j]:
            ry_copy(o).start()

    def wait_b2(o, carry):
        src = lax.rem(ctx + 2 * CHIPS - o, 2 * CHIPS)
        remote(b_send, b_ctx.at[src], b2_s.at[o], b2_r.at[o], dp, src).wait_recv()
        return carry

    lax.fori_loop(1, 2 * CHIPS, wait_b2, 0)
    b_mid[...] = jnp.sum(b_ctx[...], axis=0)
    one_start(b_mid, b_dp, b1_s, b1_r)
    b_dp[dp] = b_mid[...]

    def write(source, target, index):
        return pltpu.make_async_copy(source, target, out_sem.at[index])

    for o in range(1, NZ):
        here = orecv.at[:, lax.rem(z + NZ - o, NZ)]
        remote(here, here, oz_s.at[o], oz_r.at[o], dp, sib).wait_recv()
    so_v[...] = dot_tn(place_s[...], orecv[...].reshape(n_dp * SLEN, BLOCK)).astype(BF)
    write(so_v, short_out, 1).start()
    total = dot_nt(sgrad_s[0], wh[0])
    for h in range(1, 4):
        total = total + dot_nt(sgrad_s[h], wh[h])
    sg_v[...] = total.astype(BF)
    write(sg_v, short_grad, 3).start()

    total = rs_send[y].astype(F32)
    for o in range(1, ny):
        here = rs_mid.at[y ^ o]
        remote(here, here, ry_s.at[o], ry_r.at[o], dp, sib).wait_recv()
        total = total + rs_mid[y ^ o].astype(F32)
    rs_sum[...] = total.astype(BF)
    for o in range(1, NZ):
        rz_copy(o).start()

    lo_v[:, lanes_at(chip)] = out_s[chip]
    grad_h[chip] = grad_all[rows_at(chip, ROWS), :]
    total = dot_nt(grad_h[chip], wh[chip])
    for d in (1, 3, 2):
        src = lax.rem(chip + CHIPS - d, CHIPS)
        for k in range(4):
            here = grad_h.at[src, :, k * HEAD : (k + 1) * HEAD]
            remote(here, here, g_s.at[k, src], g_r.at[k, src], dp, sib).wait_recv()
        here = lo_v.at[:, lanes_at(src)]
        remote(out_s.at[src], here, l_s.at[src], l_r.at[src], dp, sib).wait_recv()
        total = total + dot_nt(grad_h[src], wh[src])
    tg_v[...] = total.astype(BF)
    write(tg_v, token_grad, 2).start()
    write(lo_v, long_out, 0).start()

    half_copy(up, 0, 0).wait_send()
    half_copy(up, 1, 0).wait_send()
    half_copy(down, 0, 1).wait_send()
    half_copy(down, 1, 1).wait_send()
    pass_copy(down, 0, up).wait_send()
    pass_copy(up, 1, down).wait_send()
    for d in (1, 3, 2):
        c_copy(d).wait_send()
        st_copy(d).wait_send()
        sg_copy(d).wait_send()
    one_all(dest_g, d_s, d_r).wait_send()
    dp_all(cbuf, crecv, s_s, s_r).wait_send()
    for o in range(1, ny):
        oy_copy(o).wait_send()
        ry_copy(o).wait_send()
    for o in range(1, NZ):
        oz_copy(o).wait_send()

    def ended_o(o, carry):
        t_copy(o).wait_send()
        b2_copy(o).wait_send()
        return carry

    lax.fori_loop(1, 2 * CHIPS, ended_o, 0)

    def ended_q(qs, carry):
        kv_copy(qs).wait_send()
        sib_copy(qs).wait_send()
        for d in (1, 3, 2):
            stat_copy(qs, d).wait_send()

        @pl.when(qs != chip)
        def _():
            l_copy(qs).wait_send()
            for k in range(4):
                g_copy(k, qs).wait_send()

        return carry

    lax.fori_loop(0, CHIPS, ended_q, 0)
    for j in range(2):
        swap(j).wait_send()

    total = rs_sum[z].astype(F32)
    for o in range(1, NZ):
        src = lax.rem(z + NZ - o, NZ)
        here = rs_fin.at[src]
        remote(here, here, rz_s.at[o], rz_r.at[o], dp, sib).wait_recv()
        total = total + rs_fin[src].astype(F32)
    piece[...] = total
    mine = lax.rem(chip, 2)

    def f_copy(i):
        target = 2 * (2 * core + i) + lax.div(chip, 2)
        return target, remote(
            piece.at[:, i * HEAD : (i + 1) * HEAD],
            proj_grad.at[:, lanes_at(mine)],
            f_s.at[i],
            f_r.at[mine],
            dp,
            target,
        )

    for i in range(2):
        target, copy = f_copy(i)

        @pl.when(target != ctx)
        def _():
            copy.start()

        @pl.when(target == ctx)
        def _():
            proj_grad[:, lanes_at(mine)] = piece[:, i * HEAD : (i + 1) * HEAD]

    one_all(b_dp, b1_s, b1_r).wait_recv()
    bias_out[...] = jnp.sum(b_dp[...], axis=0)[0:4, 0:LEVELS]

    for half in range(2):
        source = 2 * (2 * core + half) + lax.div(chip, 2)

        @pl.when(source != ctx)
        def _():
            remote(
                piece.at[:, 0:HEAD],
                proj_grad.at[:, half * HEAD : (half + 1) * HEAD],
                f_s.at[half],
                f_r.at[half],
                dp,
                source,
            ).wait_recv()

    for i in range(2):
        target, copy = f_copy(i)

        @pl.when(target != ctx)
        def _():
            copy.wait_send()

    for o in range(1, NZ):
        rz_copy(o).wait_send()
    one_all(b_dp, b1_s, b1_r).wait_send()
    write(lo_v, long_out, 0).wait()
    write(so_v, short_out, 1).wait()
    write(tg_v, token_grad, 2).wait()
    write(sg_v, short_grad, 3).wait()


def output_kernel(count, *refs):
    for i in range(count):
        refs[count + i][...] = refs[i][...]


VM = pl.BlockSpec(memory_space=pltpu.VMEM)
SM = pl.BlockSpec(memory_space=pltpu.SMEM)
ANY = pl.BlockSpec(memory_space=pl.ANY)
DMA = pltpu.SemaphoreType.DMA
VMEM = pltpu.VMEM


def shaped(shape, dtype):
    return jax.ShapeDtypeStruct(shape, dtype)


def per_device(
    n_dp,
    long_tokens,
    short_tokens,
    projection,
    time_bias,
    long_length,
    short_length,
    long_time,
    short_time,
    destination,
    long_cotangent,
    short_cotangent,
):
    part = MODEL // n_dp
    ny = n_dp // NZ
    spread = (n_dp, SLEN, BLOCK)
    scratch = [
        VMEM((CHIPS, MODEL, BLOCK), BF),
        VMEM((ALL_ROWS, MODEL), BF),
        VMEM((ALL_ROWS, BLOCK), BF),
        VMEM((CHIPS, ROWS, BLOCK), F32),
        VMEM((CHIPS, ROWS, BLOCK), BF),
        VMEM((2 * CHIPS * ROWS, 2 * HEAD), BF),
        VMEM((CHIPS, ROWS, HEAD), BF),
        VMEM((8, ROWS), jnp.int32),
        VMEM((2 * CHIPS, 8, ROWS), jnp.int32),
        VMEM((8, 128), F32),
        VMEM((8, 128), jnp.int32),
        VMEM((8, 128), jnp.int32),
        VMEM((n_dp, 8, 128), jnp.int32),
        VMEM((n_dp * SLEN, 128), BF),
        VMEM(spread, BF),
        VMEM(spread, BF),
        VMEM((4, SHORT, BLOCK), F32),
        VMEM((4, SHORT, BLOCK), BF),
        VMEM((4, SHORT, SHORT), BF),
        VMEM((4, SHORT, SHORT), F32),
        VMEM((4, SHORT, HEAD), F32),
        VMEM((SHORT, 128), F32),
        VMEM((SHORT, BLOCK), F32),
        VMEM((4, SHORT, BLOCK), BF),
        VMEM((ny, NZ, SLEN, BLOCK), BF),
        VMEM((ny, NZ, SLEN, BLOCK), BF),
        VMEM((ny, NZ, SLEN, BLOCK), BF),
        VMEM((LEVELS, 128), F32),
        VMEM((CHIPS, CHIPS, ROWS, PAIR), BF),
        VMEM((CHIPS, CHIPS, ROWS, PAIR), F32),
        VMEM((CHIPS, ROWS, HEAD), F32),
        VMEM((CHIPS, ROWS, HEAD), BF),
        VMEM((2 * CHIPS * ROWS, 128), BF),
        VMEM((2 * CHIPS, ROWS, 128), F32),
        VMEM((CHIPS, CHIPS, 8, ROWS), F32),
        VMEM((2 * CHIPS * ROWS, HEAD), F32),
        VMEM((2 * CHIPS * ROWS, HEAD), F32),
        VMEM((ROWS, HEAD), F32),
        VMEM((ROWS, 128), F32),
        VMEM((128, 128), F32),
        VMEM((8, PAIR), F32),
        VMEM((CHIPS, ROWS, 2 * HEAD), BF),
        VMEM((CHIPS, ROWS, 2 * HEAD), BF),
        VMEM((CHIPS, ROWS, BLOCK), BF),
        VMEM((2, MODEL // 2, 2 * HEAD), BF),
        VMEM((2, MODEL // 2, 2 * HEAD), BF),
        VMEM((MODEL // 2, 2 * HEAD), F32),
        VMEM((ny, NZ, part, 2 * HEAD), BF),
        VMEM((ny, NZ, part, 2 * HEAD), BF),
        VMEM((NZ, part, 2 * HEAD), BF),
        VMEM((NZ, part, 2 * HEAD), BF),
        VMEM((8, 128), F32),
        VMEM((n_dp, 8, 128), F32),
        VMEM((8, 128), F32),
        VMEM((2 * CHIPS, 8, 128), F32),
        VMEM((part, 2 * HEAD), F32),
        VMEM((ROWS, BLOCK), BF),
        VMEM((SHORT, BLOCK), BF),
        VMEM((ROWS, MODEL), BF),
        VMEM((SHORT, MODEL), BF),
        DMA((4, 4)),
        DMA((3,)),
        DMA((4,)),
        DMA((2, 2)),
        DMA((2, 2)),
        DMA((2,)),
        DMA((2,)),
        DMA((CHIPS,)),
        DMA((CHIPS,)),
        DMA((2 * CHIPS,)),
        DMA((2 * CHIPS,)),
        DMA((CHIPS,)),
        DMA((CHIPS,)),
        DMA((CHIPS,)),
        DMA((CHIPS,)),
        DMA((CHIPS,)),
        DMA((CHIPS,)),
        DMA,
        DMA,
        DMA,
        DMA,
        DMA((ny,)),
        DMA((ny,)),
        DMA((NZ,)),
        DMA((NZ,)),
        DMA((CHIPS, CHIPS)),
        DMA((CHIPS, CHIPS)),
        DMA((CHIPS,)),
        DMA((CHIPS,)),
        DMA((4, CHIPS)),
        DMA((4, CHIPS)),
        DMA((CHIPS,)),
        DMA((CHIPS,)),
        DMA((2,)),
        DMA((2,)),
        DMA((ny,)),
        DMA((ny,)),
        DMA((NZ,)),
        DMA((NZ,)),
        DMA,
        DMA,
        DMA((2 * CHIPS,)),
        DMA((2 * CHIPS,)),
        DMA((2,)),
        DMA((2,)),
    ]
    results = pl.pallas_call(
        functools.partial(layer_kernel, n_dp),
        out_shape=(
            shaped((ROWS, BLOCK), BF),
            shaped((SHORT, BLOCK), BF),
            shaped((ROWS, MODEL), BF),
            shaped((SHORT, MODEL), BF),
            shaped((part, 2 * HEAD), F32),
            shaped(time_bias.shape, F32),
        ),
        in_specs=[ANY, ANY, ANY, ANY, VM, VM, VM, VM, VM, SM, VM],
        out_specs=(ANY,) * 4 + (VM,) * 2,
        scratch_shapes=scratch,
        compiler_params=pltpu.CompilerParams(
            vmem_limit_bytes=VMEM_LIMIT, collective_id=0, has_side_effects=True
        ),
        name="layer",
    )(
        long_tokens[0],
        short_tokens.reshape(SHORT, MODEL),
        projection,
        long_cotangent[0],
        short_cotangent.reshape(SHORT, BLOCK),
        long_time,
        short_time,
        short_length,
        destination,
        long_length,
        time_bias,
    )
    results = pl.pallas_call(
        functools.partial(output_kernel, len(results)),
        out_shape=tuple(shaped(r.shape, r.dtype) for r in results),
        in_specs=[VM] * len(results),
        out_specs=(VM,) * len(results),
        compiler_params=pltpu.CompilerParams(vmem_limit_bytes=VMEM_LIMIT),
        name="output",
    )(*results)
    long_out, short_out, token_grad, short_grad, proj_grad, bias_out = results
    return (
        long_out[None],
        short_out.reshape(short_cotangent.shape),
        token_grad[None],
        short_grad.reshape(short_tokens.shape),
        proj_grad,
        bias_out,
    )


def solution(mesh):
    return jax.shard_map(
        functools.partial(per_device, mesh.shape["dp"]),
        mesh=mesh,
        in_specs=(
            P("dp", "ctx", None),
            P("dp", "ctx", None, None),
            P(),
            P(),
            P("dp"),
            P("dp", "ctx"),
            P("dp", "ctx"),
            P("dp", "ctx", None),
            P("dp", "ctx"),
            P("dp", "ctx", None),
            P("dp", "ctx", None, None),
        ),
        out_specs=(
            P("dp", "ctx", None),
            P("dp", "ctx", None, None),
            P("dp", "ctx", None),
            P("dp", "ctx", None, None),
            P("dp", "ctx"),
            P(),
        ),
        check_vma=False,
    )
```

```python
import functools

import jax
import jax.numpy as jnp
from jax import lax
from jax.experimental import pallas as pl
from jax.experimental.pallas import tpu as pltpu
from jax.sharding import PartitionSpec as P

epsilon = 1e-05
MESH = pl.DeviceIdType.MESH
BF = jnp.bfloat16
F32 = jnp.float32
CHIPS = 4
NZ = 8
ROWS = 256
HEAD = 128
LEVELS = 16
SLEN = 16
SHORT = 128
LONG_ROWS = CHIPS * ROWS
ALL_ROWS = CHIPS * (ROWS + SHORT)
PAIR = 2 * ROWS
MODEL = 1024
BLOCK = 512
SCALE = HEAD ** (-0.5)
VMEM_LIMIT = 56 * 1024 * 1024


def sigmoid(value):
    return 0.5 * jnp.tanh(0.5 * value) + 0.5


def silu_and_grad(value):
    sigma = sigmoid(value)
    silu = value * sigma
    return silu.astype(BF), sigma + silu * (1.0 - sigma)


def dot_nn(a, b):
    return jnp.dot(a, b, preferred_element_type=F32)


def dot_nt(a, b):
    return lax.dot_general(a, b, (((1,), (1,)), ((), ())), preferred_element_type=F32)


def dot_tn(a, b):
    return lax.dot_general(a, b, (((0,), (0,)), ((), ())), preferred_element_type=F32)


def column_of(row):
    return jnp.transpose(jnp.broadcast_to(row, (128, 128)))


def iota(shape, axis):
    return lax.broadcasted_iota(jnp.int32, shape, axis)


def remote(src, dst, send_sem, recv_sem, dp, ctx):
    return pltpu.make_async_remote_copy(
        src_ref=src,
        dst_ref=dst,
        send_sem=send_sem,
        recv_sem=recv_sem,
        device_id=(dp, ctx),
        device_id_type=MESH,
    )


def place():
    dp = lax.axis_index("dp")
    ctx = lax.axis_index("ctx")
    return dp, ctx, lax.div(ctx, 2), lax.rem(ctx, 2)


def lookup(table, diff):
    index = jnp.clip(diff, 0.0, LEVELS - 1.0).astype(jnp.int32)
    parts = [
        jnp.take_along_axis(table, index[:, i : i + 128], axis=1)
        for i in range(0, index.shape[1], 128)
    ]
    return parts[0] if len(parts) == 1 else jnp.concatenate(parts, axis=1)


def exact_dot(a, b):
    return lax.dot_general(
        a,
        b,
        (((1,), (0,)), ((), ())),
        precision=lax.Precision.HIGHEST,
        preferred_element_type=F32,
    )


def rows_at(block, rows):
    return pl.ds(pl.multiple_of(block * rows, rows), rows)


def lanes_at(block):
    return pl.ds(pl.multiple_of(block * HEAD, HEAD), HEAD)


def layer_kernel(
    n_dp,
    tok,
    stok,
    w,
    lcot,
    scot,
    ltime,
    stime,
    slen,
    dest_in,
    llen,
    tbias,
    long_out,
    short_out,
    token_grad,
    short_grad,
    proj_grad,
    bias_out,
    wh,
    tok_all,
    grad_all,
    p_s,
    act_s,
    kv,
    c_g,
    tmeta,
    times,
    tab_s,
    ints,
    dtile,
    dest_g,
    place_s,
    cbuf,
    crecv,
    sp_s,
    sact_s,
    sweight_s,
    sslope_s,
    snorm_s,
    sscale_s,
    c_home,
    sgrad_s,
    obuf,
    omid,
    orecv,
    sbias_s,
    weight_s,
    slope_s,
    mixed_s,
    out_s,
    hot_s,
    tcol_s,
    stat_s,
    dk_s,
    dv_s,
    dq_s,
    hist_s,
    htot_s,
    tot_s,
    sib_send,
    sib_recv,
    grad_h,
    half_send,
    half_recv,
    own,
    rs_send,
    rs_mid,
    rs_sum,
    rs_fin,
    b_send,
    b_dp,
    b_mid,
    b_ctx,
    piece,
    lo_v,
    so_v,
    tg_v,
    sg_v,
    w_sem,
    in_sem,
    out_sem,
    tok_s,
    tok_r,
    fwd_s,
    fwd_r,
    c_s,
    c_r,
    t_s,
    t_r,
    kv_s,
    kv_r,
    st_s,
    st_r,
    sg_s,
    sg_r,
    d_s,
    d_r,
    s_s,
    s_r,
    oy_s,
    oy_r,
    oz_s,
    oz_r,
    stat_ss,
    stat_sr,
    sib_s,
    sib_r,
    g_s,
    g_r,
    l_s,
    l_r,
    p_ss,
    p_sr,
    ry_s,
    ry_r,
    rz_s,
    rz_r,
    b1_s,
    b1_r,
    b2_s,
    b2_r,
    f_s,
    f_r,
):
    dp, ctx, chip, core = place()
    sib = ctx + 1 - 2 * core
    up = lax.rem(chip + 1, CHIPS)
    down = lax.rem(chip + CHIPS - 1, CHIPS)
    far = lax.rem(chip + 2, CHIPS)
    half_rows = ROWS // 2
    ny = n_dp // NZ
    y, z = lax.div(dp, NZ), lax.rem(dp, NZ)
    barrier = pltpu.get_barrier_semaphore()

    def greet_ctx(o, carry):
        pl.semaphore_signal(
            barrier, inc=1, device_id=(dp, lax.rem(ctx + o, 2 * CHIPS)), device_id_type=MESH
        )
        return carry

    def greet_dp(o, carry):
        pl.semaphore_signal(
            barrier, inc=1, device_id=(lax.rem(dp + o, n_dp), ctx), device_id_type=MESH
        )
        return carry

    lax.fori_loop(1, 2 * CHIPS, greet_ctx, 0)
    lax.fori_loop(1, n_dp, greet_dp, 0)

    def w_copy(h, k):
        return pltpu.make_async_copy(
            w.at[:, k * BLOCK + h * HEAD : k * BLOCK + (h + 1) * HEAD],
            wh.at[h, :, k * HEAD : (k + 1) * HEAD],
            w_sem.at[h, k],
        )

    for h in range(4):
        for k in range(4):
            w_copy(h, k).start()
    tmeta[...] = jnp.broadcast_to(ltime[...], (8, ROWS))
    ints[...] = jnp.zeros((8, 128), jnp.int32) - 1
    ints[0:1, 0:8] = slen[...]
    ints[1:2, 0:8] = dest_in[...]
    dtile[...] = jnp.broadcast_to(ints[1:2, :], (8, 128))
    tab_s[...] = jnp.zeros_like(tab_s)
    tab_s[0:4, 0:LEVELS] = tbias[...]

    def half_copy(peer, half, index):
        return remote(
            tok.at[half * half_rows : (half + 1) * half_rows, :],
            tok_all.at[rows_at(2 * chip + half, half_rows), :],
            tok_s.at[index, half],
            tok_r.at[index, half],
            dp,
            2 * peer + core,
        )

    def half_wait(src, half, index):
        here = tok_all.at[rows_at(2 * src + half, half_rows), :]
        remote(here, here, tok_s.at[index, half], tok_r.at[index, half], dp, sib).wait_recv()

    def pass_copy(src, half, peer):
        here = tok_all.at[rows_at(2 * src + half, half_rows), :]
        return remote(here, here, fwd_s.at[half], fwd_r.at[half], dp, 2 * peer + core)

    def c_copy(d):
        peer = lax.rem(chip + d, CHIPS)
        return remote(
            lcot.at[:, lanes_at(peer)], c_g.at[chip], c_s.at[d], c_r.at[d], dp, 2 * peer + core
        )

    def t_copy(o):
        return remote(
            tmeta, times.at[ctx], t_s.at[o], t_r.at[o], dp, lax.rem(ctx + o, 2 * CHIPS)
        )

    def kv_copy(src):
        here = kv.at[rows_at(2 * src + core, ROWS), :]
        return remote(here, here, kv_s.at[src], kv_r.at[src], dp, sib)

    def kv_wait(src):
        here = kv.at[rows_at(2 * src + 1 - core, ROWS), :]
        remote(here, here, kv_s.at[src], kv_r.at[src], dp, sib).wait_recv()

    def st_copy(d):
        return remote(
            stok,
            tok_all.at[pl.ds(pl.multiple_of(LONG_ROWS + chip * SHORT, SHORT), SHORT), :],
            st_s.at[d],
            st_r.at[d],
            dp,
            2 * lax.rem(chip + d, CHIPS) + core,
        )

    def sg_copy(d):
        peer = lax.rem(chip + d, CHIPS)
        return remote(
            sgrad_s.at[peer],
            grad_all.at[pl.ds(pl.multiple_of(LONG_ROWS + chip * SHORT, SHORT), SHORT), :],
            sg_s.at[d],
            sg_r.at[d],
            dp,
            2 * peer + core,
        )

    def dp_start(source, target, send, recv):
        def one(o, carry):
            peer = lax.rem(dp + o, n_dp)
            remote(source.at[peer], target.at[dp], send, recv, peer, ctx).start()
            return carry

        lax.fori_loop(1, n_dp, one, 0)

    def dp_all(source, target, send, recv):
        return remote(
            source.at[0 : n_dp - 1], target.at[0 : n_dp - 1], send, recv, dp, sib
        )

    def one_start(source, target, send, recv):
        def one(o, carry):
            remote(source, target.at[dp], send, recv, lax.rem(dp + o, n_dp), ctx).start()
            return carry

        lax.fori_loop(1, n_dp, one, 0)

    def one_all(target, send, recv):
        here = target.at[0 : n_dp - 1]
        return remote(here, here, send, recv, dp, sib)

    home_rows = pl.ds(pl.multiple_of(LONG_ROWS + chip * SHORT, SHORT), SHORT)
    loads = [
        pltpu.make_async_copy(tok, tok_all.at[rows_at(chip, ROWS), :], in_sem.at[0]),
        pltpu.make_async_copy(stok, tok_all.at[home_rows, :], in_sem.at[1]),
        pltpu.make_async_copy(lcot.at[:, lanes_at(chip)], c_g.at[chip], in_sem.at[2]),
    ]
    for load in loads:
        load.start()
    pl.semaphore_wait(barrier, n_dp - 1 + 2 * CHIPS - 1)
    half_copy(up, 0, 0).start()
    half_copy(down, 1, 1).start()
    half_copy(up, 1, 0).start()
    half_copy(down, 0, 1).start()
    one_start(dtile, dest_g, d_s, d_r)

    def start_t(o, carry):
        t_copy(o).start()
        return carry

    lax.fori_loop(1, 2 * CHIPS, start_t, 0)
    times[ctx] = tmeta[...]
    dest_g[dp] = dtile[...]
    for h in range(4):
        for k in range(4):
            w_copy(h, k).wait()
    for load in loads:
        load.wait()

    def project(src):
        projected = dot_nn(tok_all[rows_at(src, ROWS), :], wh[chip])
        act, p_s[src] = silu_and_grad(projected)
        act_s[src] = act
        kv[rows_at(2 * src + core, ROWS), 0:HEAD] = act[:, 3 * HEAD : 4 * HEAD]
        kv[rows_at(2 * src + core, ROWS), HEAD : 2 * HEAD] = act[:, HEAD : 2 * HEAD]
        kv_copy(src).start()

    project(chip)

    lane16 = iota((16, 128), 1)
    spread_time = exact_dot(
        stime[0].astype(F32), jnp.where((lane16 & 15) == iota((16, 128), 0), 1.0, 0.0)
    )
    pick = (iota((8, 128), 1) >> 4) == iota((8, 128), 0)
    stime_row = jnp.sum(jnp.where(pick, spread_time, 0.0), axis=0, keepdims=True)
    repeat = jnp.where((iota((128, 128), 1) >> 4) == iota((128, 128), 0), 1.0, 0.0)
    rep_rows = exact_dot(ints[...].astype(F32), repeat)
    slen_row, home_row = rep_rows[0:1, :], rep_rows[1:2, :]
    owner_row = (home_row.astype(jnp.int32) >> 3).astype(F32)
    shape = (SHORT, SHORT)
    row = iota(shape, 0)
    col = iota(shape, 1)
    stime_diff = column_of(stime_row) - stime_row
    inside = (row & 15).astype(F32) < column_of(slen_row)
    svisible = ((row >> 4) == (col >> 4)) & (col <= row) & inside

    short_tokens = tok_all[home_rows, :]
    mixes = []
    for h in range(4):
        act, sp_s[h] = silu_and_grad(dot_nn(short_tokens, wh[h]))
        sact_s[h] = act
        queries, keys = act[:, 2 * HEAD : 3 * HEAD], act[:, 3 * HEAD : 4 * HEAD]
        tab = jnp.broadcast_to(tab_s[h : h + 1, :], (SHORT, 128))
        total = dot_nt(queries, keys) * SCALE + lookup(tab, stime_diff)
        sg = sigmoid(total)
        weight = total * sg
        weight16 = jnp.where(svisible, weight, 0.0).astype(BF)
        sweight_s[h] = weight16
        sslope_s[h] = jnp.where(svisible, sg + weight * (1.0 - sg), 0.0)
        mixes.append(dot_nn(weight16, act[:, HEAD : 2 * HEAD]))
    mean = sum(jnp.sum(m, axis=1, keepdims=True) for m in mixes) * (1.0 / BLOCK)
    centred = [m - mean for m in mixes]
    spread = sum(jnp.sum(m * m, axis=1, keepdims=True) for m in centred) * (1.0 / BLOCK)
    scale = lax.rsqrt(spread + epsilon)
    sscale_s[...] = jnp.broadcast_to(scale, sscale_s.shape)
    for h in range(4):
        snorm_s[h] = centred[h] * scale

    one_all(dest_g, d_s, d_r).wait_recv()
    dest = dest_g[...]
    code = jnp.sum(
        jnp.where((dest >> 3) == dp, ((dest & 7) + 1).astype(F32), 0.0), axis=2, keepdims=True
    )
    code = jnp.broadcast_to(code, (n_dp, 8, 128))
    code = jnp.concatenate([code, code], axis=1).reshape(n_dp * SLEN, 128)
    shape = (n_dp * SLEN, 128)
    same = (iota(shape, 0) & 15) == (iota(shape, 1) & 15)
    slot = ((iota(shape, 1) >> 4) + 1).astype(F32)
    placer = jnp.where(same & (code == slot), 1.0, 0.0).astype(BF)
    place_s[...] = placer
    cbuf[...] = dot_nn(placer, scot[...]).astype(BF).reshape(cbuf.shape)
    dp_start(cbuf, crecv, s_s, s_r)
    crecv[dp] = cbuf[dp]

    half_wait(down, 0, 0)
    pass_copy(down, 0, up).start()
    half_wait(up, 1, 1)
    pass_copy(up, 1, down).start()
    for d in (1, 3, 2):
        c_copy(d).start()

    def wait_t(o, carry):
        src = lax.rem(ctx + 2 * CHIPS - o, 2 * CHIPS)
        remote(tmeta, times.at[src], t_s.at[o], t_r.at[o], dp, src).wait_recv()
        return carry

    lax.fori_loop(1, 2 * CHIPS, wait_t, 0)
    lane = iota((ROWS, 128), 1)

    def times_of(b, carry):
        line = times[b, 0:1, :].astype(F32)
        column = jnp.concatenate(
            [column_of(line[:, 0:128]), column_of(line[:, 128:256])], axis=0
        )
        tcol_s[b] = column
        hot_s[rows_at(b, ROWS), :] = jnp.where(
            (column.astype(jnp.int32) & 15) == lane, 1.0, 0.0
        ).astype(BF)
        return carry

    lax.fori_loop(0, 2 * CHIPS, times_of, 0)
    dk_s[...] = jnp.zeros_like(dk_s)
    dv_s[...] = jnp.zeros_like(dv_s)
    htot_s[...] = jnp.zeros_like(htot_s)
    tot_s[...] = jnp.zeros_like(tot_s)
    mixed_s[...] = jnp.zeros_like(mixed_s)

    half_wait(down, 1, 0)
    project(down)
    half_wait(up, 0, 1)
    project(up)

    table = jnp.broadcast_to(tab_s[pl.ds(chip, 1), :], (ROWS, 128))
    length = llen[0]

    def key_times(p):
        return jnp.concatenate(
            [times[2 * p, 0:1, :], times[2 * p + 1, 0:1, :]], axis=1
        ).astype(F32)

    def forward_tile(qs, p):
        block = 2 * qs + core
        queries = act_s[qs, :, 2 * HEAD : 3 * HEAD]
        tq = tcol_s[block][:, 0:1]
        spot = iota((ROWS, 1), 0) + block * ROWS
        limit = jnp.where(spot < length, spot, -1)
        keys = kv[rows_at(p, PAIR), 0:HEAD]
        values = kv[rows_at(p, PAIR), HEAD : 2 * HEAD]
        total = dot_nt(queries, keys) * SCALE + lookup(table, tq - key_times(p))
        sg = sigmoid(total)
        weight = total * sg
        visible = (iota((ROWS, PAIR), 1) + p * PAIR) <= limit
        weight16 = jnp.where(visible, weight, 0.0).astype(BF)
        weight_s[qs, p] = weight16
        slope_s[qs, p] = jnp.where(visible, sg + weight * (1.0 - sg), 0.0)
        mixed_s[qs] += dot_nn(weight16, values)

    for d in (0, 1, 3):
        kv_wait(lax.rem(chip + CHIPS - d, CHIPS))

    def near_block(step, carry):
        qs = CHIPS - 1 - step

        def one(p, carry):
            @pl.when(p != far)
            def _():
                forward_tile(qs, p)

            return carry

        lax.fori_loop(0, jnp.where(qs == far, 0, qs + 1), one, 0)
        return carry

    lax.fori_loop(0, CHIPS, near_block, 0)

    for half in range(2):
        here = tok_all.at[rows_at(2 * far + half, half_rows), :]
        remote(here, here, fwd_s.at[half], fwd_r.at[half], dp, sib).wait_recv()
    project(far)
    for d in (1, 3, 2):
        st_copy(d).start()
    for d in (1, 3, 2):
        src = lax.rem(chip + CHIPS - d, CHIPS)
        remote(c_g.at[src], c_g.at[src], c_s.at[d], c_r.at[d], dp, sib).wait_recv()
    kv_wait(far)

    def stat_copy(qs, d):
        here = stat_s.at[qs, chip]
        return remote(
            here,
            here,
            stat_ss.at[qs, d],
            stat_sr.at[qs, d],
            dp,
            2 * lax.rem(chip + d, CHIPS) + core,
        )

    def far_block(step, carry):
        qs = CHIPS - 1 - step

        def one(p, carry):
            forward_tile(qs, p)
            return carry

        first = jnp.where(qs == far, 0, far)
        last = jnp.where(qs >= far, jnp.where(qs == far, qs, far) + 1, first)
        lax.fori_loop(first, last, one, 0)
        mixed = mixed_s[qs]
        q = c_g[qs].astype(F32) * act_s[qs, :, 0:HEAD].astype(F32)
        s1 = jnp.sum(mixed, axis=1, keepdims=True)
        centred = mixed - s1 * (1.0 / HEAD)
        s2 = jnp.sum(centred * centred, axis=1, keepdims=True)
        s3 = jnp.sum(q, axis=1, keepdims=True)
        s4 = jnp.sum(q * centred, axis=1, keepdims=True)
        stats = jnp.where(
            lane == 0, s1, jnp.where(lane == 1, s2, jnp.where(lane == 2, s3, s4))
        )
        stat_s[qs, chip] = jnp.transpose(stats)[0:8, :]
        for d in (1, 3, 2):
            stat_copy(qs, d).start()
        return carry

    lax.fori_loop(0, CHIPS, far_block, 0)

    dp_all(cbuf, crecv, s_s, s_r).wait_recv()
    owner = jnp.concatenate([column_of(owner_row)] * (n_dp * SLEN // 128), axis=1)
    shape = (SHORT, n_dp * SLEN)
    same = (iota(shape, 0) & 15) == (iota(shape, 1) & 15)
    chooser = jnp.where(
        same & (owner == (iota(shape, 1) >> 4).astype(F32)), 1.0, 0.0
    ).astype(BF)
    c_home[...] = dot_nn(chooser, crecv[...].reshape(n_dp * SLEN, BLOCK))
    scale = sscale_s[:, 0:1]
    mean_q = jnp.zeros((SHORT, 1), F32)
    mean_qn = jnp.zeros((SHORT, 1), F32)
    for h in range(4):
        q = c_home[:, h * HEAD : (h + 1) * HEAD] * sact_s[h, :, 0:HEAD].astype(F32)
        mean_q = mean_q + jnp.sum(q, axis=1, keepdims=True)
        mean_qn = mean_qn + jnp.sum(q * snorm_s[h], axis=1, keepdims=True)
    mean_q = mean_q * (1.0 / BLOCK)
    mean_qn = mean_qn * (1.0 / BLOCK)
    bucket = jnp.clip(stime_diff, 0.0, LEVELS - 1.0).astype(jnp.int32)
    level_lane = iota((LEVELS, 128), 1)
    sums = jnp.zeros((LEVELS, 128), F32)
    outs = []
    for h in range(4):
        act = sact_s[h]
        gates = act[:, 0:HEAD].astype(F32)
        values = act[:, HEAD : 2 * HEAD]
        queries = act[:, 2 * HEAD : 3 * HEAD]
        keys = act[:, 3 * HEAD : 4 * HEAD]
        normed = snorm_s[h]
        cot = c_home[:, h * HEAD : (h + 1) * HEAD]
        outs.append((normed * gates).astype(BF))
        mixed_grad = ((cot * gates - mean_q - normed * mean_qn) * scale).astype(BF)
        score = dot_nt(mixed_grad, values) * sslope_s[h]
        rows = [
            jnp.sum(jnp.where(bucket == b, score, 0.0), axis=0, keepdims=True)
            for b in range(LEVELS)
        ]
        per_level = jnp.sum(jnp.concatenate(rows, axis=0), axis=1, keepdims=True)
        sums = sums + jnp.where(level_lane == h, per_level, 0.0)
        half = score.astype(BF)
        grads = [
            cot * normed,
            dot_tn(sweight_s[h], mixed_grad),
            dot_nn(half, keys) * SCALE,
            dot_tn(half, queries) * SCALE,
        ]
        for k in range(4):
            lanes = slice(k * HEAD, (k + 1) * HEAD)
            sgrad_s[h, :, lanes] = (grads[k] * sp_s[h, :, lanes]).astype(BF)
    sbias_s[...] = sums
    shape = (n_dp * SLEN, SHORT)
    same = (iota(shape, 0) & 15) == (iota(shape, 1) & 15)
    sender = jnp.where(
        same & (owner_row == (iota(shape, 0) >> 4).astype(F32)), 1.0, 0.0
    ).astype(BF)
    obuf[...] = dot_nn(sender, jnp.concatenate(outs, axis=1)).astype(BF).reshape(obuf.shape)
    for d in (1, 3, 2):
        sg_copy(d).start()
    grad_all[pl.ds(pl.multiple_of(LONG_ROWS + chip * SHORT, SHORT), SHORT), :] = sgrad_s[chip]

    def oy_copy(o):
        peer = lax.rem(y + o, ny)
        return remote(
            obuf.at[peer], omid.at[y], oy_s.at[o], oy_r.at[o], peer * NZ + z, ctx
        )

    def oz_copy(o):
        peer = lax.rem(z + o, NZ)
        return remote(
            omid.at[:, peer], orecv.at[:, z], oz_s.at[o], oz_r.at[o], y * NZ + peer, ctx
        )

    for o in range(1, ny):
        oy_copy(o).start()
    omid[y] = obuf[y]

    def sib_copy(qs):
        return remote(
            sib_send.at[qs], sib_recv.at[qs], sib_s.at[qs], sib_r.at[qs], dp, sib
        )

    def g_copy(k, qs):
        return remote(
            grad_all.at[rows_at(qs, ROWS), k * HEAD : (k + 1) * HEAD],
            grad_h.at[chip, :, k * HEAD : (k + 1) * HEAD],
            g_s.at[k, qs],
            g_r.at[k, chip],
            dp,
            2 * qs + core,
        )

    def l_copy(qs):
        return remote(
            out_s.at[qs], lo_v.at[:, lanes_at(chip)], l_s.at[qs], l_r.at[chip], dp, 2 * qs + core
        )

    def backward(step, carry):
        qs = CHIPS - 1 - step

        @pl.when(step == CHIPS - 1)
        def _():
            for o in range(1, ny):
                here = omid.at[lax.rem(y + ny - o, ny)]
                remote(here, here, oy_s.at[o], oy_r.at[o], dp, sib).wait_recv()
            for o in range(1, NZ):
                oz_copy(o).start()
            orecv[:, z] = omid[:, z]

        block = 2 * qs + core
        mine = rows_at(qs, ROWS)
        for d in (1, 3, 2):
            here = stat_s.at[qs, lax.rem(chip + CHIPS - d, CHIPS)]
            remote(here, here, stat_ss.at[qs, d], stat_sr.at[qs, d], dp, sib).wait_recv()
        stats = [stat_s[qs, h] for h in range(4)]
        mean = sum(s[0:1, :] for s in stats) * (1.0 / BLOCK)
        gaps = [s[0:1, :] * (1.0 / HEAD) - mean for s in stats]
        spread = sum(s[1:2, :] + HEAD * g * g for s, g in zip(stats, gaps)) * (1.0 / BLOCK)
        scale = lax.rsqrt(spread + epsilon)
        mean_q = sum(s[2:3, :] for s in stats) * (1.0 / BLOCK)
        mean_qn = sum(s[3:4, :] + g * s[2:3, :] for s, g in zip(stats, gaps))
        mean_qn = mean_qn * scale * (1.0 / BLOCK)
        whole = jnp.concatenate(
            [mean, scale, mean_q, mean_qn, jnp.zeros((124, ROWS), F32)], axis=0
        )
        cols = jnp.transpose(whole)
        mean, scale = cols[:, 0:1], cols[:, 1:2]
        mean_q, mean_qn = cols[:, 2:3], cols[:, 3:4]
        normed = (mixed_s[qs] - mean) * scale
        gates = act_s[qs, :, 0:HEAD].astype(F32)
        cotangent = c_g[qs].astype(F32)
        out_s[qs] = (normed * gates).astype(BF)
        mixed_grad = ((cotangent * gates - mean_q - normed * mean_qn) * scale).astype(BF)
        grad_all[mine, 0:HEAD] = (cotangent * normed * p_s[qs, :, 0:HEAD]).astype(BF)

        @pl.when(qs != chip)
        def _():
            l_copy(qs).start()
            g_copy(0, qs).start()

        queries = act_s[qs, :, 2 * HEAD : 3 * HEAD]
        tq = tcol_s[block][:, 0:1]
        dq_s[...] = jnp.zeros_like(dq_s)
        hist_s[...] = jnp.zeros_like(hist_s)

        def tile(p, carry):
            span = rows_at(p, PAIR)
            keys = kv[span, 0:HEAD]
            values = kv[span, HEAD : 2 * HEAD]
            score = dot_nt(mixed_grad, values) * slope_s[qs, p]
            near = jnp.where(tq - key_times(p) < LEVELS - 1.0, score, 0.0).astype(BF)
            half = score.astype(BF)
            tot_s[...] += jnp.sum(score.reshape(ROWS // 8, 8, PAIR), axis=0)
            hist_s[...] += dot_nn(near, hot_s[span, :])
            dq_s[...] += dot_nn(half, keys)
            dk_s[span, :] += dot_tn(half, queries)
            dv_s[span, :] += dot_tn(weight_s[qs, p], mixed_grad)
            return carry

        lax.fori_loop(0, qs + 1, tile, 0)
        hot = hot_s[rows_at(block, ROWS), :]
        high = hist_s[...].astype(BF)
        low = (hist_s[...] - high.astype(F32)).astype(BF)
        htot_s[...] += dot_tn(hot, high) + dot_tn(hot, low)
        grad_all[mine, 2 * HEAD : 3 * HEAD] = (
            dq_s[...] * SCALE * p_s[qs, :, 2 * HEAD : 3 * HEAD]
        ).astype(BF)
        other = rows_at(2 * qs + 1 - core, ROWS)
        sib_send[qs, :, 0:HEAD] = dk_s[other, :].astype(BF)
        sib_send[qs, :, HEAD : 2 * HEAD] = dv_s[other, :].astype(BF)
        sib_copy(qs).start()

        @pl.when(qs != chip)
        def _():
            g_copy(2, qs).start()

        return carry

    lax.fori_loop(0, CHIPS, backward, 0)

    shape = (128, 128)
    gap = (iota(shape, 0) - iota(shape, 1)) & 15
    hist = htot_s[...]
    rows = [
        jnp.sum(jnp.where(gap == b, hist, 0.0), axis=0, keepdims=True) for b in range(LEVELS - 1)
    ]
    total = jnp.sum(tot_s[...], axis=0, keepdims=True)
    total = sum(total[:, i : i + 128] for i in range(0, PAIR, 128))
    rows.append(total - sum(rows))
    levels = jnp.sum(jnp.concatenate(rows, axis=0), axis=1, keepdims=True)
    levels = sbias_s[...] + jnp.where(level_lane == chip, levels, 0.0)
    levels = jnp.concatenate([levels, jnp.zeros((128 - LEVELS, 128), F32)], axis=0)
    b_send[...] = jnp.transpose(levels)[0:8, :]

    def b2_copy(o):
        return remote(
            b_send, b_ctx.at[ctx], b2_s.at[o], b2_r.at[o], dp, lax.rem(ctx + o, 2 * CHIPS)
        )

    def start_b2(o, carry):
        b2_copy(o).start()
        return carry

    lax.fori_loop(1, 2 * CHIPS, start_b2, 0)
    b_ctx[ctx] = b_send[...]

    def finish(step, carry):
        qs = CHIPS - 1 - step
        sib_copy(qs).wait_recv()
        mine = rows_at(qs, ROWS)
        block = rows_at(2 * qs + core, ROWS)
        dk = (dk_s[block, :] + sib_recv[qs, :, 0:HEAD].astype(F32)) * SCALE
        dv = dv_s[block, :] + sib_recv[qs, :, HEAD : 2 * HEAD].astype(F32)
        grad_all[mine, HEAD : 2 * HEAD] = (
            dv * p_s[qs, :, HEAD : 2 * HEAD]
        ).astype(BF)
        grad_all[mine, 3 * HEAD : 4 * HEAD] = (
            dk * p_s[qs, :, 3 * HEAD : 4 * HEAD]
        ).astype(BF)

        @pl.when(qs != chip)
        def _():
            g_copy(1, qs).start()
            g_copy(3, qs).start()

        return carry

    lax.fori_loop(0, CHIPS, finish, 0)

    for d in (1, 3, 2):
        src = lax.rem(chip + CHIPS - d, CHIPS)
        there = pl.ds(pl.multiple_of(LONG_ROWS + src * SHORT, SHORT), SHORT)
        remote(stok, tok_all.at[there, :], st_s.at[d], st_r.at[d], dp, sib).wait_recv()
        remote(sgrad_s.at[src], grad_all.at[there, :], sg_s.at[d], sg_r.at[d], dp, sib).wait_recv()

    half_dp = n_dp // 2
    half_model = MODEL // 2
    my_half = lax.div(dp, half_dp)
    halves = (my_half, 1 - my_half)

    def outer(pair, half):
        cols = pl.ds(pl.multiple_of(pair * 2 * HEAD, 2 * HEAD), 2 * HEAD)
        rows = pl.ds(pl.multiple_of(half * half_model, half_model), half_model)
        return dot_tn(tok_all[:, rows], grad_all[:, cols])

    def swap(j):
        return remote(half_send.at[j], half_recv.at[j], p_ss.at[j], p_sr.at[j], dp, sib)

    def ry_copy(o):
        return remote(
            rs_send.at[y ^ o], rs_mid.at[y], ry_s.at[o], ry_r.at[o], (y ^ o) * NZ + z, ctx
        )

    def rz_copy(o):
        peer = lax.rem(z + o, NZ)
        return remote(
            rs_sum.at[peer], rs_fin.at[z], rz_s.at[o], rz_r.at[o], y * NZ + peer, ctx
        )

    for j in range(2):
        half_send[j] = outer(1 - core, halves[j]).astype(BF)
        swap(j).start()
    for j in range(2):
        own[...] = outer(core, halves[j])
        swap(j).wait_recv()
        total = (own[...] + half_recv[j].astype(F32)).astype(BF)
        rs_send[pl.ds(halves[j] * (ny // 2), ny // 2)] = total.reshape(
            (ny // 2,) + rs_send.shape[1:]
        )
        for o in ((1,), (2, 3))[j]:
            ry_copy(o).start()

    def wait_b2(o, carry):
        src = lax.rem(ctx + 2 * CHIPS - o, 2 * CHIPS)
        remote(b_send, b_ctx.at[src], b2_s.at[o], b2_r.at[o], dp, src).wait_recv()
        return carry

    lax.fori_loop(1, 2 * CHIPS, wait_b2, 0)
    b_mid[...] = jnp.sum(b_ctx[...], axis=0)
    one_start(b_mid, b_dp, b1_s, b1_r)
    b_dp[dp] = b_mid[...]

    def write(source, target, index):
        return pltpu.make_async_copy(source, target, out_sem.at[index])

    total = dot_nt(sgrad_s[0], wh[0])
    for h in range(1, 4):
        total = total + dot_nt(sgrad_s[h], wh[h])
    sg_v[...] = total.astype(BF)
    write(sg_v, short_grad, 3).start()

    total = rs_send[y].astype(F32)
    for o in range(1, ny):
        here = rs_mid.at[y ^ o]
        remote(here, here, ry_s.at[o], ry_r.at[o], dp, sib).wait_recv()
        total = total + rs_mid[y ^ o].astype(F32)
    rs_sum[...] = total.astype(BF)
    for o in range(1, NZ):
        rz_copy(o).start()

    for o in range(1, NZ):
        here = orecv.at[:, lax.rem(z + NZ - o, NZ)]
        remote(here, here, oz_s.at[o], oz_r.at[o], dp, sib).wait_recv()
    so_v[...] = dot_tn(place_s[...], orecv[...].reshape(n_dp * SLEN, BLOCK)).astype(BF)
    write(so_v, short_out, 1).start()

    lo_v[:, lanes_at(chip)] = out_s[chip]
    grad_h[chip] = grad_all[rows_at(chip, ROWS), :]
    total = dot_nt(grad_h[chip], wh[chip])
    for d in (1, 3, 2):
        src = lax.rem(chip + CHIPS - d, CHIPS)
        for k in range(4):
            here = grad_h.at[src, :, k * HEAD : (k + 1) * HEAD]
            remote(here, here, g_s.at[k, src], g_r.at[k, src], dp, sib).wait_recv()
        here = lo_v.at[:, lanes_at(src)]
        remote(out_s.at[src], here, l_s.at[src], l_r.at[src], dp, sib).wait_recv()
        total = total + dot_nt(grad_h[src], wh[src])
    tg_v[...] = total.astype(BF)
    write(tg_v, token_grad, 2).start()
    write(lo_v, long_out, 0).start()

    half_copy(up, 0, 0).wait_send()
    half_copy(up, 1, 0).wait_send()
    half_copy(down, 0, 1).wait_send()
    half_copy(down, 1, 1).wait_send()
    pass_copy(down, 0, up).wait_send()
    pass_copy(up, 1, down).wait_send()
    for d in (1, 3, 2):
        c_copy(d).wait_send()
        st_copy(d).wait_send()
        sg_copy(d).wait_send()
    one_all(dest_g, d_s, d_r).wait_send()
    dp_all(cbuf, crecv, s_s, s_r).wait_send()
    for o in range(1, ny):
        oy_copy(o).wait_send()
        ry_copy(o).wait_send()
    for o in range(1, NZ):
        oz_copy(o).wait_send()

    def ended_o(o, carry):
        t_copy(o).wait_send()
        b2_copy(o).wait_send()
        return carry

    lax.fori_loop(1, 2 * CHIPS, ended_o, 0)

    def ended_q(qs, carry):
        kv_copy(qs).wait_send()
        sib_copy(qs).wait_send()
        for d in (1, 3, 2):
            stat_copy(qs, d).wait_send()

        @pl.when(qs != chip)
        def _():
            l_copy(qs).wait_send()
            for k in range(4):
                g_copy(k, qs).wait_send()

        return carry

    lax.fori_loop(0, CHIPS, ended_q, 0)
    for j in range(2):
        swap(j).wait_send()

    total = rs_sum[z].astype(F32)
    for o in range(1, NZ):
        src = lax.rem(z + NZ - o, NZ)
        here = rs_fin.at[src]
        remote(here, here, rz_s.at[o], rz_r.at[o], dp, sib).wait_recv()
        total = total + rs_fin[src].astype(F32)
    piece[...] = total
    mine = lax.rem(chip, 2)

    def f_copy(i):
        target = 2 * (2 * core + i) + lax.div(chip, 2)
        return target, remote(
            piece.at[:, i * HEAD : (i + 1) * HEAD],
            proj_grad.at[:, lanes_at(mine)],
            f_s.at[i],
            f_r.at[mine],
            dp,
            target,
        )

    for i in range(2):
        target, copy = f_copy(i)

        @pl.when(target != ctx)
        def _():
            copy.start()

        @pl.when(target == ctx)
        def _():
            proj_grad[:, lanes_at(mine)] = piece[:, i * HEAD : (i + 1) * HEAD]

    one_all(b_dp, b1_s, b1_r).wait_recv()
    bias_out[...] = jnp.sum(b_dp[...], axis=0)[0:4, 0:LEVELS]

    for half in range(2):
        source = 2 * (2 * core + half) + lax.div(chip, 2)

        @pl.when(source != ctx)
        def _():
            remote(
                piece.at[:, 0:HEAD],
                proj_grad.at[:, half * HEAD : (half + 1) * HEAD],
                f_s.at[half],
                f_r.at[half],
                dp,
                source,
            ).wait_recv()

    for i in range(2):
        target, copy = f_copy(i)

        @pl.when(target != ctx)
        def _():
            copy.wait_send()

    for o in range(1, NZ):
        rz_copy(o).wait_send()
    one_all(b_dp, b1_s, b1_r).wait_send()
    write(lo_v, long_out, 0).wait()
    write(so_v, short_out, 1).wait()
    write(tg_v, token_grad, 2).wait()
    write(sg_v, short_grad, 3).wait()


def output_kernel(count, *refs):
    for i in range(count):
        refs[count + i][...] = refs[i][...]


VM = pl.BlockSpec(memory_space=pltpu.VMEM)
SM = pl.BlockSpec(memory_space=pltpu.SMEM)
ANY = pl.BlockSpec(memory_space=pl.ANY)
DMA = pltpu.SemaphoreType.DMA
VMEM = pltpu.VMEM


def shaped(shape, dtype):
    return jax.ShapeDtypeStruct(shape, dtype)


def per_device(
    n_dp,
    long_tokens,
    short_tokens,
    projection,
    time_bias,
    long_length,
    short_length,
    long_time,
    short_time,
    destination,
    long_cotangent,
    short_cotangent,
):
    part = MODEL // n_dp
    ny = n_dp // NZ
    spread = (n_dp, SLEN, BLOCK)
    scratch = [
        VMEM((CHIPS, MODEL, BLOCK), BF),
        VMEM((ALL_ROWS, MODEL), BF),
        VMEM((ALL_ROWS, BLOCK), BF),
        VMEM((CHIPS, ROWS, BLOCK), F32),
        VMEM((CHIPS, ROWS, BLOCK), BF),
        VMEM((2 * CHIPS * ROWS, 2 * HEAD), BF),
        VMEM((CHIPS, ROWS, HEAD), BF),
        VMEM((8, ROWS), jnp.int32),
        VMEM((2 * CHIPS, 8, ROWS), jnp.int32),
        VMEM((8, 128), F32),
        VMEM((8, 128), jnp.int32),
        VMEM((8, 128), jnp.int32),
        VMEM((n_dp, 8, 128), jnp.int32),
        VMEM((n_dp * SLEN, 128), BF),
        VMEM(spread, BF),
        VMEM(spread, BF),
        VMEM((4, SHORT, BLOCK), F32),
        VMEM((4, SHORT, BLOCK), BF),
        VMEM((4, SHORT, SHORT), BF),
        VMEM((4, SHORT, SHORT), F32),
        VMEM((4, SHORT, HEAD), F32),
        VMEM((SHORT, 128), F32),
        VMEM((SHORT, BLOCK), F32),
        VMEM((4, SHORT, BLOCK), BF),
        VMEM((ny, NZ, SLEN, BLOCK), BF),
        VMEM((ny, NZ, SLEN, BLOCK), BF),
        VMEM((ny, NZ, SLEN, BLOCK), BF),
        VMEM((LEVELS, 128), F32),
        VMEM((CHIPS, CHIPS, ROWS, PAIR), BF),
        VMEM((CHIPS, CHIPS, ROWS, PAIR), F32),
        VMEM((CHIPS, ROWS, HEAD), F32),
        VMEM((CHIPS, ROWS, HEAD), BF),
        VMEM((2 * CHIPS * ROWS, 128), BF),
        VMEM((2 * CHIPS, ROWS, 128), F32),
        VMEM((CHIPS, CHIPS, 8, ROWS), F32),
        VMEM((2 * CHIPS * ROWS, HEAD), F32),
        VMEM((2 * CHIPS * ROWS, HEAD), F32),
        VMEM((ROWS, HEAD), F32),
        VMEM((ROWS, 128), F32),
        VMEM((128, 128), F32),
        VMEM((8, PAIR), F32),
        VMEM((CHIPS, ROWS, 2 * HEAD), BF),
        VMEM((CHIPS, ROWS, 2 * HEAD), BF),
        VMEM((CHIPS, ROWS, BLOCK), BF),
        VMEM((2, MODEL // 2, 2 * HEAD), BF),
        VMEM((2, MODEL // 2, 2 * HEAD), BF),
        VMEM((MODEL // 2, 2 * HEAD), F32),
        VMEM((ny, NZ, part, 2 * HEAD), BF),
        VMEM((ny, NZ, part, 2 * HEAD), BF),
        VMEM((NZ, part, 2 * HEAD), BF),
        VMEM((NZ, part, 2 * HEAD), BF),
        VMEM((8, 128), F32),
        VMEM((n_dp, 8, 128), F32),
        VMEM((8, 128), F32),
        VMEM((2 * CHIPS, 8, 128), F32),
        VMEM((part, 2 * HEAD), F32),
        VMEM((ROWS, BLOCK), BF),
        VMEM((SHORT, BLOCK), BF),
        VMEM((ROWS, MODEL), BF),
        VMEM((SHORT, MODEL), BF),
        DMA((4, 4)),
        DMA((3,)),
        DMA((4,)),
        DMA((2, 2)),
        DMA((2, 2)),
        DMA((2,)),
        DMA((2,)),
        DMA((CHIPS,)),
        DMA((CHIPS,)),
        DMA((2 * CHIPS,)),
        DMA((2 * CHIPS,)),
        DMA((CHIPS,)),
        DMA((CHIPS,)),
        DMA((CHIPS,)),
        DMA((CHIPS,)),
        DMA((CHIPS,)),
        DMA((CHIPS,)),
        DMA,
        DMA,
        DMA,
        DMA,
        DMA((ny,)),
        DMA((ny,)),
        DMA((NZ,)),
        DMA((NZ,)),
        DMA((CHIPS, CHIPS)),
        DMA((CHIPS, CHIPS)),
        DMA((CHIPS,)),
        DMA((CHIPS,)),
        DMA((4, CHIPS)),
        DMA((4, CHIPS)),
        DMA((CHIPS,)),
        DMA((CHIPS,)),
        DMA((2,)),
        DMA((2,)),
        DMA((ny,)),
        DMA((ny,)),
        DMA((NZ,)),
        DMA((NZ,)),
        DMA,
        DMA,
        DMA((2 * CHIPS,)),
        DMA((2 * CHIPS,)),
        DMA((2,)),
        DMA((2,)),
    ]
    results = pl.pallas_call(
        functools.partial(layer_kernel, n_dp),
        out_shape=(
            shaped((ROWS, BLOCK), BF),
            shaped((SHORT, BLOCK), BF),
            shaped((ROWS, MODEL), BF),
            shaped((SHORT, MODEL), BF),
            shaped((part, 2 * HEAD), F32),
            shaped(time_bias.shape, F32),
        ),
        in_specs=[ANY, ANY, ANY, ANY, VM, VM, VM, VM, VM, SM, VM],
        out_specs=(ANY,) * 4 + (VM,) * 2,
        scratch_shapes=scratch,
        compiler_params=pltpu.CompilerParams(
            vmem_limit_bytes=VMEM_LIMIT, collective_id=0, has_side_effects=True
        ),
        name="layer",
    )(
        long_tokens[0],
        short_tokens.reshape(SHORT, MODEL),
        projection,
        long_cotangent[0],
        short_cotangent.reshape(SHORT, BLOCK),
        long_time,
        short_time,
        short_length,
        destination,
        long_length,
        time_bias,
    )
    results = pl.pallas_call(
        functools.partial(output_kernel, len(results)),
        out_shape=tuple(shaped(r.shape, r.dtype) for r in results),
        in_specs=[VM] * len(results),
        out_specs=(VM,) * len(results),
        compiler_params=pltpu.CompilerParams(vmem_limit_bytes=VMEM_LIMIT),
        name="output",
    )(*results)
    long_out, short_out, token_grad, short_grad, proj_grad, bias_out = results
    return (
        long_out[None],
        short_out.reshape(short_cotangent.shape),
        token_grad[None],
        short_grad.reshape(short_tokens.shape),
        proj_grad,
        bias_out,
    )


def solution(mesh):
    return jax.shard_map(
        functools.partial(per_device, mesh.shape["dp"]),
        mesh=mesh,
        in_specs=(
            P("dp", "ctx", None),
            P("dp", "ctx", None, None),
            P(),
            P(),
            P("dp"),
            P("dp", "ctx"),
            P("dp", "ctx"),
            P("dp", "ctx", None),
            P("dp", "ctx"),
            P("dp", "ctx", None),
            P("dp", "ctx", None, None),
        ),
        out_specs=(
            P("dp", "ctx", None),
            P("dp", "ctx", None, None),
            P("dp", "ctx", None),
            P("dp", "ctx", None, None),
            P("dp", "ctx"),
            P(),
        ),
        check_vma=False,
    )
```

```python
import functools

import jax
import jax.numpy as jnp
from jax import lax
from jax.experimental import pallas as pl
from jax.experimental.pallas import tpu as pltpu
from jax.sharding import PartitionSpec as P

epsilon = 1e-05
MESH = pl.DeviceIdType.MESH
BF = jnp.bfloat16
F32 = jnp.float32
CHIPS = 4
NZ = 8
ROWS = 256
HEAD = 128
LEVELS = 16
SLEN = 16
SHORT = 128
LONG_ROWS = CHIPS * ROWS
ALL_ROWS = CHIPS * (ROWS + SHORT)
PAIR = 2 * ROWS
MODEL = 1024
BLOCK = 512
SCALE = HEAD ** (-0.5)
VMEM_LIMIT = 56 * 1024 * 1024


def sigmoid(value):
    return 0.5 * jnp.tanh(0.5 * value) + 0.5


def silu_and_grad(value):
    sigma = sigmoid(value)
    silu = value * sigma
    return silu.astype(BF), sigma + silu * (1.0 - sigma)


def dot_nn(a, b):
    return jnp.dot(a, b, preferred_element_type=F32)


def dot_nt(a, b):
    return lax.dot_general(a, b, (((1,), (1,)), ((), ())), preferred_element_type=F32)


def dot_tn(a, b):
    return lax.dot_general(a, b, (((0,), (0,)), ((), ())), preferred_element_type=F32)


def column_of(row):
    return jnp.transpose(jnp.broadcast_to(row, (128, 128)))


def iota(shape, axis):
    return lax.broadcasted_iota(jnp.int32, shape, axis)


def remote(src, dst, send_sem, recv_sem, dp, ctx):
    return pltpu.make_async_remote_copy(
        src_ref=src,
        dst_ref=dst,
        send_sem=send_sem,
        recv_sem=recv_sem,
        device_id=(dp, ctx),
        device_id_type=MESH,
    )


def place():
    dp = lax.axis_index("dp")
    ctx = lax.axis_index("ctx")
    return dp, ctx, lax.div(ctx, 2), lax.rem(ctx, 2)


def lookup(table, diff):
    index = jnp.clip(diff, 0.0, LEVELS - 1.0).astype(jnp.int32)
    parts = [
        jnp.take_along_axis(table, index[:, i : i + 128], axis=1)
        for i in range(0, index.shape[1], 128)
    ]
    return parts[0] if len(parts) == 1 else jnp.concatenate(parts, axis=1)


def exact_dot(a, b):
    return lax.dot_general(
        a,
        b,
        (((1,), (0,)), ((), ())),
        precision=lax.Precision.HIGHEST,
        preferred_element_type=F32,
    )


def rows_at(block, rows):
    return pl.ds(pl.multiple_of(block * rows, rows), rows)


def lanes_at(block):
    return pl.ds(pl.multiple_of(block * HEAD, HEAD), HEAD)


def layer_kernel(
    n_dp,
    tok,
    stok,
    w,
    lcot,
    scot,
    ltime,
    stime,
    slen,
    dest_in,
    llen,
    tbias,
    long_out,
    short_out,
    token_grad,
    short_grad,
    proj_grad,
    bias_out,
    wh,
    tok_all,
    grad_all,
    p_s,
    act_s,
    kv,
    c_g,
    tmeta,
    times,
    tab_s,
    ints,
    dtile,
    dest_g,
    place_s,
    cbuf,
    crecv,
    sp_s,
    sact_s,
    sweight_s,
    sslope_s,
    snorm_s,
    sscale_s,
    c_home,
    sgrad_s,
    obuf,
    omid,
    orecv,
    sbias_s,
    weight_s,
    slope_s,
    mixed_s,
    out_s,
    hot_s,
    tcol_s,
    stat_s,
    dk_s,
    dv_s,
    dq_s,
    hist_s,
    htot_s,
    tot_s,
    sib_send,
    sib_recv,
    grad_h,
    half_send,
    half_recv,
    own,
    rs_send,
    rs_mid,
    rs_sum,
    rs_fin,
    b_send,
    b_dp,
    b_mid,
    b_ctx,
    piece,
    lo_v,
    so_v,
    tg_v,
    sg_v,
    w_sem,
    in_sem,
    out_sem,
    tok_s,
    tok_r,
    fwd_s,
    fwd_r,
    c_s,
    c_r,
    t_s,
    t_r,
    kv_s,
    kv_r,
    st_s,
    st_r,
    sg_s,
    sg_r,
    d_s,
    d_r,
    s_s,
    s_r,
    oy_s,
    oy_r,
    oz_s,
    oz_r,
    stat_ss,
    stat_sr,
    sib_s,
    sib_r,
    g_s,
    g_r,
    l_s,
    l_r,
    p_ss,
    p_sr,
    ry_s,
    ry_r,
    rz_s,
    rz_r,
    b1_s,
    b1_r,
    b2_s,
    b2_r,
    f_s,
    f_r,
):
    dp, ctx, chip, core = place()
    sib = ctx + 1 - 2 * core
    up = lax.rem(chip + 1, CHIPS)
    down = lax.rem(chip + CHIPS - 1, CHIPS)
    far = lax.rem(chip + 2, CHIPS)
    half_rows = ROWS // 2
    ny = n_dp // NZ
    y, z = lax.div(dp, NZ), lax.rem(dp, NZ)
    barrier = pltpu.get_barrier_semaphore()

    def greet_ctx(o, carry):
        pl.semaphore_signal(
            barrier, inc=1, device_id=(dp, lax.rem(ctx + o, 2 * CHIPS)), device_id_type=MESH
        )
        return carry

    def greet_dp(o, carry):
        pl.semaphore_signal(
            barrier, inc=1, device_id=(lax.rem(dp + o, n_dp), ctx), device_id_type=MESH
        )
        return carry

    lax.fori_loop(1, 2 * CHIPS, greet_ctx, 0)
    lax.fori_loop(1, n_dp, greet_dp, 0)

    def w_copy(h, k):
        return pltpu.make_async_copy(
            w.at[:, k * BLOCK + h * HEAD : k * BLOCK + (h + 1) * HEAD],
            wh.at[h, :, k * HEAD : (k + 1) * HEAD],
            w_sem.at[h, k],
        )

    for h in range(4):
        for k in range(4):
            w_copy(h, k).start()
    tmeta[...] = jnp.broadcast_to(ltime[...], (8, ROWS))
    ints[...] = jnp.zeros((8, 128), jnp.int32) - 1
    ints[0:1, 0:8] = slen[...]
    ints[1:2, 0:8] = dest_in[...]
    dtile[...] = jnp.broadcast_to(ints[1:2, :], (8, 128))
    tab_s[...] = jnp.zeros_like(tab_s)
    tab_s[0:4, 0:LEVELS] = tbias[...]

    def half_copy(peer, half, index):
        return remote(
            tok.at[half * half_rows : (half + 1) * half_rows, :],
            tok_all.at[rows_at(2 * chip + half, half_rows), :],
            tok_s.at[index, half],
            tok_r.at[index, half],
            dp,
            2 * peer + core,
        )

    def half_wait(src, half, index):
        here = tok_all.at[rows_at(2 * src + half, half_rows), :]
        remote(here, here, tok_s.at[index, half], tok_r.at[index, half], dp, sib).wait_recv()

    def pass_copy(src, half, peer):
        here = tok_all.at[rows_at(2 * src + half, half_rows), :]
        return remote(here, here, fwd_s.at[half], fwd_r.at[half], dp, 2 * peer + core)

    def c_copy(d):
        peer = lax.rem(chip + d, CHIPS)
        return remote(
            lcot.at[:, lanes_at(peer)], c_g.at[chip], c_s.at[d], c_r.at[d], dp, 2 * peer + core
        )

    def t_copy(o):
        return remote(
            tmeta, times.at[ctx], t_s.at[o], t_r.at[o], dp, lax.rem(ctx + o, 2 * CHIPS)
        )

    def kv_copy(src):
        here = kv.at[rows_at(2 * src + core, ROWS), :]
        return remote(here, here, kv_s.at[src], kv_r.at[src], dp, sib)

    def kv_wait(src):
        here = kv.at[rows_at(2 * src + 1 - core, ROWS), :]
        remote(here, here, kv_s.at[src], kv_r.at[src], dp, sib).wait_recv()

    def st_copy(d):
        return remote(
            stok,
            tok_all.at[pl.ds(pl.multiple_of(LONG_ROWS + chip * SHORT, SHORT), SHORT), :],
            st_s.at[d],
            st_r.at[d],
            dp,
            2 * lax.rem(chip + d, CHIPS) + core,
        )

    def sg_copy(d):
        peer = lax.rem(chip + d, CHIPS)
        return remote(
            sgrad_s.at[peer],
            grad_all.at[pl.ds(pl.multiple_of(LONG_ROWS + chip * SHORT, SHORT), SHORT), :],
            sg_s.at[d],
            sg_r.at[d],
            dp,
            2 * peer + core,
        )

    def dp_start(source, target, send, recv):
        def one(o, carry):
            peer = lax.rem(dp + o, n_dp)
            remote(source.at[peer], target.at[dp], send, recv, peer, ctx).start()
            return carry

        lax.fori_loop(1, n_dp, one, 0)

    def dp_all(source, target, send, recv):
        return remote(
            source.at[0 : n_dp - 1], target.at[0 : n_dp - 1], send, recv, dp, sib
        )

    def one_start(source, target, send, recv):
        def one(o, carry):
            remote(source, target.at[dp], send, recv, lax.rem(dp + o, n_dp), ctx).start()
            return carry

        lax.fori_loop(1, n_dp, one, 0)

    def one_all(target, send, recv):
        here = target.at[0 : n_dp - 1]
        return remote(here, here, send, recv, dp, sib)

    home_rows = pl.ds(pl.multiple_of(LONG_ROWS + chip * SHORT, SHORT), SHORT)
    loads = [
        pltpu.make_async_copy(tok, tok_all.at[rows_at(chip, ROWS), :], in_sem.at[0]),
        pltpu.make_async_copy(stok, tok_all.at[home_rows, :], in_sem.at[1]),
        pltpu.make_async_copy(lcot.at[:, lanes_at(chip)], c_g.at[chip], in_sem.at[2]),
    ]
    for load in loads:
        load.start()
    pl.semaphore_wait(barrier, n_dp - 1 + 2 * CHIPS - 1)
    half_copy(up, 0, 0).start()
    half_copy(down, 1, 1).start()
    half_copy(up, 1, 0).start()
    half_copy(down, 0, 1).start()
    one_start(dtile, dest_g, d_s, d_r)

    def start_t(o, carry):
        t_copy(o).start()
        return carry

    lax.fori_loop(1, 2 * CHIPS, start_t, 0)
    times[ctx] = tmeta[...]
    dest_g[dp] = dtile[...]
    for h in range(4):
        for k in range(4):
            w_copy(h, k).wait()
    for load in loads:
        load.wait()

    def project(src):
        projected = dot_nn(tok_all[rows_at(src, ROWS), :], wh[chip])
        act, p_s[src] = silu_and_grad(projected)
        act_s[src] = act
        kv[rows_at(2 * src + core, ROWS), 0:HEAD] = act[:, 3 * HEAD : 4 * HEAD]
        kv[rows_at(2 * src + core, ROWS), HEAD : 2 * HEAD] = act[:, HEAD : 2 * HEAD]
        kv_copy(src).start()

    project(chip)

    lane16 = iota((16, 128), 1)
    spread_time = exact_dot(
        stime[0].astype(F32), jnp.where((lane16 & 15) == iota((16, 128), 0), 1.0, 0.0)
    )
    pick = (iota((8, 128), 1) >> 4) == iota((8, 128), 0)
    stime_row = jnp.sum(jnp.where(pick, spread_time, 0.0), axis=0, keepdims=True)
    repeat = jnp.where((iota((128, 128), 1) >> 4) == iota((128, 128), 0), 1.0, 0.0)
    rep_rows = exact_dot(ints[...].astype(F32), repeat)
    slen_row, home_row = rep_rows[0:1, :], rep_rows[1:2, :]
    owner_row = (home_row.astype(jnp.int32) >> 3).astype(F32)
    shape = (SHORT, SHORT)
    row = iota(shape, 0)
    col = iota(shape, 1)
    stime_diff = column_of(stime_row) - stime_row
    inside = (row & 15).astype(F32) < column_of(slen_row)
    svisible = ((row >> 4) == (col >> 4)) & (col <= row) & inside

    short_tokens = tok_all[home_rows, :]
    mixes = []
    for h in range(4):
        act, sp_s[h] = silu_and_grad(dot_nn(short_tokens, wh[h]))
        sact_s[h] = act
        queries, keys = act[:, 2 * HEAD : 3 * HEAD], act[:, 3 * HEAD : 4 * HEAD]
        tab = jnp.broadcast_to(tab_s[h : h + 1, :], (SHORT, 128))
        total = dot_nt(queries, keys) * SCALE + lookup(tab, stime_diff)
        sg = sigmoid(total)
        weight = total * sg
        weight16 = jnp.where(svisible, weight, 0.0).astype(BF)
        sweight_s[h] = weight16
        sslope_s[h] = jnp.where(svisible, sg + weight * (1.0 - sg), 0.0)
        mixes.append(dot_nn(weight16, act[:, HEAD : 2 * HEAD]))
    mean = sum(jnp.sum(m, axis=1, keepdims=True) for m in mixes) * (1.0 / BLOCK)
    centred = [m - mean for m in mixes]
    spread = sum(jnp.sum(m * m, axis=1, keepdims=True) for m in centred) * (1.0 / BLOCK)
    scale = lax.rsqrt(spread + epsilon)
    sscale_s[...] = jnp.broadcast_to(scale, sscale_s.shape)
    for h in range(4):
        snorm_s[h] = centred[h] * scale

    one_all(dest_g, d_s, d_r).wait_recv()
    dest = dest_g[...]
    code = jnp.sum(
        jnp.where((dest >> 3) == dp, ((dest & 7) + 1).astype(F32), 0.0), axis=2, keepdims=True
    )
    code = jnp.broadcast_to(code, (n_dp, 8, 128))
    code = jnp.concatenate([code, code], axis=1).reshape(n_dp * SLEN, 128)
    shape = (n_dp * SLEN, 128)
    same = (iota(shape, 0) & 15) == (iota(shape, 1) & 15)
    slot = ((iota(shape, 1) >> 4) + 1).astype(F32)
    placer = jnp.where(same & (code == slot), 1.0, 0.0).astype(BF)
    place_s[...] = placer
    cbuf[...] = dot_nn(placer, scot[...]).astype(BF).reshape(cbuf.shape)
    dp_start(cbuf, crecv, s_s, s_r)
    crecv[dp] = cbuf[dp]

    half_wait(down, 0, 0)
    pass_copy(down, 0, up).start()
    half_wait(up, 1, 1)
    pass_copy(up, 1, down).start()
    for d in (1, 3, 2):
        c_copy(d).start()

    def wait_t(o, carry):
        src = lax.rem(ctx + 2 * CHIPS - o, 2 * CHIPS)
        remote(tmeta, times.at[src], t_s.at[o], t_r.at[o], dp, src).wait_recv()
        return carry

    lax.fori_loop(1, 2 * CHIPS, wait_t, 0)
    lane = iota((ROWS, 128), 1)

    def times_of(b, carry):
        line = times[b, 0:1, :].astype(F32)
        column = jnp.concatenate(
            [column_of(line[:, 0:128]), column_of(line[:, 128:256])], axis=0
        )
        tcol_s[b] = column
        hot_s[rows_at(b, ROWS), :] = jnp.where(
            (column.astype(jnp.int32) & 15) == lane, 1.0, 0.0
        ).astype(BF)
        return carry

    lax.fori_loop(0, 2 * CHIPS, times_of, 0)
    dk_s[...] = jnp.zeros_like(dk_s)
    dv_s[...] = jnp.zeros_like(dv_s)
    htot_s[...] = jnp.zeros_like(htot_s)
    tot_s[...] = jnp.zeros_like(tot_s)
    mixed_s[...] = jnp.zeros_like(mixed_s)

    half_wait(down, 1, 0)
    project(down)
    half_wait(up, 0, 1)
    project(up)

    table = jnp.broadcast_to(tab_s[pl.ds(chip, 1), :], (ROWS, 128))
    length = llen[0]

    def key_times(p):
        return jnp.concatenate(
            [times[2 * p, 0:1, :], times[2 * p + 1, 0:1, :]], axis=1
        ).astype(F32)

    def forward_tile(qs, p):
        block = 2 * qs + core
        queries = act_s[qs, :, 2 * HEAD : 3 * HEAD]
        tq = tcol_s[block][:, 0:1]
        spot = iota((ROWS, 1), 0) + block * ROWS
        limit = jnp.where(spot < length, spot, -1)
        keys = kv[rows_at(p, PAIR), 0:HEAD]
        values = kv[rows_at(p, PAIR), HEAD : 2 * HEAD]
        total = dot_nt(queries, keys) * SCALE + lookup(table, tq - key_times(p))
        sg = sigmoid(total)
        weight = total * sg
        visible = (iota((ROWS, PAIR), 1) + p * PAIR) <= limit
        weight16 = jnp.where(visible, weight, 0.0).astype(BF)
        weight_s[qs, p] = weight16
        slope_s[qs, p] = jnp.where(visible, sg + weight * (1.0 - sg), 0.0)
        mixed_s[qs] += dot_nn(weight16, values)

    for d in (0, 1, 3):
        kv_wait(lax.rem(chip + CHIPS - d, CHIPS))

    def near_block(step, carry):
        qs = CHIPS - 1 - step

        def one(p, carry):
            @pl.when(p != far)
            def _():
                forward_tile(qs, p)

            return carry

        lax.fori_loop(0, jnp.where(qs == far, 0, qs + 1), one, 0)
        return carry

    lax.fori_loop(0, CHIPS, near_block, 0)

    for half in range(2):
        here = tok_all.at[rows_at(2 * far + half, half_rows), :]
        remote(here, here, fwd_s.at[half], fwd_r.at[half], dp, sib).wait_recv()
    project(far)
    for d in (1, 3, 2):
        st_copy(d).start()
    for d in (1, 3, 2):
        src = lax.rem(chip + CHIPS - d, CHIPS)
        remote(c_g.at[src], c_g.at[src], c_s.at[d], c_r.at[d], dp, sib).wait_recv()
    kv_wait(far)

    def stat_copy(qs, d):
        here = stat_s.at[qs, chip]
        return remote(
            here,
            here,
            stat_ss.at[qs, d],
            stat_sr.at[qs, d],
            dp,
            2 * lax.rem(chip + d, CHIPS) + core,
        )

    def far_block(step, carry):
        qs = CHIPS - 1 - step

        def one(p, carry):
            forward_tile(qs, p)
            return carry

        first = jnp.where(qs == far, 0, far)
        last = jnp.where(qs >= far, jnp.where(qs == far, qs, far) + 1, first)
        lax.fori_loop(first, last, one, 0)
        mixed = mixed_s[qs]
        q = c_g[qs].astype(F32) * act_s[qs, :, 0:HEAD].astype(F32)
        s1 = jnp.sum(mixed, axis=1, keepdims=True)
        centred = mixed - s1 * (1.0 / HEAD)
        s2 = jnp.sum(centred * centred, axis=1, keepdims=True)
        s3 = jnp.sum(q, axis=1, keepdims=True)
        s4 = jnp.sum(q * centred, axis=1, keepdims=True)
        stats = jnp.where(
            lane == 0, s1, jnp.where(lane == 1, s2, jnp.where(lane == 2, s3, s4))
        )
        stat_s[qs, chip] = jnp.transpose(stats)[0:8, :]
        for d in (1, 3, 2):
            stat_copy(qs, d).start()
        return carry

    lax.fori_loop(0, CHIPS, far_block, 0)

    dp_all(cbuf, crecv, s_s, s_r).wait_recv()
    owner = jnp.concatenate([column_of(owner_row)] * (n_dp * SLEN // 128), axis=1)
    shape = (SHORT, n_dp * SLEN)
    same = (iota(shape, 0) & 15) == (iota(shape, 1) & 15)
    chooser = jnp.where(
        same & (owner == (iota(shape, 1) >> 4).astype(F32)), 1.0, 0.0
    ).astype(BF)
    c_home[...] = dot_nn(chooser, crecv[...].reshape(n_dp * SLEN, BLOCK))
    scale = sscale_s[:, 0:1]
    mean_q = jnp.zeros((SHORT, 1), F32)
    mean_qn = jnp.zeros((SHORT, 1), F32)
    for h in range(4):
        q = c_home[:, h * HEAD : (h + 1) * HEAD] * sact_s[h, :, 0:HEAD].astype(F32)
        mean_q = mean_q + jnp.sum(q, axis=1, keepdims=True)
        mean_qn = mean_qn + jnp.sum(q * snorm_s[h], axis=1, keepdims=True)
    mean_q = mean_q * (1.0 / BLOCK)
    mean_qn = mean_qn * (1.0 / BLOCK)
    bucket = jnp.clip(stime_diff, 0.0, LEVELS - 1.0).astype(jnp.int32)
    level_lane = iota((LEVELS, 128), 1)
    sums = jnp.zeros((LEVELS, 128), F32)
    outs = []
    for h in range(4):
        act = sact_s[h]
        gates = act[:, 0:HEAD].astype(F32)
        values = act[:, HEAD : 2 * HEAD]
        queries = act[:, 2 * HEAD : 3 * HEAD]
        keys = act[:, 3 * HEAD : 4 * HEAD]
        normed = snorm_s[h]
        cot = c_home[:, h * HEAD : (h + 1) * HEAD]
        outs.append((normed * gates).astype(BF))
        mixed_grad = ((cot * gates - mean_q - normed * mean_qn) * scale).astype(BF)
        score = dot_nt(mixed_grad, values) * sslope_s[h]
        rows = [
            jnp.sum(jnp.where(bucket == b, score, 0.0), axis=0, keepdims=True)
            for b in range(LEVELS)
        ]
        per_level = jnp.sum(jnp.concatenate(rows, axis=0), axis=1, keepdims=True)
        sums = sums + jnp.where(level_lane == h, per_level, 0.0)
        half = score.astype(BF)
        grads = [
            cot * normed,
            dot_tn(sweight_s[h], mixed_grad),
            dot_nn(half, keys) * SCALE,
            dot_tn(half, queries) * SCALE,
        ]
        for k in range(4):
            lanes = slice(k * HEAD, (k + 1) * HEAD)
            sgrad_s[h, :, lanes] = (grads[k] * sp_s[h, :, lanes]).astype(BF)
    sbias_s[...] = sums
    shape = (n_dp * SLEN, SHORT)
    same = (iota(shape, 0) & 15) == (iota(shape, 1) & 15)
    sender = jnp.where(
        same & (owner_row == (iota(shape, 0) >> 4).astype(F32)), 1.0, 0.0
    ).astype(BF)
    obuf[...] = dot_nn(sender, jnp.concatenate(outs, axis=1)).astype(BF).reshape(obuf.shape)
    for d in (1, 3, 2):
        sg_copy(d).start()
    grad_all[pl.ds(pl.multiple_of(LONG_ROWS + chip * SHORT, SHORT), SHORT), :] = sgrad_s[chip]

    def oy_copy(o):
        peer = lax.rem(y + o, ny)
        return remote(
            obuf.at[peer], omid.at[y], oy_s.at[o], oy_r.at[o], peer * NZ + z, ctx
        )

    def oz_copy(o):
        peer = lax.rem(z + o, NZ)
        return remote(
            omid.at[:, peer], orecv.at[:, z], oz_s.at[o], oz_r.at[o], y * NZ + peer, ctx
        )

    for o in range(1, ny):
        oy_copy(o).start()
    omid[y] = obuf[y]

    def sib_copy(qs):
        return remote(
            sib_send.at[qs], sib_recv.at[qs], sib_s.at[qs], sib_r.at[qs], dp, sib
        )

    def g_copy(k, qs):
        return remote(
            grad_all.at[rows_at(qs, ROWS), k * HEAD : (k + 1) * HEAD],
            grad_h.at[chip, :, k * HEAD : (k + 1) * HEAD],
            g_s.at[k, qs],
            g_r.at[k, chip],
            dp,
            2 * qs + core,
        )

    def l_copy(qs):
        return remote(
            out_s.at[qs], lo_v.at[:, lanes_at(chip)], l_s.at[qs], l_r.at[chip], dp, 2 * qs + core
        )

    def backward(step, carry):
        qs = CHIPS - 1 - step

        @pl.when(step == CHIPS - 1)
        def _():
            for o in range(1, ny):
                here = omid.at[lax.rem(y + ny - o, ny)]
                remote(here, here, oy_s.at[o], oy_r.at[o], dp, sib).wait_recv()
            for o in range(1, NZ):
                oz_copy(o).start()
            orecv[:, z] = omid[:, z]

        block = 2 * qs + core
        mine = rows_at(qs, ROWS)
        for d in (1, 3, 2):
            here = stat_s.at[qs, lax.rem(chip + CHIPS - d, CHIPS)]
            remote(here, here, stat_ss.at[qs, d], stat_sr.at[qs, d], dp, sib).wait_recv()
        stats = [stat_s[qs, h] for h in range(4)]
        mean = sum(s[0:1, :] for s in stats) * (1.0 / BLOCK)
        gaps = [s[0:1, :] * (1.0 / HEAD) - mean for s in stats]
        spread = sum(s[1:2, :] + HEAD * g * g for s, g in zip(stats, gaps)) * (1.0 / BLOCK)
        scale = lax.rsqrt(spread + epsilon)
        mean_q = sum(s[2:3, :] for s in stats) * (1.0 / BLOCK)
        mean_qn = sum(s[3:4, :] + g * s[2:3, :] for s, g in zip(stats, gaps))
        mean_qn = mean_qn * scale * (1.0 / BLOCK)
        whole = jnp.concatenate(
            [mean, scale, mean_q, mean_qn, jnp.zeros((124, ROWS), F32)], axis=0
        )
        cols = jnp.transpose(whole)
        mean, scale = cols[:, 0:1], cols[:, 1:2]
        mean_q, mean_qn = cols[:, 2:3], cols[:, 3:4]
        normed = (mixed_s[qs] - mean) * scale
        gates = act_s[qs, :, 0:HEAD].astype(F32)
        cotangent = c_g[qs].astype(F32)
        out_s[qs] = (normed * gates).astype(BF)
        mixed_grad = ((cotangent * gates - mean_q - normed * mean_qn) * scale).astype(BF)
        grad_all[mine, 0:HEAD] = (cotangent * normed * p_s[qs, :, 0:HEAD]).astype(BF)

        @pl.when(qs != chip)
        def _():
            l_copy(qs).start()
            g_copy(0, qs).start()

        queries = act_s[qs, :, 2 * HEAD : 3 * HEAD]
        tq = tcol_s[block][:, 0:1]
        dq_s[...] = jnp.zeros_like(dq_s)
        hist_s[...] = jnp.zeros_like(hist_s)

        def tile(p, carry):
            span = rows_at(p, PAIR)
            keys = kv[span, 0:HEAD]
            values = kv[span, HEAD : 2 * HEAD]
            score = dot_nt(mixed_grad, values) * slope_s[qs, p]
            near = jnp.where(tq - key_times(p) < LEVELS - 1.0, score, 0.0).astype(BF)
            half = score.astype(BF)
            tot_s[...] += jnp.sum(score.reshape(ROWS // 8, 8, PAIR), axis=0)
            hist_s[...] += dot_nn(near, hot_s[span, :])
            dq_s[...] += dot_nn(half, keys)
            dk_s[span, :] += dot_tn(half, queries)
            dv_s[span, :] += dot_tn(weight_s[qs, p], mixed_grad)
            return carry

        lax.fori_loop(0, qs + 1, tile, 0)
        hot = hot_s[rows_at(block, ROWS), :]
        high = hist_s[...].astype(BF)
        low = (hist_s[...] - high.astype(F32)).astype(BF)
        htot_s[...] += dot_tn(hot, high) + dot_tn(hot, low)
        grad_all[mine, 2 * HEAD : 3 * HEAD] = (
            dq_s[...] * SCALE * p_s[qs, :, 2 * HEAD : 3 * HEAD]
        ).astype(BF)
        other = rows_at(2 * qs + 1 - core, ROWS)
        sib_send[qs, :, 0:HEAD] = dk_s[other, :].astype(BF)
        sib_send[qs, :, HEAD : 2 * HEAD] = dv_s[other, :].astype(BF)
        sib_copy(qs).start()

        @pl.when(qs != chip)
        def _():
            g_copy(2, qs).start()

        return carry

    lax.fori_loop(0, CHIPS, backward, 0)

    shape = (128, 128)
    gap = (iota(shape, 0) - iota(shape, 1)) & 15
    hist = htot_s[...]
    rows = [
        jnp.sum(jnp.where(gap == b, hist, 0.0), axis=0, keepdims=True) for b in range(LEVELS - 1)
    ]
    total = jnp.sum(tot_s[...], axis=0, keepdims=True)
    total = sum(total[:, i : i + 128] for i in range(0, PAIR, 128))
    rows.append(total - sum(rows))
    levels = jnp.sum(jnp.concatenate(rows, axis=0), axis=1, keepdims=True)
    levels = sbias_s[...] + jnp.where(level_lane == chip, levels, 0.0)
    levels = jnp.concatenate([levels, jnp.zeros((128 - LEVELS, 128), F32)], axis=0)
    b_send[...] = jnp.transpose(levels)[0:8, :]

    def b2_copy(o):
        return remote(
            b_send, b_ctx.at[ctx], b2_s.at[o], b2_r.at[o], dp, lax.rem(ctx + o, 2 * CHIPS)
        )

    def start_b2(o, carry):
        b2_copy(o).start()
        return carry

    lax.fori_loop(1, 2 * CHIPS, start_b2, 0)
    b_ctx[ctx] = b_send[...]

    def finish(step, carry):
        qs = CHIPS - 1 - step
        sib_copy(qs).wait_recv()
        mine = rows_at(qs, ROWS)
        block = rows_at(2 * qs + core, ROWS)
        dk = (dk_s[block, :] + sib_recv[qs, :, 0:HEAD].astype(F32)) * SCALE
        dv = dv_s[block, :] + sib_recv[qs, :, HEAD : 2 * HEAD].astype(F32)
        grad_all[mine, HEAD : 2 * HEAD] = (
            dv * p_s[qs, :, HEAD : 2 * HEAD]
        ).astype(BF)
        grad_all[mine, 3 * HEAD : 4 * HEAD] = (
            dk * p_s[qs, :, 3 * HEAD : 4 * HEAD]
        ).astype(BF)

        @pl.when(qs != chip)
        def _():
            g_copy(1, qs).start()
            g_copy(3, qs).start()

        return carry

    lax.fori_loop(0, CHIPS, finish, 0)

    for d in (1, 3, 2):
        src = lax.rem(chip + CHIPS - d, CHIPS)
        there = pl.ds(pl.multiple_of(LONG_ROWS + src * SHORT, SHORT), SHORT)
        remote(stok, tok_all.at[there, :], st_s.at[d], st_r.at[d], dp, sib).wait_recv()
        remote(sgrad_s.at[src], grad_all.at[there, :], sg_s.at[d], sg_r.at[d], dp, sib).wait_recv()

    half_dp = n_dp // 2
    half_model = MODEL // 2
    my_half = lax.div(dp, half_dp)
    halves = (1 - my_half, my_half)

    def outer(pair, half):
        cols = pl.ds(pl.multiple_of(pair * 2 * HEAD, 2 * HEAD), 2 * HEAD)
        rows = pl.ds(pl.multiple_of(half * half_model, half_model), half_model)
        return dot_tn(tok_all[:, rows], grad_all[:, cols])

    def swap(j):
        return remote(half_send.at[j], half_recv.at[j], p_ss.at[j], p_sr.at[j], dp, sib)

    def ry_copy(o):
        return remote(
            rs_send.at[y ^ o], rs_mid.at[y], ry_s.at[o], ry_r.at[o], (y ^ o) * NZ + z, ctx
        )

    def rz_copy(o):
        peer = lax.rem(z + o, NZ)
        return remote(
            rs_sum.at[peer], rs_fin.at[z], rz_s.at[o], rz_r.at[o], y * NZ + peer, ctx
        )

    for j in range(2):
        half_send[j] = outer(1 - core, halves[j]).astype(BF)
        swap(j).start()
    for j in range(2):
        own[...] = outer(core, halves[j])
        swap(j).wait_recv()
        total = (own[...] + half_recv[j].astype(F32)).astype(BF)
        rs_send[pl.ds(halves[j] * (ny // 2), ny // 2)] = total.reshape(
            (ny // 2,) + rs_send.shape[1:]
        )
        for o in ((2, 3), (1,))[j]:
            ry_copy(o).start()

    def wait_b2(o, carry):
        src = lax.rem(ctx + 2 * CHIPS - o, 2 * CHIPS)
        remote(b_send, b_ctx.at[src], b2_s.at[o], b2_r.at[o], dp, src).wait_recv()
        return carry

    lax.fori_loop(1, 2 * CHIPS, wait_b2, 0)
    b_mid[...] = jnp.sum(b_ctx[...], axis=0)

    def write(source, target, index):
        return pltpu.make_async_copy(source, target, out_sem.at[index])

    total = dot_nt(sgrad_s[0], wh[0])
    for h in range(1, 4):
        total = total + dot_nt(sgrad_s[h], wh[h])
    sg_v[...] = total.astype(BF)
    write(sg_v, short_grad, 3).start()

    total = rs_send[y].astype(F32)
    for o in range(1, ny):
        here = rs_mid.at[y ^ o]
        remote(here, here, ry_s.at[o], ry_r.at[o], dp, sib).wait_recv()
        total = total + rs_mid[y ^ o].astype(F32)
    rs_sum[...] = total.astype(BF)
    for o in range(1, NZ):
        rz_copy(o).start()

    one_start(b_mid, b_dp, b1_s, b1_r)
    b_dp[dp] = b_mid[...]

    for o in range(1, NZ):
        here = orecv.at[:, lax.rem(z + NZ - o, NZ)]
        remote(here, here, oz_s.at[o], oz_r.at[o], dp, sib).wait_recv()
    so_v[...] = dot_tn(place_s[...], orecv[...].reshape(n_dp * SLEN, BLOCK)).astype(BF)
    write(so_v, short_out, 1).start()

    lo_v[:, lanes_at(chip)] = out_s[chip]
    grad_h[chip] = grad_all[rows_at(chip, ROWS), :]
    total = dot_nt(grad_h[chip], wh[chip])
    for d in (1, 3, 2):
        src = lax.rem(chip + CHIPS - d, CHIPS)
        for k in range(4):
            here = grad_h.at[src, :, k * HEAD : (k + 1) * HEAD]
            remote(here, here, g_s.at[k, src], g_r.at[k, src], dp, sib).wait_recv()
        here = lo_v.at[:, lanes_at(src)]
        remote(out_s.at[src], here, l_s.at[src], l_r.at[src], dp, sib).wait_recv()
        total = total + dot_nt(grad_h[src], wh[src])
    tg_v[...] = total.astype(BF)
    write(tg_v, token_grad, 2).start()
    write(lo_v, long_out, 0).start()

    half_copy(up, 0, 0).wait_send()
    half_copy(up, 1, 0).wait_send()
    half_copy(down, 0, 1).wait_send()
    half_copy(down, 1, 1).wait_send()
    pass_copy(down, 0, up).wait_send()
    pass_copy(up, 1, down).wait_send()
    for d in (1, 3, 2):
        c_copy(d).wait_send()
        st_copy(d).wait_send()
        sg_copy(d).wait_send()
    one_all(dest_g, d_s, d_r).wait_send()
    dp_all(cbuf, crecv, s_s, s_r).wait_send()
    for o in range(1, ny):
        oy_copy(o).wait_send()
        ry_copy(o).wait_send()
    for o in range(1, NZ):
        oz_copy(o).wait_send()

    def ended_o(o, carry):
        t_copy(o).wait_send()
        b2_copy(o).wait_send()
        return carry

    lax.fori_loop(1, 2 * CHIPS, ended_o, 0)

    def ended_q(qs, carry):
        kv_copy(qs).wait_send()
        sib_copy(qs).wait_send()
        for d in (1, 3, 2):
            stat_copy(qs, d).wait_send()

        @pl.when(qs != chip)
        def _():
            l_copy(qs).wait_send()
            for k in range(4):
                g_copy(k, qs).wait_send()

        return carry

    lax.fori_loop(0, CHIPS, ended_q, 0)
    for j in range(2):
        swap(j).wait_send()

    total = rs_sum[z].astype(F32)
    for o in range(1, NZ):
        src = lax.rem(z + NZ - o, NZ)
        here = rs_fin.at[src]
        remote(here, here, rz_s.at[o], rz_r.at[o], dp, sib).wait_recv()
        total = total + rs_fin[src].astype(F32)
    piece[...] = total
    mine = lax.rem(chip, 2)

    def f_copy(i):
        target = 2 * (2 * core + i) + lax.div(chip, 2)
        return target, remote(
            piece.at[:, i * HEAD : (i + 1) * HEAD],
            proj_grad.at[:, lanes_at(mine)],
            f_s.at[i],
            f_r.at[mine],
            dp,
            target,
        )

    for i in range(2):
        target, copy = f_copy(i)

        @pl.when(target != ctx)
        def _():
            copy.start()

        @pl.when(target == ctx)
        def _():
            proj_grad[:, lanes_at(mine)] = piece[:, i * HEAD : (i + 1) * HEAD]

    one_all(b_dp, b1_s, b1_r).wait_recv()
    bias_out[...] = jnp.sum(b_dp[...], axis=0)[0:4, 0:LEVELS]

    for half in range(2):
        source = 2 * (2 * core + half) + lax.div(chip, 2)

        @pl.when(source != ctx)
        def _():
            remote(
                piece.at[:, 0:HEAD],
                proj_grad.at[:, half * HEAD : (half + 1) * HEAD],
                f_s.at[half],
                f_r.at[half],
                dp,
                source,
            ).wait_recv()

    for i in range(2):
        target, copy = f_copy(i)

        @pl.when(target != ctx)
        def _():
            copy.wait_send()

    for o in range(1, NZ):
        rz_copy(o).wait_send()
    one_all(b_dp, b1_s, b1_r).wait_send()
    write(lo_v, long_out, 0).wait()
    write(so_v, short_out, 1).wait()
    write(tg_v, token_grad, 2).wait()
    write(sg_v, short_grad, 3).wait()


def output_kernel(count, *refs):
    for i in range(count):
        refs[count + i][...] = refs[i][...]


VM = pl.BlockSpec(memory_space=pltpu.VMEM)
SM = pl.BlockSpec(memory_space=pltpu.SMEM)
ANY = pl.BlockSpec(memory_space=pl.ANY)
DMA = pltpu.SemaphoreType.DMA
VMEM = pltpu.VMEM


def shaped(shape, dtype):
    return jax.ShapeDtypeStruct(shape, dtype)


def per_device(
    n_dp,
    long_tokens,
    short_tokens,
    projection,
    time_bias,
    long_length,
    short_length,
    long_time,
    short_time,
    destination,
    long_cotangent,
    short_cotangent,
):
    part = MODEL // n_dp
    ny = n_dp // NZ
    spread = (n_dp, SLEN, BLOCK)
    scratch = [
        VMEM((CHIPS, MODEL, BLOCK), BF),
        VMEM((ALL_ROWS, MODEL), BF),
        VMEM((ALL_ROWS, BLOCK), BF),
        VMEM((CHIPS, ROWS, BLOCK), F32),
        VMEM((CHIPS, ROWS, BLOCK), BF),
        VMEM((2 * CHIPS * ROWS, 2 * HEAD), BF),
        VMEM((CHIPS, ROWS, HEAD), BF),
        VMEM((8, ROWS), jnp.int32),
        VMEM((2 * CHIPS, 8, ROWS), jnp.int32),
        VMEM((8, 128), F32),
        VMEM((8, 128), jnp.int32),
        VMEM((8, 128), jnp.int32),
        VMEM((n_dp, 8, 128), jnp.int32),
        VMEM((n_dp * SLEN, 128), BF),
        VMEM(spread, BF),
        VMEM(spread, BF),
        VMEM((4, SHORT, BLOCK), F32),
        VMEM((4, SHORT, BLOCK), BF),
        VMEM((4, SHORT, SHORT), BF),
        VMEM((4, SHORT, SHORT), F32),
        VMEM((4, SHORT, HEAD), F32),
        VMEM((SHORT, 128), F32),
        VMEM((SHORT, BLOCK), F32),
        VMEM((4, SHORT, BLOCK), BF),
        VMEM((ny, NZ, SLEN, BLOCK), BF),
        VMEM((ny, NZ, SLEN, BLOCK), BF),
        VMEM((ny, NZ, SLEN, BLOCK), BF),
        VMEM((LEVELS, 128), F32),
        VMEM((CHIPS, CHIPS, ROWS, PAIR), BF),
        VMEM((CHIPS, CHIPS, ROWS, PAIR), F32),
        VMEM((CHIPS, ROWS, HEAD), F32),
        VMEM((CHIPS, ROWS, HEAD), BF),
        VMEM((2 * CHIPS * ROWS, 128), BF),
        VMEM((2 * CHIPS, ROWS, 128), F32),
        VMEM((CHIPS, CHIPS, 8, ROWS), F32),
        VMEM((2 * CHIPS * ROWS, HEAD), F32),
        VMEM((2 * CHIPS * ROWS, HEAD), F32),
        VMEM((ROWS, HEAD), F32),
        VMEM((ROWS, 128), F32),
        VMEM((128, 128), F32),
        VMEM((8, PAIR), F32),
        VMEM((CHIPS, ROWS, 2 * HEAD), BF),
        VMEM((CHIPS, ROWS, 2 * HEAD), BF),
        VMEM((CHIPS, ROWS, BLOCK), BF),
        VMEM((2, MODEL // 2, 2 * HEAD), BF),
        VMEM((2, MODEL // 2, 2 * HEAD), BF),
        VMEM((MODEL // 2, 2 * HEAD), F32),
        VMEM((ny, NZ, part, 2 * HEAD), BF),
        VMEM((ny, NZ, part, 2 * HEAD), BF),
        VMEM((NZ, part, 2 * HEAD), BF),
        VMEM((NZ, part, 2 * HEAD), BF),
        VMEM((8, 128), F32),
        VMEM((n_dp, 8, 128), F32),
        VMEM((8, 128), F32),
        VMEM((2 * CHIPS, 8, 128), F32),
        VMEM((part, 2 * HEAD), F32),
        VMEM((ROWS, BLOCK), BF),
        VMEM((SHORT, BLOCK), BF),
        VMEM((ROWS, MODEL), BF),
        VMEM((SHORT, MODEL), BF),
        DMA((4, 4)),
        DMA((3,)),
        DMA((4,)),
        DMA((2, 2)),
        DMA((2, 2)),
        DMA((2,)),
        DMA((2,)),
        DMA((CHIPS,)),
        DMA((CHIPS,)),
        DMA((2 * CHIPS,)),
        DMA((2 * CHIPS,)),
        DMA((CHIPS,)),
        DMA((CHIPS,)),
        DMA((CHIPS,)),
        DMA((CHIPS,)),
        DMA((CHIPS,)),
        DMA((CHIPS,)),
        DMA,
        DMA,
        DMA,
        DMA,
        DMA((ny,)),
        DMA((ny,)),
        DMA((NZ,)),
        DMA((NZ,)),
        DMA((CHIPS, CHIPS)),
        DMA((CHIPS, CHIPS)),
        DMA((CHIPS,)),
        DMA((CHIPS,)),
        DMA((4, CHIPS)),
        DMA((4, CHIPS)),
        DMA((CHIPS,)),
        DMA((CHIPS,)),
        DMA((2,)),
        DMA((2,)),
        DMA((ny,)),
        DMA((ny,)),
        DMA((NZ,)),
        DMA((NZ,)),
        DMA,
        DMA,
        DMA((2 * CHIPS,)),
        DMA((2 * CHIPS,)),
        DMA((2,)),
        DMA((2,)),
    ]
    results = pl.pallas_call(
        functools.partial(layer_kernel, n_dp),
        out_shape=(
            shaped((ROWS, BLOCK), BF),
            shaped((SHORT, BLOCK), BF),
            shaped((ROWS, MODEL), BF),
            shaped((SHORT, MODEL), BF),
            shaped((part, 2 * HEAD), F32),
            shaped(time_bias.shape, F32),
        ),
        in_specs=[ANY, ANY, ANY, ANY, VM, VM, VM, VM, VM, SM, VM],
        out_specs=(ANY,) * 4 + (VM,) * 2,
        scratch_shapes=scratch,
        compiler_params=pltpu.CompilerParams(
            vmem_limit_bytes=VMEM_LIMIT, collective_id=0, has_side_effects=True
        ),
        name="layer",
    )(
        long_tokens[0],
        short_tokens.reshape(SHORT, MODEL),
        projection,
        long_cotangent[0],
        short_cotangent.reshape(SHORT, BLOCK),
        long_time,
        short_time,
        short_length,
        destination,
        long_length,
        time_bias,
    )
    results = pl.pallas_call(
        functools.partial(output_kernel, len(results)),
        out_shape=tuple(shaped(r.shape, r.dtype) for r in results),
        in_specs=[VM] * len(results),
        out_specs=(VM,) * len(results),
        compiler_params=pltpu.CompilerParams(vmem_limit_bytes=VMEM_LIMIT),
        name="output",
    )(*results)
    long_out, short_out, token_grad, short_grad, proj_grad, bias_out = results
    return (
        long_out[None],
        short_out.reshape(short_cotangent.shape),
        token_grad[None],
        short_grad.reshape(short_tokens.shape),
        proj_grad,
        bias_out,
    )


def solution(mesh):
    return jax.shard_map(
        functools.partial(per_device, mesh.shape["dp"]),
        mesh=mesh,
        in_specs=(
            P("dp", "ctx", None),
            P("dp", "ctx", None, None),
            P(),
            P(),
            P("dp"),
            P("dp", "ctx"),
            P("dp", "ctx"),
            P("dp", "ctx", None),
            P("dp", "ctx"),
            P("dp", "ctx", None),
            P("dp", "ctx", None, None),
        ),
        out_specs=(
            P("dp", "ctx", None),
            P("dp", "ctx", None, None),
            P("dp", "ctx", None),
            P("dp", "ctx", None, None),
            P("dp", "ctx"),
            P(),
        ),
        check_vma=False,
    )
```
